128 devices in a mesh: ctx: 32 (over z, y, core), tp: 2 (over x_lo), dp: 2 (over x_hi).
Axes of the slice: x: 4 (x_hi: 2, x_lo: 2; x = x_hi * 2 + x_lo), y: 4, z: 4, core: 2. Of those that a mesh axis runs over, the one named last changes fastest.
Arguments:
- base_ids: int32 [2, 8192], P('dp', 'ctx'), may hold values from 0 to 4
- stream: bfloat16 [2, 8192, 1024], P('dp', 'ctx'), may hold values from -6 to 6
- cotangent: bfloat16 [2, 8192, 1024], P('dp', 'ctx'), may hold values from -0.0625 to 0.0625
- table: float32 [5, 1024], replicated, may hold values from -6 to 6
- gain: float32 [1024], replicated, may hold values from 0.5 to 1.5
- projections: bfloat16 [1024, 3, 2048], P(None, None, 'tp'), may hold values from -0.1875 to 0.1875
- mixer_weight: bfloat16 [1024, 128], replicated, may hold values from -0.0625 to 0.0625
- step_weight: bfloat16 [1024, 32], P(None, 'tp'), may hold values from -0.1875 to 0.1875
- step_bias: float32 [32], P('tp'), may hold values from -4 to -0.5
- rate: float32 [32], P('tp'), may hold values from 0.0001 to 0.3
Outputs:
- grad_projections: float32 [1024, 3, 2048], P(('ctx', 'dp'), None, 'tp')
- grad_mixer: float32 [1024, 128], replicated
- grad_step_weight: float32 [1024, 32], P(None, 'tp')
- grad_step_bias: float32 [32], P('tp')
- grad_rate: float32 [32], P('tp')
- grad_table: float32 [5, 1024], replicated
- grad_gain: float32 [1024], replicated
- grad_stream: float32 [2, 8192, 1024], P('dp', 'ctx', 'tp')
The draws below stay inside these ranges and needn't reach their ends.
All inputs are finite; a program needn't handle non-finite values.
Results may differ from the reference program's by a relative error of at most 0.011.
Values sent between devices are 32-bit elements; how exact they have to be, the bound alone decides.
A program may use at most 192 MiB of HBM per device.

```python
import math
import jax
import jax.numpy as jnp
from jax import lax

D = 1024
HEADS = 32
HEAD_DIM = 64
STATE = 64
GROUP = 256
INNER = 2048
LEN = 8192
SEQS = 2


def plant(values, key, least, top_value):
    index_at = [jax.random.randint(jax.random.fold_in(key, axis), (), 0, length) for axis, length in enumerate(values.shape)]
    main_axis = values.shape.index(max(values.shape))
    beside = index_at[:main_axis] + [(index_at[main_axis] + 1) % values.shape[main_axis]] + index_at[main_axis + 1:]
    return values.at[tuple(index_at)].set(least).at[tuple(beside)].set(top_value)


def with_spikes(values, own_key, source, target, shards_of, factor):
    def block_of(position):
        return (jnp.arange(values.shape[position]) // (values.shape[position] // shards_of)).reshape((-1,) + (1,) * (values.ndim - 1 - position))

    near = jax.random.permutation(own_key, shards_of)[block_of(target)]
    other_side = (block_of(target) + shards_of // 2) % shards_of
    return jnp.where((block_of(source) == near) | (block_of(source) == other_side), factor * values, values)


def level_of(rng, dims, cuts, smallest, top_value):
    factor_of = 1.0
    for dim, blocks in cuts:
        heights = jax.random.uniform(jax.random.fold_in(jax.random.fold_in(rng, 6), dim), (blocks,), jnp.float32, smallest / len(cuts), top_value / len(cuts))
        factor_of = factor_of * jnp.repeat(jnp.exp(heights), dims[dim] // blocks).reshape((-1,) + (1,) * (len(dims) - 1 - dim))
    return factor_of


def normal_values(own_key, dims, scale, limit, cuts=(), kind=jnp.bfloat16):
    values = scale * jax.random.normal(own_key, dims, jnp.float32)
    if cuts:
        values = values * level_of(own_key, dims, cuts, -0.22, 0.18)
    return jnp.clip(values, -limit, limit).astype(kind)


def gaussian_with(rng, extent, width, reach, cuts, heavy, kind=jnp.bfloat16):
    values = width * jax.random.normal(rng, extent, jnp.float32)
    if cuts:
        values = values * level_of(rng, extent, cuts, -0.22, 0.18)
    return jnp.clip(with_spikes(values, jax.random.fold_in(rng, 3), *heavy), -reach, reach).astype(kind)


def setup_inputs(seed: int = 0) -> dict:
    streams_of = jax.random.split(jax.random.key(seed), 11)
    return {
        "base_ids": plant(jax.random.randint(streams_of[0], (SEQS, LEN), 0, 5), jax.random.fold_in(streams_of[0], 1), 0, 4).astype(jnp.int32),
        "stream": normal_values(streams_of[1], (SEQS, LEN, D), 1.0, 6.0, ((0, 2), (1, 32))),
        "cotangent": gaussian_with(streams_of[2], (SEQS, LEN, D), ((2 * SEQS * LEN) ** -0.5), 0.0625, ((0, 2), (1, 32)), (1, 2, 32, 2.75)),
        "table": normal_values(streams_of[3], (5, D), 1.0, 6.0, (), jnp.float32),
        "gain": jnp.clip(1.0 + 0.1 * jax.random.normal(streams_of[4], (D,), jnp.float32), 0.5, 1.5),
        "projections": normal_values(streams_of[5], (D, 3, INNER), D ** -0.5, 0.1875, ((2, 2),)),
        "mixer_weight": normal_values(streams_of[6], (D, 2 * STATE), (8 * D) ** -0.5, 0.0625),
        "step_weight": normal_values(streams_of[7], (D, HEADS), D ** -0.5, 0.1875, ((1, 2),)),
        "step_bias": jnp.clip(-4.0 + 3.5 * jax.random.uniform(streams_of[8], (HEADS,), jnp.float32) ** level_of(streams_of[8], (HEADS,), ((0, 2),), -0.2, 0.2), -4.0, -0.5),
        "rate": jnp.clip(jnp.exp(math.log(0.3) - 8.006368 * jax.random.uniform(streams_of[9], (HEADS,), jnp.float32) ** level_of(streams_of[9], (HEADS,), ((0, 2),), -0.2, 0.2)), 0.0001, 0.3),
    }


EPS = 1e-05
HIGH = lax.Precision.HIGHEST

def complement(bases):
    return jnp.where(bases == 4, 4, 3 - bases).astype(jnp.int32)

def one_hot(bases):
    letters = jnp.arange(5, dtype=jnp.int32)
    return (bases[:, None] == letters[None, :]).astype(jnp.float32)

def lower_ones(length):
    rows = lax.broadcasted_iota(jnp.int32, (length, length), 0)
    columns = lax.broadcasted_iota(jnp.int32, (length, length), 1)
    return (rows >= columns).astype(jnp.float32)

def cumulative(lower, series):
    return jnp.dot(lower, series, precision=HIGH)

def times_transposed(left, right):
    return lax.dot_general(left, right, (((1,), (1,)), ((), ())), preferred_element_type=jnp.float32)

def outer_sum(left, right):
    return lax.dot_general(left, right, (((0,), (0,)), ((), ())), preferred_element_type=jnp.float32)

def heads_view(array, heads):
    return array.reshape(array.shape[0], heads, array.shape[1] // heads)

def prepare(bases, incoming, upstream, table, gain, projections, mixer_weight, step_weight, step_bias, rate):
    embedded = incoming.astype(jnp.float32) + jnp.dot(one_hot(bases), table, precision=HIGH)
    inv_scale = lax.rsqrt(lax.optimization_barrier(jnp.mean(embedded * embedded, axis=1, keepdims=True)) + EPS)
    normed = embedded * inv_scale
    features = (normed * gain[None, :]).astype(jnp.bfloat16)
    values = jnp.dot(features, projections[:, 0, :], preferred_element_type=jnp.float32)
    gates = jnp.dot(features, projections[:, 1, :], preferred_element_type=jnp.float32)
    mapped = jnp.dot(features, mixer_weight, preferred_element_type=jnp.float32)
    step_logit = jnp.dot(features, step_weight, preferred_element_type=jnp.float32) + step_bias[None, :]
    step = jax.nn.softplus(step_logit)
    log_decay = -step * rate[None, :]
    grad_gated = jnp.dot(upstream, projections[:, 2, :], preferred_element_type=jnp.float32)
    swish = jax.nn.silu(gates)
    grad_output = grad_gated * swish
    return (normed, inv_scale, features, values, gates, mapped, step_logit, step, log_decay, swish, grad_gated, grad_output)

def group_ends(log_decay, step, values, inflow, readout, grad_output):
    lower = lower_ones(log_decay.shape[0])
    running = cumulative(lower, log_decay)
    final_log = running[-1]
    tail = jnp.exp(final_log[None, :] - running)
    drive = step[:, :, None] * values
    state = jnp.einsum('jn,jhp->hnp', inflow, drive * tail[:, :, None], precision=HIGH)
    grad_state = jnp.einsum('in,ihp->hnp', readout, grad_output * jnp.exp(running)[:, :, None], precision=HIGH)
    return (jnp.exp(final_log), state, grad_state)

def group_full(log_decay, step, values, inflow, readout, grad_output, initial, later_grad, rate):
    lower = lower_ones(log_decay.shape[0])
    running = cumulative(lower, log_decay)
    final_log = running[-1]
    head = jnp.exp(running)
    tail = jnp.exp(final_log[None, :] - running)
    spread = running.T[:, :, None] - running.T[:, None, :]
    decay_grid = jnp.exp(jnp.where(lower[None] > 0, spread, -1e+30))
    drive = step[:, :, None] * values
    affinity = jnp.dot(readout, inflow.T, precision=HIGH)
    mixing = decay_grid * affinity[None]
    carried = jnp.einsum('in,hnp->ihp', readout, initial, precision=HIGH) * head[:, :, None]
    output = jnp.einsum('hij,jhp->ihp', mixing, drive, precision=HIGH) + carried
    pulled = jnp.einsum('jn,hnp->jhp', inflow, later_grad, precision=HIGH) * tail[:, :, None]
    grad_drive = jnp.einsum('hkj,khp->jhp', mixing, grad_output, precision=HIGH) + pulled
    pairing = decay_grid * jnp.einsum('khp,jhp->hkj', grad_output, drive, precision=HIGH)
    grad_inflow = jnp.einsum('hkj,kn->jn', pairing, readout, precision=HIGH) + jnp.einsum('hnp,jhp->jn', later_grad, drive * tail[:, :, None], precision=HIGH)
    grad_readout = jnp.einsum('hij,jn->in', pairing, inflow, precision=HIGH) + jnp.einsum('hnp,ihp->in', initial, grad_output * head[:, :, None], precision=HIGH)
    weighted = pairing * affinity[None]
    column_sums = lax.optimization_barrier(jnp.sum(weighted, axis=1)).T
    row_sums = lax.optimization_barrier(jnp.sum(weighted, axis=2)).T
    inside = cumulative(lower, column_sums) - cumulative(lower, row_sums) + row_sums
    before = jnp.dot(lower.T, lax.optimization_barrier(jnp.sum(grad_output * carried, axis=2)), precision=HIGH)
    boundary = jnp.exp(final_log) * lax.optimization_barrier(jnp.sum(initial * later_grad, axis=(1, 2)))
    after = cumulative(lower, lax.optimization_barrier(jnp.sum(pulled * drive, axis=2)))
    grad_log = inside + before + boundary[None, :] + after - lax.optimization_barrier(jnp.sum(grad_drive * drive, axis=2))
    grad_values = step[:, :, None] * grad_drive
    grad_step = lax.optimization_barrier(jnp.sum(grad_drive * values, axis=2)) - grad_log * rate[None, :]
    grad_rate = -lax.optimization_barrier(jnp.sum(grad_log * step, axis=0))
    return (output, grad_values, grad_step, grad_rate, grad_inflow, grad_readout)

def finish(prepared, mixer_terms, projections, mixer_weight, step_weight):
    normed, inv_scale, features, values, gates, mapped, step_logit, step, log_decay, swish, grad_gated, grad_output = prepared
    output, grad_values, grad_step, grad_rate, grad_inflow, grad_readout = mixer_terms
    gated = (output * swish).astype(jnp.bfloat16)
    sigma = jax.nn.sigmoid(gates)
    grad_gates = (grad_gated * output * sigma * (1.0 + gates * (1.0 - sigma))).astype(jnp.bfloat16)
    grad_values_rounded = grad_values.astype(jnp.bfloat16)
    grad_mapped = jnp.concatenate([grad_inflow, grad_readout], axis=1).astype(jnp.bfloat16)
    grad_logit = grad_step * jax.nn.sigmoid(step_logit)
    grad_logit_rounded = grad_logit.astype(jnp.bfloat16)
    grad_features = times_transposed(grad_values_rounded, projections[:, 0, :]) + times_transposed(grad_gates, projections[:, 1, :])
    grad_features = grad_features + times_transposed(grad_mapped, mixer_weight) + times_transposed(grad_logit_rounded, step_weight)
    return (features, gated, grad_values_rounded, grad_gates, grad_mapped, grad_logit_rounded, lax.optimization_barrier(jnp.sum(grad_logit, axis=0)), grad_features)

def norm_back(grad_features, normed, inv_scale, gain, residual):
    grad_normed = grad_features * gain[None, :]
    centred = grad_normed - normed * lax.optimization_barrier(jnp.mean(grad_normed * normed, axis=1, keepdims=True))
    return (inv_scale * centred + residual, lax.optimization_barrier(jnp.sum(grad_features * normed, axis=0)))

def mixer_sequence(prepared, rate):
    log_decay, step, values, mapped, grad_output = (prepared[8], prepared[7], prepared[3], prepared[5], prepared[11])
    length = step.shape[0]
    heads = step.shape[1]
    blocks = length // GROUP

    def split(array):
        return array.reshape((blocks, GROUP) + array.shape[1:])
    pieces = (split(log_decay), split(step), split(heads_view(values, heads)), split(mapped[:, :STATE]), split(mapped[:, STATE:]), split(heads_view(grad_output, heads)))
    decays, states, grad_states = lax.map(lambda piece: group_ends(*piece), pieces)
    empty = jnp.zeros((heads, STATE, HEAD_DIM), jnp.float32)

    def forward_link(carry, item):
        return (item[0][:, None, None] * carry + item[1], carry)

    def backward_link(carry, item):
        return (item[1] + item[0][:, None, None] * carry, carry)
    _, initials = lax.scan(forward_link, empty, (decays, states))
    _, laters = lax.scan(backward_link, empty, (decays, grad_states), reverse=True)
    results = lax.map(lambda piece: group_full(*piece, rate), pieces + (initials, laters))
    output = results[0].reshape(length, -1)
    grad_values = results[1].reshape(length, -1)
    grad_step = results[2].reshape(length, heads)
    grad_rate = lax.optimization_barrier(jnp.sum(results[3], axis=0))
    grad_inflow = results[4].reshape(length, STATE)
    grad_readout = results[5].reshape(length, STATE)
    return (output, grad_values, grad_step, grad_rate, grad_inflow, grad_readout)

def reference(base_ids, stream, cotangent, table, gain, projections, mixer_weight, step_weight, step_bias, rate):
    totals = None
    stream_grads = []
    for sequence in range(SEQS):
        strand_grads = []
        for strand in range(2):
            bases = base_ids[sequence]
            incoming = stream[sequence]
            upstream = cotangent[sequence]
            if strand == 1:
                bases = complement(bases)[::-1]
                incoming = incoming[::-1]
                upstream = upstream[::-1]
            prepared = prepare(bases, incoming, upstream, table, gain, projections, mixer_weight, step_weight, step_bias, rate)
            mixer_terms = mixer_sequence(prepared, rate)
            features, gated, grad_values, grad_gates, grad_mapped, grad_logit, grad_bias, grad_features = finish(prepared, mixer_terms, projections, mixer_weight, step_weight)
            grad_embedded, grad_gain = norm_back(grad_features, prepared[0], prepared[1], gain, upstream.astype(jnp.float32))
            strand_grads.append(grad_embedded)
            stacked = jnp.stack([outer_sum(features, grad_values), outer_sum(features, grad_gates), outer_sum(upstream, gated)], axis=1)
            terms = (stacked, outer_sum(features, grad_mapped), outer_sum(features, grad_logit), grad_bias, mixer_terms[3], jnp.dot(one_hot(bases).T, grad_embedded, precision=HIGH), grad_gain)
            totals = terms if totals is None else jax.tree.map(jnp.add, totals, terms)
        stream_grads.append(strand_grads[0] + strand_grads[1][::-1])
    grad_stream = jnp.stack(stream_grads, axis=0)
    return (totals[0], totals[1], totals[2], totals[3], totals[4], totals[5], totals[6], grad_stream)
```

```python
import functools

import jax
import jax.numpy as jnp
from jax import lax
from jax.experimental import pallas as pl
from jax.experimental.pallas import tpu as pltpu
from jax.sharding import PartitionSpec as P

EPS = 1e-05
HIGH = lax.Precision.HIGHEST
F32 = jnp.float32
BF16 = jnp.bfloat16
MESH = pl.DeviceIdType.MESH
BASES = 256
WIDTH = 1024
HEADS = 16
PAIRS = 8
STATE = 64


def nt(left, right):
    return lax.dot_general(left, right, (((1,), (1,)), ((), ())), preferred_element_type=F32)


def tn(left, right):
    return lax.dot_general(left, right, (((0,), (0,)), ((), ())), preferred_element_type=F32)


def dot(left, right):
    return jnp.dot(left, right, preferred_element_type=F32)


def exact(left, right):
    return jnp.dot(left, right, preferred_element_type=F32, precision=HIGH)


def scan_kernel(src, res, recv, out, send_a, recv_a, send_b, recv_b):
    me = lax.axis_index("ctx")
    count = 32

    barrier = pltpu.get_barrier_semaphore()

    def greet(s, c):
        pl.semaphore_signal(barrier, inc=1, device_id={"ctx": lax.rem(me + s, count)}, device_id_type=MESH)
        return c

    lax.fori_loop(1, count, greet, 0)
    pl.semaphore_wait(barrier, count - 1)

    def to_owner(s):
        there = lax.rem(me + s, count)
        return pltpu.make_async_remote_copy(
            src_ref=src.at[there], dst_ref=recv.at[s], send_sem=send_a.at[s], recv_sem=recv_a.at[s],
            device_id={"ctx": there}, device_id_type=MESH)

    def back(s):
        there = lax.rem(me + s, count)
        return pltpu.make_async_remote_copy(
            src_ref=out.at[there], dst_ref=res.at[me], send_sem=send_b.at[s], recv_sem=recv_b.at[s],
            device_id={"ctx": there}, device_id_type=MESH)

    def start_a(s, c):
        to_owner(s).start()
        return c

    def wait_a(s, c):
        to_owner(s).wait()
        return c

    def start_b(s, c):
        back(s).start()
        return c

    def wait_b(s, c):
        there = lax.rem(me + s, count)
        back(s).wait_send()
        return c

    lax.fori_loop(1, count, start_a, 0)
    recv[0] = src[me]
    lax.fori_loop(1, count, wait_a, 0)
    falling = me // 16

    def step(i, carry):
        at = i + falling * (count - 1 - 2 * i)
        out[at] = carry
        slot = lax.rem(me - at + count, count)
        decay = recv[slot, 64:65, :]
        return carry * decay + recv[slot, 0:64, :]

    lax.fori_loop(0, count, step, jnp.zeros((STATE, 128), F32))
    lax.fori_loop(1, count, start_b, 0)
    res[me] = out[me]
    lax.fori_loop(1, count, wait_b, 0)

    def arrived(s, c):
        frm = lax.rem(me - s + count, count)
        pltpu.make_async_remote_copy(
            src_ref=out.at[frm], dst_ref=res.at[frm], send_sem=send_b.at[s], recv_sem=recv_b.at[s],
            device_id={"ctx": frm}, device_id_type=MESH).wait_recv()
        return c

    lax.fori_loop(1, count, arrived, 0)


def exchange_states(src):
    return pl.pallas_call(
        scan_kernel,
        out_shape=jax.ShapeDtypeStruct((32, STATE, 128), F32),
        in_specs=[pl.BlockSpec(memory_space=pltpu.VMEM)],
        out_specs=pl.BlockSpec(memory_space=pltpu.VMEM),
        scratch_shapes=[
            pltpu.VMEM((32, 72, 128), F32),
            pltpu.VMEM((32, STATE, 128), F32),
            pltpu.SemaphoreType.DMA((32,)),
            pltpu.SemaphoreType.DMA((32,)),
            pltpu.SemaphoreType.DMA((32,)),
            pltpu.SemaphoreType.DMA((32,)),
        ],
        compiler_params=pltpu.CompilerParams(collective_id=0, has_side_effects=True, vmem_limit_bytes=32 << 20),
        name="exchange_states",
    )(src)


def block_kernel(v, g, gg, run, run_t, step, logit, inflow, readout, init, later, rate,
                 gv_out, gate_out, gated_out, mapped_out, logit_out, rate_out,
                 affinity, pairs, dd, dv, kk, gin, gread):
    d, j = pl.program_id(0), pl.program_id(1)
    sign = 1 - 2 * d
    rows = lax.broadcasted_iota(jnp.int32, (BASES, BASES), 0)
    columns = lax.broadcasted_iota(jnp.int32, (BASES, BASES), 1)
    order = (rows - columns) * sign
    inflow_b = inflow[0].astype(BF16)
    readout_b = readout[0].astype(BF16)

    @pl.when(j == 0)
    def _():
        affinity[...] = nt(readout_b, inflow_b)
        pairs[...] = jnp.zeros_like(pairs)
        dd[...] = jnp.zeros_like(dd)
        dv[...] = jnp.zeros_like(dv)
        kk[...] = jnp.zeros_like(kk)
        gin[...] = jnp.zeros_like(gin)
        gread[...] = jnp.zeros_like(gread)

    lane_head = lax.broadcasted_iota(jnp.int32, (HEADS, 128), 1) // 64 + 2 * j
    spread_out = (lax.broadcasted_iota(jnp.int32, (HEADS, 128), 0) == lane_head).astype(F32)
    lane_head_t = lax.broadcasted_iota(jnp.int32, (128, HEADS), 0) // 64 + 2 * j
    gather_in = (lax.broadcasted_iota(jnp.int32, (128, HEADS), 1) == lane_head_t).astype(F32)

    run_e = exact(run[0], spread_out)
    step_e = exact(step[0], spread_out)
    last = (BASES - 1) * (1 - d)
    at_last = lax.broadcasted_iota(jnp.int32, (BASES, 128), 0) == last
    final = jnp.sum(jnp.where(at_last, run_e, 0.0), axis=0, keepdims=True)
    head = jnp.exp(run_e)
    tail = jnp.exp(final - run_e)
    values, gates, grad_gated = v[...], g[...], gg[...]
    drive = step_e * values
    sigma = jax.nn.sigmoid(gates)
    swish = gates * sigma
    go = grad_gated * swish
    drive_b = drive.astype(BF16)
    go_b = go.astype(BF16)
    drive_r = drive_b.astype(F32)
    go_r = go_b.astype(F32)
    initial, after = init[0], later[0]
    initial_b, after_b = initial.astype(BF16), after.astype(BF16)
    carried = dot(readout_b, initial_b) * head
    pulled = dot(inflow_b, after_b) * tail
    low = lax.broadcasted_iota(jnp.int32, (BASES, 128), 1) < 64
    output, grad_drive = carried, pulled
    aff = affinity[...]
    total = pairs[...]
    for half in range(2):
        mine = low if half == 0 else jnp.logical_not(low)
        column = run_e[:, 64 * half:64 * half + 1]
        row = run_t[0, pl.ds(2 * j + half, 1), :]
        decay = jnp.exp(jnp.where(order >= 0, column - row, -1e30))
        mixing = (decay * aff).astype(BF16)
        drive_h = jnp.where(mine, drive_r, 0.0).astype(BF16)
        go_h = jnp.where(mine, go_r, 0.0).astype(BF16)
        output = output + dot(mixing, drive_h)
        grad_drive = grad_drive + tn(mixing, go_h)
        total = total + decay * nt(go_h, drive_b)
    pairs[...] = total
    dd[...] += exact(grad_drive * drive_r - go_r * output, gather_in)
    dv[...] += exact(grad_drive * values, gather_in)
    boundary = jnp.sum(go_r * carried, axis=0, keepdims=True) + jnp.exp(final) * jnp.sum(
        initial * after, axis=0, keepdims=True)
    kk[...] += exact(jnp.broadcast_to(boundary, (8, 128)), gather_in)
    gin[...] += nt((drive * tail).astype(BF16), after_b)
    gread[...] += nt((go * head).astype(BF16), initial_b)
    gv_out[...] = (step_e * grad_drive).astype(BF16)
    gate_out[...] = (grad_gated * output * sigma * (1.0 + gates * (1.0 - sigma))).astype(BF16)
    gated_out[...] = (output * swish).astype(BF16)

    @pl.when(j == PAIRS - 1)
    def _():
        pairs_b = pairs[...].astype(BF16)
        grad_in = gin[...] + tn(pairs_b, readout_b)
        grad_read = gread[...] + dot(pairs_b, inflow_b)
        mapped_out[...] = jnp.concatenate([grad_in, grad_read], axis=1).astype(BF16)
        before = (order > 0).astype(F32)
        grad_log = exact(before, dd[...]) + kk[0:1, :]
        grad_step = dv[...] - grad_log * rate[...]
        logit_out[0] = grad_step * jax.nn.sigmoid(logit[0])
        rate_out[0] = jnp.broadcast_to(-jnp.sum(grad_log * step[0], axis=0, keepdims=True), (8, HEADS))


def blocks(v, g, gg, run, run_t, step, logit, inflow, readout, states, rate):
    heads_of = pl.BlockSpec((BASES, 128), lambda d, j: (d, j))
    small = pl.BlockSpec((1, BASES, HEADS), lambda d, j: (d, 0, 0))
    mapped = pl.BlockSpec((1, BASES, STATE), lambda d, j: (d, 0, 0))
    wide = jax.ShapeDtypeStruct((2 * BASES, WIDTH), BF16)
    return pl.pallas_call(
        block_kernel,
        grid=(2, PAIRS),
        in_specs=[
            heads_of, heads_of, pl.BlockSpec((BASES, 128), lambda d, j: (0, j)),
            small, pl.BlockSpec((1, HEADS, BASES), lambda d, j: (d, 0, 0)), small, small, mapped, mapped,
            pl.BlockSpec((1, STATE, 128), lambda d, j: (16 * d + j, 0, 0)),
            pl.BlockSpec((1, STATE, 128), lambda d, j: (24 - 16 * d + j, 0, 0)),
            pl.BlockSpec((1, HEADS), lambda d, j: (0, 0)),
        ],
        out_specs=[
            heads_of, heads_of, heads_of,
            pl.BlockSpec((BASES, 128), lambda d, j: (d, 0)),
            small,
            pl.BlockSpec((1, 8, HEADS), lambda d, j: (d, 0, 0)),
        ],
        out_shape=[
            wide, wide, wide,
            jax.ShapeDtypeStruct((2 * BASES, 128), BF16),
            jax.ShapeDtypeStruct((2, BASES, HEADS), F32),
            jax.ShapeDtypeStruct((2, 8, HEADS), F32),
        ],
        scratch_shapes=[
            pltpu.VMEM((BASES, BASES), F32),
            pltpu.VMEM((BASES, BASES), F32),
            pltpu.VMEM((BASES, HEADS), F32),
            pltpu.VMEM((BASES, HEADS), F32),
            pltpu.VMEM((8, HEADS), F32),
            pltpu.VMEM((BASES, STATE), F32),
            pltpu.VMEM((BASES, STATE), F32),
        ],
        compiler_params=pltpu.CompilerParams(vmem_limit_bytes=32 << 20),
        name="blocks",
    )(v, g, gg, run, run_t, step, logit, inflow, readout, states, states, rate)


SEMS = 128


def sum_kernel(p0, p1, p2, small, both, grads_out, small_out, stream_out,
               acc, core_in, ring, mid, ring2, fin, dp_in,
               acc_e, core_in_e, ring_e, mid_e, ring2_e, fin_e, dp_in_e,
               tp_in, tp_in_e, piece, row, send, recv, local):
    ctx, tp, dp = lax.axis_index("ctx"), lax.axis_index("tp"), lax.axis_index("dp")
    core, y, z = ctx % 2, (ctx // 2) % 4, ctx // 8

    def at(zz, yy, cc):
        return {"ctx": (zz * 4 + yy) * 2 + cc}

    other = at(z, y, 1 - core)
    y_dev = [at(z, (y + i) % 4, core) for i in range(4)]
    z_dev = [at((z + i) % 4, y, core) for i in range(4)]
    dp_dev, tp_dev = {"dp": 1 - dp}, {"tp": 1 - tp}

    barrier = pltpu.get_barrier_semaphore()
    partners = [other, dp_dev, tp_dev] + y_dev[1:] + z_dev[1:]
    for partner in partners:
        pl.semaphore_signal(barrier, inc=1, device_id=partner, device_id_type=MESH)
    pl.semaphore_wait(barrier, len(partners))

    started = []

    def put(src, dst, device):
        i = len(started)
        copy = pltpu.make_async_remote_copy(
            src_ref=src, dst_ref=dst, send_sem=send.at[i], recv_sem=recv.at[i], device_id=device, device_id_type=MESH)
        copy.start()
        started.append(copy)
        return copy

    half = WIDTH // 2
    here, there = pl.multiple_of(tp * half, half), pl.multiple_of((1 - tp) * half, half)
    to_tp = put(both.at[:, pl.ds(there, half)], tp_in, tp_dev)

    jobs = [dict(src=small, width=128, first=0, stream=1, acc=acc_e, core=core_in_e, ring=ring_e, mid=mid_e,
                 ring2=ring2_e, fin=fin_e, dp=dp_in_e)]
    for k, array in enumerate((p0, p1, p2)):
        for stream in range(2):
            n = 2 * k + stream
            jobs.append(dict(src=array, width=256, first=512 * stream, stream=stream, acc=acc.at[n], core=core_in.at[n],
                             ring=ring.at[n], mid=mid.at[n], ring2=ring2.at[n], fin=fin.at[n], dp=dp_in.at[n]))

    for n, job in enumerate(jobs):
        job["core_copy"], job["own_copy"] = [], []
        for h in range(2):
            lanes = pl.ds(job["first"] + h * job["width"], job["width"])
            job["core_copy"].append(put(job["src"].at[:, :, 1 - core, :, lanes], job["core"].at[h], other))
            own = pltpu.make_async_copy(job["src"].at[:, :, core, :, lanes], job["acc"].at[h], local.at[2 * n + h])
            own.start()
            job["own_copy"].append(own)

    def chunk(ref, h, c, stream, stage):
        if stream == 0 and stage == 1:
            return ref.at[h, :, c]
        return ref.at[h, c]

    def place(job, stage):
        over_y = (job["stream"] == 0) == (stage == 1)
        return (y, y_dev) if over_y else (z, z_dev)

    def ring_start(job, ref, buffer, stage):
        p, dev = place(job, stage)
        s = job["stream"]
        job["m1"] = put(chunk(ref, 0, (p + 2) % 4, s, stage), buffer.at[0], dev[1])
        job["m1p"] = put(chunk(ref, 1, (p + 2) % 4, s, stage), buffer.at[1], dev[3])
        job["m2"] = put(chunk(ref, 1, (p + 1) % 4, s, stage), buffer.at[2], dev[1])
        job["m2p"] = put(chunk(ref, 0, (p + 3) % 4, s, stage), buffer.at[3], dev[3])

    def ring_middle(job, ref, buffer, stage):
        p, dev = place(job, stage)
        s = job["stream"]
        job["m1"].wait_recv()
        up = chunk(ref, 0, (p + 1) % 4, s, stage)
        up[...] = up[...] + buffer[0]
        job["m3"] = put(up, buffer.at[4], dev[1])
        job["m1p"].wait_recv()
        down = chunk(ref, 1, (p + 3) % 4, s, stage)
        down[...] = down[...] + buffer[1]
        job["m3p"] = put(down, buffer.at[5], dev[3])

    def ring_end(job, ref, buffer, stage, into):
        p, dev = place(job, stage)
        s = job["stream"]
        for name in ("m2", "m2p", "m3", "m3p"):
            job[name].wait_recv()
        into[0] = chunk(ref, 0, p, s, stage)[...] + buffer[3] + buffer[4]
        into[1] = chunk(ref, 1, p, s, stage)[...] + buffer[2] + buffer[5]

    for job in jobs:
        for h in range(2):
            job["own_copy"][h].wait()
            job["core_copy"][h].wait_recv()
            job["acc"][h] = job["acc"][h] + job["core"][h]
        ring_start(job, job["acc"], job["ring"], 1)
    for job in jobs:
        ring_middle(job, job["acc"], job["ring"], 1)
    for job in jobs:
        ring_end(job, job["acc"], job["ring"], 1, job["mid"])
        ring_start(job, job["mid"], job["ring2"], 2)
    for job in jobs:
        ring_middle(job, job["mid"], job["ring2"], 2)
    mine = pl.ds(pl.multiple_of(16 * dp, 16), 16)
    yours = pl.ds(pl.multiple_of(16 * (1 - dp), 16), 16)
    for job in jobs:
        ring_end(job, job["mid"], job["ring2"], 2, job["fin"])
        job["dp_copy"] = put(job["fin"].at[:, yours, :], job["dp"], dp_dev)

    job = jobs[0]
    job["dp_copy"].wait_recv()
    for h in range(2):
        piece[0, mine, 128 * h:128 * h + 128] = job["fin"][h, mine, :] + job["dp"][h]
    over_tp = put(piece.at[0, mine, :], tp_in_e, tp_dev)
    for k in range(3):
        for stream in range(2):
            done = jobs[1 + 2 * k + stream]
            done["dp_copy"].wait_recv()
            for h in range(2):
                first = 512 * stream + 256 * h
                grads_out[k, :, first:first + 256] = done["fin"][h, mine, :] + done["dp"][h]
    over_tp.wait_recv()
    piece[1, mine, :] = piece[0, mine, :] + tp_in_e[...]
    put(piece.at[1, mine, :], piece.at[1, mine, :], dp_dev).wait_recv()
    row[y] = piece[1]
    for copy in [put(piece.at[1], row.at[y], dev) for dev in y_dev[1:]]:
        copy.wait_recv()
    small_out[z, :, core] = row[...]
    for copy in [put(row, small_out.at[z, :, core], dev) for dev in z_dev[1:]]:
        copy.wait_recv()
    put(small_out.at[:, :, core], small_out.at[:, :, core], other).wait_recv()

    to_tp.wait_recv()
    stream_out[...] = both[:, pl.ds(here, half)] + tp_in[...]
    for copy in started:
        copy.wait_send()


def sum_all(p0, p1, p2, small, both):
    def cut(array):
        return array.reshape(4, 4, 2, 32, array.shape[1])

    vmem, anywhere = pl.BlockSpec(memory_space=pltpu.VMEM), pl.BlockSpec(memory_space=pl.ANY)

    def buffers(lead, width):
        return [pltpu.VMEM(lead + shape + (32, width), F32) for shape in ((2, 4, 4), (2, 4, 4), (6, 4), (2, 4), (6,), (2,))
                ] + [pltpu.VMEM(lead + (2, 16, width), F32)]

    return pl.pallas_call(
        sum_kernel,
        out_shape=[
            jax.ShapeDtypeStruct((3, 16, WIDTH), F32),
            jax.ShapeDtypeStruct((4, 4, 2, 32, 256), F32),
            jax.ShapeDtypeStruct((BASES, WIDTH // 2), F32),
        ],
        in_specs=[anywhere] * 4 + [vmem],
        out_specs=[vmem] * 3,
        scratch_shapes=buffers((6,), 256) + buffers((), 128) + [
            pltpu.VMEM((BASES, WIDTH // 2), F32),
            pltpu.VMEM((16, 256), F32),
            pltpu.VMEM((2, 32, 256), F32),
            pltpu.VMEM((4, 32, 256), F32),
            pltpu.SemaphoreType.DMA((SEMS,)),
            pltpu.SemaphoreType.DMA((SEMS,)),
            pltpu.SemaphoreType.DMA((14,)),
        ],
        compiler_params=pltpu.CompilerParams(collective_id=1, has_side_effects=True, vmem_limit_bytes=48 << 20),
        name="sum_all",
    )(cut(p0), cut(p1), cut(p2), cut(small), both)


def body(base_ids, stream, cotangent, table, gain, projections, mixer_weight, step_weight, step_bias, rate):
    bases = base_ids[0]
    letters = jnp.arange(5, dtype=jnp.int32)
    own = bases[:, None] == letters[None, :]
    paired = jnp.where(bases == 4, 4, 3 - bases)[:, None] == letters[None, :]
    incoming = stream[0].astype(F32)
    upstream = cotangent[0]
    w = jnp.transpose(projections, (1, 0, 2))

    def picked(hot):
        return sum(jnp.where(hot[:, k:k + 1], table[k][None, :], 0.0) for k in range(5))

    embedded = jnp.concatenate([incoming + picked(own), incoming + picked(paired)], axis=0)
    inv_scale = lax.rsqrt(jnp.mean(embedded * embedded, axis=1, keepdims=True) + EPS)
    normed = embedded * inv_scale
    features = (normed * gain[None, :]).astype(BF16)
    v = dot(features, w[0])
    g = dot(features, w[1])
    gg = dot(upstream, w[2])
    mapped = dot(features, mixer_weight)
    logit = (dot(features, step_weight) + step_bias[None, :]).reshape(2, BASES, HEADS)
    step = jax.nn.softplus(logit)
    log_decay = -step * rate
    index = lax.broadcasted_iota(jnp.int32, (BASES, BASES), 0) - lax.broadcasted_iota(jnp.int32, (BASES, BASES), 1)
    run = jnp.stack([exact((index >= 0).astype(F32), log_decay[0]), exact((index <= 0).astype(F32), log_decay[1])])
    final = jnp.stack([run[0, BASES - 1], run[1, 0]])
    tail = jnp.exp(final[:, None, :] - run)
    head = jnp.exp(run)
    inflow, readout = mapped[:, :STATE].reshape(2, BASES, STATE), mapped[:, STATE:].reshape(2, BASES, STATE)

    def wide(small):
        return jnp.repeat(small, 64, axis=1)

    def pieces(d):
        rows = slice(BASES * d, BASES * (d + 1))
        decay = jnp.broadcast_to(wide(jnp.exp(final[d])[None]).reshape(PAIRS, 1, 128), (PAIRS, 8, 128))
        state = tn(inflow[d].astype(BF16), (v[rows] * wide(step[d] * tail[d])).astype(BF16))
        grad = tn(readout[d].astype(BF16), (gg * jax.nn.silu(g[rows]) * wide(head[d])).astype(BF16))
        return [jnp.concatenate([a.reshape(STATE, PAIRS, 128).transpose(1, 0, 2), decay], axis=1) for a in (state, grad)]

    (s0, g0), (s1, g1) = pieces(0), pieces(1)
    states = exchange_states(jnp.concatenate([s0, g1, s1, g0], axis=0))
    gv, gate, gated, gm, glogit, grate = blocks(
        v, g, gg, run, jnp.transpose(run, (0, 2, 1)), step, logit, inflow, readout, states, rate[None])

    glogit_b = glogit.reshape(2 * BASES, HEADS).astype(BF16)
    gf = nt(gv, w[0]) + nt(gate, w[1]) + nt(gm, mixer_weight) + nt(glogit_b, step_weight)
    gn = gf * gain[None, :]
    ge = inv_scale * (gn - normed * jnp.mean(gn * normed, axis=1, keepdims=True))
    ge = ge + 0.5 * jnp.concatenate([upstream, upstream], axis=0).astype(F32)
    both = ge[:BASES] + ge[BASES:]
    ggain = jnp.sum(gf * normed, axis=0)
    hot = jnp.concatenate([own, paired], axis=0).astype(F32)
    gtable = lax.dot_general(ge, hot, (((0,), (0,)), ((), ())), preferred_element_type=F32, precision=HIGH)
    tp = lax.axis_index("tp")
    gstep = tn(features, glogit_b)
    heads_at = HEADS * tp
    gbias = jnp.sum(glogit, axis=(0, 1))
    grate = grate[0, 0] + grate[1, 0]
    rest = jnp.concatenate([ggain[:, None], gtable, jnp.zeros((WIDTH, 128 - 38), F32)], axis=1)
    scalars = jnp.zeros((32, 2), F32)
    scalars = lax.dynamic_update_slice(scalars, jnp.stack([gbias, grate], axis=1), (heads_at, 0))
    steps = lax.dynamic_update_slice(jnp.zeros((WIDTH, 32), F32), gstep, (0, heads_at))
    rest = jnp.concatenate([
        steps, ggain[:, None], gtable, jnp.pad(scalars, ((0, WIDTH - 32), (0, 0))), jnp.zeros((WIDTH, 88), F32)], axis=1)
    small = jnp.concatenate([tn(features, gm), rest], axis=1)
    up2 = jnp.concatenate([upstream, upstream], axis=0)
    grads, small, stream_grad = sum_all(tn(features, gv), tn(features, gate), tn(up2, gated), small, both)
    small = small.reshape(WIDTH, 256)
    heads = lax.dynamic_slice(small, (0, 128 + heads_at), (WIDTH, HEADS))
    pair = lax.dynamic_slice(small, (heads_at, 128 + 38), (HEADS, 2))
    return (
        jnp.transpose(grads, (1, 0, 2)),
        small[:, :128],
        heads,
        pair[:, 0],
        pair[:, 1],
        jnp.transpose(small[:, 161:166]),
        small[:, 160],
        stream_grad[None],
    )


def solution(mesh):
    return jax.shard_map(
        body,
        mesh=mesh,
        in_specs=(
            P("dp", "ctx"),
            P("dp", "ctx", None),
            P("dp", "ctx", None),
            P(),
            P(),
            P(None, None, "tp"),
            P(),
            P(None, "tp"),
            P("tp"),
            P("tp"),
        ),
        out_specs=(
            P(("ctx", "dp"), None, "tp"),
            P(),
            P(None, "tp"),
            P("tp"),
            P("tp"),
            P(),
            P(),
            P("dp", "ctx", "tp"),
        ),
        check_vma=False,
    )
```

```python
import functools

import jax
import jax.numpy as jnp
from jax import lax
from jax.experimental import pallas as pl
from jax.experimental.pallas import tpu as pltpu
from jax.sharding import PartitionSpec as P

EPS = 1e-05
HIGH = lax.Precision.HIGHEST
F32 = jnp.float32
BF16 = jnp.bfloat16
MESH = pl.DeviceIdType.MESH
BASES = 256
WIDTH = 1024
HEADS = 16
PAIRS = 8
STATE = 64


def nt(left, right):
    return lax.dot_general(left, right, (((1,), (1,)), ((), ())), preferred_element_type=F32)


def tn(left, right):
    return lax.dot_general(left, right, (((0,), (0,)), ((), ())), preferred_element_type=F32)


def dot(left, right):
    return jnp.dot(left, right, preferred_element_type=F32)


def exact(left, right):
    return jnp.dot(left, right, preferred_element_type=F32, precision=HIGH)


def split3(x):
    a = x.astype(BF16).astype(F32)
    b = (x - a).astype(BF16).astype(F32)
    return a, b, x - a - b


def split2(x):
    a = x.astype(BF16)
    return a, (x - a.astype(F32)).astype(BF16)


def summed3(x, ones):
    r = dot(jnp.concatenate(split3(x), axis=0).astype(BF16), ones)
    n = x.shape[0]
    return r[0:n] + r[n:2 * n] + r[2 * n:3 * n]


def iota(shape, dim):
    return lax.broadcasted_iota(jnp.int32, shape, dim)


def spreads(j):
    r, c = iota((128, 256), 0), iota((128, 256), 1)
    kind = (r >= 48).astype(jnp.int32) + (r >= 96).astype(jnp.int32)
    return jnp.logical_and(kind == c // 128, (r & 15) == 2 * j + (c & 127) // 64).astype(F32).astype(BF16)


def gathers(j, base):
    r, c = iota((128, 128), 0), iota((128, 128), 1)
    return (c == base + 2 * j + r // 64).astype(F32).astype(BF16)


def front_kernel(base, x, up, table, gain, w, mw, swt, bias, rate,
                 f_out, normed_out, inv_out, gv_out, gate_out, gated_out, mapped_out, logit_out, rate_out,
                 wv, tab, v, g, gg, quant, maps, maps_t, logit_t, step_t, drive_b, go_b, out, gd, pairs, acc, kk,
                 src, recv, scanned, res, wsem, send_a, recv_a, send_b, recv_b):
    me = lax.axis_index("ctx")
    count = 32
    barrier = pltpu.get_barrier_semaphore()

    def greet(s, c):
        pl.semaphore_signal(barrier, inc=1, device_id={"ctx": lax.rem(me + s, count)}, device_id_type=MESH)
        return c

    lax.fori_loop(1, count, greet, 0)
    copies = [pltpu.make_async_copy(w.at[k], wv.at[k], wsem.at[k]) for k in range(3)]
    for copy in copies:
        copy.start()

    tab[...] = jnp.zeros_like(tab)
    tab[0:5, :] = table[...]
    pieces = jnp.concatenate(split3(tab[...]), axis=0).astype(BF16)
    incoming = x[0].astype(F32)
    for d in range(2):
        ids = base[...]
        if d:
            ids = jnp.where(ids == 4, 4, 3 - ids)
        hot = (iota((8, BASES), 0) == ids).astype(F32)
        embedded = incoming + tn(jnp.concatenate([hot, hot, hot], axis=0).astype(BF16), pieces)
        inv = lax.rsqrt(jnp.mean(embedded * embedded, axis=1, keepdims=True) + EPS)
        normed = embedded * inv
        rows = slice(BASES * d, BASES * (d + 1))
        normed_out[rows, :] = normed
        inv_out[rows, :] = inv
        f_out[rows, :] = (normed * gain[...]).astype(BF16)

    mapped = dot(f_out[...], mw[...])
    for d in range(2):
        maps[d] = mapped[BASES * d:BASES * (d + 1)].astype(BF16)
        maps_t[d] = jnp.transpose(mapped[BASES * d:BASES * (d + 1)]).astype(BF16)
    logits = nt(swt[...], f_out[...]) + bias[...]
    rows_i, cols_i = iota((BASES, BASES), 0), iota((BASES, BASES), 1)
    for d in range(2):
        logit = logits[:, BASES * d:BASES * (d + 1)]
        step = jnp.maximum(logit, 0.0) + jnp.log1p(jnp.exp(-jnp.abs(logit)))
        logit_t[d] = logit
        step_t[d] = step
        upto = (rows_i <= cols_i) if d == 0 else (rows_i >= cols_i)
        run = summed3(-step * rate[...], upto.astype(F32).astype(BF16))
        whole = jnp.concatenate(split3(run) + split3(step) + (jnp.zeros((32, BASES), F32),), axis=0)
        quant[d] = jnp.transpose(whole).astype(BF16)
        pairs[d] = jnp.zeros((BASES, BASES), F32)
        acc[d] = jnp.zeros((BASES, 128), F32)
        kk[d] = jnp.zeros((8, 128), F32)
        src_rows = run
        logit_out[:, BASES * d:BASES * (d + 1)] = src_rows
    for k, target in ((0, v), (1, g)):
        copies[k].wait()
        for c in range(4):
            block = dot(f_out[...], wv[k, :, 256 * c:256 * c + 256])
            for d in range(2):
                for i in range(2):
                    target[d, 2 * c + i] = block[BASES * d:BASES * (d + 1), 128 * i:128 * i + 128]
    copies[2].wait()
    for c in range(4):
        block = dot(up[0], wv[2, :, 256 * c:256 * c + 256])
        for i in range(2):
            gg[2 * c + i] = block[:, 128 * i:128 * i + 128]

    def expand(d, j):
        both = dot(quant[d], spreads(j))
        run_e, step_e = both[:, 0:128], both[:, 128:256]
        final = run_e[BASES - 1:BASES] if d == 0 else run_e[0:1]
        return run_e, step_e, final

    def to_owner(t):
        return pltpu.make_async_remote_copy(
            src_ref=src.at[t], dst_ref=recv.at[me], send_sem=send_a.at[t], recv_sem=recv_a.at[me],
            device_id={"ctx": t}, device_id_type=MESH)

    def from_device(t):
        return pltpu.make_async_remote_copy(
            src_ref=src.at[t], dst_ref=recv.at[t], send_sem=send_a.at[t], recv_sem=recv_a.at[t],
            device_id={"ctx": t}, device_id_type=MESH)

    def back(t):
        return pltpu.make_async_remote_copy(
            src_ref=scanned.at[t], dst_ref=res.at[me], send_sem=send_b.at[t], recv_sem=recv_b.at[me],
            device_id={"ctx": t}, device_id_type=MESH)

    def from_owner(t):
        return pltpu.make_async_remote_copy(
            src_ref=scanned.at[t], dst_ref=res.at[t], send_sem=send_b.at[t], recv_sem=recv_b.at[t],
            device_id={"ctx": t}, device_id_type=MESH)

    pl.semaphore_wait(barrier, count - 1)
    for d in range(2):
        def ends(j, c, d=d):
            run_e, step_e, final = expand(d, j)
            drive = step_e * v[d, j]
            gates = g[d, j]
            go = gg[j] * (gates * jax.nn.sigmoid(gates))
            drive_b[d, j] = drive.astype(BF16)
            go_b[d, j] = go.astype(BF16)
            state = dot(maps_t[d, 0:64, :], (drive * jnp.exp(final - run_e)).astype(BF16))
            grad = dot(maps_t[d, 64:128, :], (go * jnp.exp(run_e)).astype(BF16))
            decay = jnp.broadcast_to(jnp.exp(final), (8, 128))
            for t, value in ((16 * d + j, state), (24 - 16 * d + j, grad)):
                src[t, 0:64, :] = value
                src[t, 64:72, :] = decay

                @pl.when(t != me)
                def _():
                    to_owner(t).start()
            return c

        lax.fori_loop(0, PAIRS, ends, 0)

    low = iota((BASES, 128), 1) < 64

    def inside(d):
        seen = (rows_i >= cols_i) if d == 0 else (rows_i <= cols_i)
        inflow_b, readout_b = maps[d, :, 0:64], maps[d, :, 64:128]
        affinity = nt(readout_b, inflow_b)

        def step(j, c):
            run_e, _, _ = expand(d, j)
            drive, go = drive_b[d, j], go_b[d, j]
            zero = jnp.zeros_like(drive)
            output = grad_drive = total = None
            for half in range(2):
                mine = low if half == 0 else jnp.logical_not(low)
                row = logit_out[pl.ds(2 * j + half, 1), BASES * d:BASES * (d + 1)]
                column = run_e[:, 64 * half:64 * half + 1]
                decay = jnp.exp(jnp.where(seen, column - row, -1e30))
                mixing = (decay * affinity).astype(BF16)
                drive_h = jnp.where(mine, drive, zero)
                go_h = jnp.where(mine, go, zero)
                a, b, e = dot(mixing, drive_h), tn(mixing, go_h), decay * nt(go_h, drive)
                output = a if output is None else output + a
                grad_drive = b if grad_drive is None else grad_drive + b
                total = e if total is None else total + e
            out[d, j] = output
            gd[d, j] = grad_drive
            pairs[d] += total
            return c

        lax.fori_loop(0, PAIRS, step, 0)

    inside(0)

    def wait_a(s, c):
        t = lax.rem(me + s, count)
        from_device(t).wait_recv()
        return c

    recv[me] = src[me]
    lax.fori_loop(1, count, wait_a, 0)
    falling = me // 16

    def scan(i, carry):
        t = i + falling * (count - 1 - 2 * i)
        scanned[t] = carry

        @pl.when(t != me)
        def _():
            back(t).start()
        return carry * recv[t, 64:65, :] + recv[t, 0:64, :]

    lax.fori_loop(0, count, scan, jnp.zeros((STATE, 128), F32))
    res[me] = scanned[me]

    inside(1)

    def wait_b(s, c):
        t = lax.rem(me + s, count)
        from_owner(t).wait_recv()
        return c

    lax.fori_loop(1, count, wait_b, 0)

    for d in range(2):
        rows = slice(BASES * d, BASES * (d + 1))
        inflow_b, readout_b = maps[d, :, 0:64], maps[d, :, 64:128]

        def outside(j, c, d=d, rows=rows, inflow_b=inflow_b, readout_b=readout_b):
            gin, gread = c
            run_e, step_e, final = expand(d, j)
            initial, after = res[16 * d + j], res[24 - 16 * d + j]
            initial_b, after_b = initial.astype(BF16), after.astype(BF16)
            head, tail = jnp.exp(run_e), jnp.exp(final - run_e)
            drive_r, go_r = drive_b[d, j].astype(F32), go_b[d, j].astype(F32)
            carried = dot(readout_b, initial_b) * head
            output = out[d, j] + carried
            grad_drive = gd[d, j] + dot(inflow_b, after_b) * tail
            values, gates, grad_gated = v[d, j], g[d, j], gg[j]
            sigma = jax.nn.sigmoid(gates)
            swish = gates * sigma
            a, b = split2(grad_drive * drive_r - go_r * output)
            p, q = split2(grad_drive * values)
            acc[d] += dot(a, gathers(j, 0)) + dot(b, gathers(j, 0)) + dot(p, gathers(j, 16)) + dot(q, gathers(j, 16))
            boundary = jnp.sum(go_r * carried, axis=0, keepdims=True) + jnp.exp(final) * jnp.sum(
                initial * after, axis=0, keepdims=True)
            a, b = split2(jnp.broadcast_to(boundary, (16, 128)))
            kk[d] += (dot(a, gathers(j, 32)) + dot(b, gathers(j, 32)))[0:8]
            gin = gin + nt((drive_r * tail).astype(BF16), after_b)
            gread = gread + nt((go_r * head).astype(BF16), initial_b)
            lanes = pl.ds(pl.multiple_of(128 * j, 128), 128)
            gv_out[rows, lanes] = (step_e * grad_drive).astype(BF16)
            gate_out[rows, lanes] = (grad_gated * output * sigma * (1.0 + gates * (1.0 - sigma))).astype(BF16)
            gated_out[rows, lanes] = (output * swish).astype(BF16)
            return gin, gread

        zeros = jnp.zeros((BASES, STATE), F32)
        gin, gread = lax.fori_loop(0, PAIRS, outside, (zeros, zeros))
        pairs_b = pairs[d].astype(BF16)
        gin = gin + tn(pairs_b, readout_b)
        gread = gread + dot(pairs_b, inflow_b)
        mapped_out[rows, :] = jnp.concatenate([gin, gread], axis=1).astype(BF16)
        per_head = jnp.transpose(acc[d] + kk[d, 0:1, :])
        earlier = (rows_i < cols_i) if d == 0 else (rows_i > cols_i)
        grad_log = summed3(per_head[0:16], earlier.astype(F32).astype(BF16)) + per_head[32:48]
        grad_step = per_head[16:32] - grad_log * rate[...]
        logit_out[:, rows] = grad_step * jax.nn.sigmoid(logit_t[d])
        rate_out[:, d:d + 1] = -jnp.sum(grad_log * step_t[d], axis=1, keepdims=True)

    def wait_sent(s, c):
        t = lax.rem(me + s, count)
        to_owner(t).wait_send()
        back(t).wait_send()
        return c

    lax.fori_loop(1, count, wait_sent, 0)


def front(base, stream, cotangent, table, gain, w, mw, swt, bias, rate):
    vmem, anywhere = pl.BlockSpec(memory_space=pltpu.VMEM), pl.BlockSpec(memory_space=pl.ANY)
    rows = 2 * BASES

    def shape(*dims, kind=F32):
        return jax.ShapeDtypeStruct(dims, kind)

    return pl.pallas_call(
        front_kernel,
        out_shape=[
            shape(rows, WIDTH, kind=BF16), shape(rows, WIDTH), shape(rows, 1),
            shape(rows, WIDTH, kind=BF16), shape(rows, WIDTH, kind=BF16), shape(rows, WIDTH, kind=BF16),
            shape(rows, 128, kind=BF16), shape(HEADS, rows), shape(HEADS, 2),
        ],
        in_specs=[vmem] * 5 + [anywhere] + [vmem] * 4,
        out_specs=[vmem] * 9,
        scratch_shapes=[
            pltpu.VMEM((3, WIDTH, WIDTH), BF16),
            pltpu.VMEM((8, WIDTH), F32),
            pltpu.VMEM((2, PAIRS, BASES, 128), F32),
            pltpu.VMEM((2, PAIRS, BASES, 128), F32),
            pltpu.VMEM((PAIRS, BASES, 128), F32),
            pltpu.VMEM((2, BASES, 128), BF16),
            pltpu.VMEM((2, BASES, 128), BF16),
            pltpu.VMEM((2, 128, BASES), BF16),
            pltpu.VMEM((2, HEADS, BASES), F32),
            pltpu.VMEM((2, HEADS, BASES), F32),
            pltpu.VMEM((2, PAIRS, BASES, 128), BF16),
            pltpu.VMEM((2, PAIRS, BASES, 128), BF16),
            pltpu.VMEM((2, PAIRS, BASES, 128), F32),
            pltpu.VMEM((2, PAIRS, BASES, 128), F32),
            pltpu.VMEM((2, BASES, BASES), F32),
            pltpu.VMEM((2, BASES, 128), F32),
            pltpu.VMEM((2, 8, 128), F32),
            pltpu.VMEM((32, 72, 128), F32),
            pltpu.VMEM((32, 72, 128), F32),
            pltpu.VMEM((32, STATE, 128), F32),
            pltpu.VMEM((32, STATE, 128), F32),
            pltpu.SemaphoreType.DMA((3,)),
            pltpu.SemaphoreType.DMA((32,)),
            pltpu.SemaphoreType.DMA((32,)),
            pltpu.SemaphoreType.DMA((32,)),
            pltpu.SemaphoreType.DMA((32,)),
        ],
        compiler_params=pltpu.CompilerParams(collective_id=0, has_side_effects=True, vmem_limit_bytes=56 << 20),
        name="front",
    )(base, stream, cotangent, table, gain, w, mw, swt, bias, rate)


SEMS = 128


def sum_kernel(p0, p1, p2, small, both, grads_out, small_out, stream_out,
               acc, core_in, ring, mid, ring2, fin, dp_in,
               acc_e, core_in_e, ring_e, mid_e, ring2_e, fin_e, dp_in_e,
               tp_in, tp_in_e, piece, row, send, recv, local):
    ctx, tp, dp = lax.axis_index("ctx"), lax.axis_index("tp"), lax.axis_index("dp")
    core, y, z = ctx % 2, (ctx // 2) % 4, ctx // 8

    def at(zz, yy, cc):
        return {"ctx": (zz * 4 + yy) * 2 + cc}

    other = at(z, y, 1 - core)
    y_dev = [at(z, (y + i) % 4, core) for i in range(4)]
    z_dev = [at((z + i) % 4, y, core) for i in range(4)]
    dp_dev, tp_dev = {"dp": 1 - dp}, {"tp": 1 - tp}

    barrier = pltpu.get_barrier_semaphore()
    partners = [other, dp_dev, tp_dev] + y_dev[1:] + z_dev[1:]
    for partner in partners:
        pl.semaphore_signal(barrier, inc=1, device_id=partner, device_id_type=MESH)
    pl.semaphore_wait(barrier, len(partners))

    started = []

    def put(src, dst, device):
        i = len(started)
        copy = pltpu.make_async_remote_copy(
            src_ref=src, dst_ref=dst, send_sem=send.at[i], recv_sem=recv.at[i], device_id=device, device_id_type=MESH)
        copy.start()
        started.append(copy)
        return copy

    half = WIDTH // 2
    here, there = pl.multiple_of(tp * half, half), pl.multiple_of((1 - tp) * half, half)
    to_tp = put(both.at[:, pl.ds(there, half)], tp_in, tp_dev)

    jobs = [dict(src=small, width=128, first=0, stream=1, acc=acc_e, core=core_in_e, ring=ring_e, mid=mid_e,
                 ring2=ring2_e, fin=fin_e, dp=dp_in_e)]
    for k, array in enumerate((p0, p1, p2)):
        for stream in range(2):
            n = 2 * k + stream
            jobs.append(dict(src=array, width=256, first=512 * stream, stream=stream, acc=acc.at[n], core=core_in.at[n],
                             ring=ring.at[n], mid=mid.at[n], ring2=ring2.at[n], fin=fin.at[n], dp=dp_in.at[n]))

    for n, job in enumerate(jobs):
        job["core_copy"], job["own_copy"] = [], []
        for h in range(2):
            lanes = pl.ds(job["first"] + h * job["width"], job["width"])
            job["core_copy"].append(put(job["src"].at[:, :, 1 - core, :, lanes], job["core"].at[h], other))
            own = pltpu.make_async_copy(job["src"].at[:, :, core, :, lanes], job["acc"].at[h], local.at[2 * n + h])
            own.start()
            job["own_copy"].append(own)

    def chunk(ref, h, c, stream, stage):
        if stream == 0 and stage == 1:
            return ref.at[h, :, c]
        return ref.at[h, c]

    def place(job, stage):
        over_y = (job["stream"] == 0) == (stage == 1)
        return (y, y_dev) if over_y else (z, z_dev)

    def ring_start(job, ref, buffer, stage):
        p, dev = place(job, stage)
        s = job["stream"]
        job["m1"] = put(chunk(ref, 0, (p + 2) % 4, s, stage), buffer.at[0], dev[1])
        job["m1p"] = put(chunk(ref, 1, (p + 2) % 4, s, stage), buffer.at[1], dev[3])
        job["m2"] = put(chunk(ref, 1, (p + 1) % 4, s, stage), buffer.at[2], dev[1])
        job["m2p"] = put(chunk(ref, 0, (p + 3) % 4, s, stage), buffer.at[3], dev[3])

    def ring_middle(job, ref, buffer, stage):
        p, dev = place(job, stage)
        s = job["stream"]
        job["m1"].wait_recv()
        up = chunk(ref, 0, (p + 1) % 4, s, stage)
        up[...] = up[...] + buffer[0]
        job["m3"] = put(up, buffer.at[4], dev[1])
        job["m1p"].wait_recv()
        down = chunk(ref, 1, (p + 3) % 4, s, stage)
        down[...] = down[...] + buffer[1]
        job["m3p"] = put(down, buffer.at[5], dev[3])

    def ring_end(job, ref, buffer, stage, into):
        p, dev = place(job, stage)
        s = job["stream"]
        for name in ("m2", "m2p", "m3", "m3p"):
            job[name].wait_recv()
        into[0] = chunk(ref, 0, p, s, stage)[...] + buffer[3] + buffer[4]
        into[1] = chunk(ref, 1, p, s, stage)[...] + buffer[2] + buffer[5]

    for job in jobs:
        for h in range(2):
            job["own_copy"][h].wait()
            job["core_copy"][h].wait_recv()
            job["acc"][h] = job["acc"][h] + job["core"][h]
        ring_start(job, job["acc"], job["ring"], 1)
    for job in jobs:
        ring_middle(job, job["acc"], job["ring"], 1)
    for job in jobs:
        ring_end(job, job["acc"], job["ring"], 1, job["mid"])
        ring_start(job, job["mid"], job["ring2"], 2)
    for job in jobs:
        ring_middle(job, job["mid"], job["ring2"], 2)
    mine = pl.ds(pl.multiple_of(16 * dp, 16), 16)
    yours = pl.ds(pl.multiple_of(16 * (1 - dp), 16), 16)
    for job in jobs:
        ring_end(job, job["mid"], job["ring2"], 2, job["fin"])
        job["dp_copy"] = put(job["fin"].at[:, yours, :], job["dp"], dp_dev)

    job = jobs[0]
    job["dp_copy"].wait_recv()
    for h in range(2):
        piece[0, mine, 128 * h:128 * h + 128] = job["fin"][h, mine, :] + job["dp"][h]
    over_tp = put(piece.at[0, mine, :], tp_in_e, tp_dev)
    for k in range(3):
        for stream in range(2):
            done = jobs[1 + 2 * k + stream]
            done["dp_copy"].wait_recv()
            for h in range(2):
                first = 512 * stream + 256 * h
                grads_out[k, :, first:first + 256] = done["fin"][h, mine, :] + done["dp"][h]
    over_tp.wait_recv()
    piece[1, mine, :] = piece[0, mine, :] + tp_in_e[...]
    put(piece.at[1, mine, :], piece.at[1, mine, :], dp_dev).wait_recv()
    row[y] = piece[1]
    for copy in [put(piece.at[1], row.at[y], dev) for dev in y_dev[1:]]:
        copy.wait_recv()
    small_out[z, :, core] = row[...]
    for copy in [put(row, small_out.at[z, :, core], dev) for dev in z_dev[1:]]:
        copy.wait_recv()
    put(small_out.at[:, :, core], small_out.at[:, :, core], other).wait_recv()

    to_tp.wait_recv()
    stream_out[...] = both[:, pl.ds(here, half)] + tp_in[...]
    for copy in started:
        copy.wait_send()


def sum_all(p0, p1, p2, small, both):
    def cut(array):
        return array.reshape(4, 4, 2, 32, array.shape[1])

    vmem, anywhere = pl.BlockSpec(memory_space=pltpu.VMEM), pl.BlockSpec(memory_space=pl.ANY)

    def buffers(lead, width):
        return [pltpu.VMEM(lead + shape + (32, width), F32) for shape in ((2, 4, 4), (2, 4, 4), (6, 4), (2, 4), (6,), (2,))
                ] + [pltpu.VMEM(lead + (2, 16, width), F32)]

    return pl.pallas_call(
        sum_kernel,
        out_shape=[
            jax.ShapeDtypeStruct((3, 16, WIDTH), F32),
            jax.ShapeDtypeStruct((4, 4, 2, 32, 256), F32),
            jax.ShapeDtypeStruct((BASES, WIDTH // 2), F32),
        ],
        in_specs=[anywhere] * 4 + [vmem],
        out_specs=[vmem] * 3,
        scratch_shapes=buffers((6,), 256) + buffers((), 128) + [
            pltpu.VMEM((BASES, WIDTH // 2), F32),
            pltpu.VMEM((16, 256), F32),
            pltpu.VMEM((2, 32, 256), F32),
            pltpu.VMEM((4, 32, 256), F32),
            pltpu.SemaphoreType.DMA((SEMS,)),
            pltpu.SemaphoreType.DMA((SEMS,)),
            pltpu.SemaphoreType.DMA((14,)),
        ],
        compiler_params=pltpu.CompilerParams(collective_id=1, has_side_effects=True, vmem_limit_bytes=48 << 20),
        name="sum_all",
    )(cut(p0), cut(p1), cut(p2), cut(small), both)


def body(base_ids, stream, cotangent, table, gain, projections, mixer_weight, step_weight, step_bias, rate):
    bases = base_ids[0]
    letters = jnp.arange(5, dtype=jnp.int32)
    own = bases[:, None] == letters[None, :]
    paired = jnp.where(bases == 4, 4, 3 - bases)[:, None] == letters[None, :]
    upstream = cotangent[0]
    w = jnp.transpose(projections, (1, 0, 2))
    features, normed, inv_scale, gv, gate, gated, gm, glogit, grate = front(
        base_ids, stream, cotangent, table, gain[None], w, mixer_weight, jnp.transpose(step_weight),
        step_bias[:, None], rate[:, None])

    glogit_b = jnp.transpose(glogit).astype(BF16)
    gf = nt(gv, w[0]) + nt(gate, w[1]) + nt(gm, mixer_weight) + nt(glogit_b, step_weight)
    gn = gf * gain[None, :]
    ge = inv_scale * (gn - normed * jnp.mean(gn * normed, axis=1, keepdims=True))
    ge = ge + 0.5 * jnp.concatenate([upstream, upstream], axis=0).astype(F32)
    both = ge[:BASES] + ge[BASES:]
    ggain = jnp.sum(gf * normed, axis=0)
    hot = jnp.concatenate([own, paired], axis=0).astype(F32)
    gtable = lax.dot_general(ge, hot, (((0,), (0,)), ((), ())), preferred_element_type=F32, precision=HIGH)
    tp = lax.axis_index("tp")
    gstep = tn(features, glogit_b)
    heads_at = HEADS * tp
    gbias = jnp.sum(glogit, axis=1)
    grate = jnp.sum(grate, axis=1)
    scalars = jnp.zeros((32, 2), F32)
    scalars = lax.dynamic_update_slice(scalars, jnp.stack([gbias, grate], axis=1), (heads_at, 0))
    steps = lax.dynamic_update_slice(jnp.zeros((WIDTH, 32), F32), gstep, (0, heads_at))
    rest = jnp.concatenate([
        steps, ggain[:, None], gtable, jnp.pad(scalars, ((0, WIDTH - 32), (0, 0))), jnp.zeros((WIDTH, 88), F32)], axis=1)
    small = jnp.concatenate([tn(features, gm), rest], axis=1)
    up2 = jnp.concatenate([upstream, upstream], axis=0)
    grads, small, stream_grad = sum_all(tn(features, gv), tn(features, gate), tn(up2, gated), small, both)
    small = small.reshape(WIDTH, 256)
    heads = lax.dynamic_slice(small, (0, 128 + heads_at), (WIDTH, HEADS))
    pair = lax.dynamic_slice(small, (heads_at, 128 + 38), (HEADS, 2))
    return (
        jnp.transpose(grads, (1, 0, 2)),
        small[:, :128],
        heads,
        pair[:, 0],
        pair[:, 1],
        jnp.transpose(small[:, 161:166]),
        small[:, 160],
        stream_grad[None],
    )


def solution(mesh):
    return jax.shard_map(
        body,
        mesh=mesh,
        in_specs=(
            P("dp", "ctx"),
            P("dp", "ctx", None),
            P("dp", "ctx", None),
            P(),
            P(),
            P(None, None, "tp"),
            P(),
            P(None, "tp"),
            P("tp"),
            P("tp"),
        ),
        out_specs=(
            P(("ctx", "dp"), None, "tp"),
            P(),
            P(None, "tp"),
            P("tp"),
            P("tp"),
            P(),
            P(),
            P("dp", "ctx", "tp"),
        ),
        check_vma=False,
    )
```

```python
import functools

import jax
import jax.numpy as jnp
from jax import lax
from jax.experimental import pallas as pl
from jax.experimental.pallas import tpu as pltpu
from jax.sharding import PartitionSpec as P

EPS = 1e-05
HIGH = lax.Precision.HIGHEST
F32 = jnp.float32
BF16 = jnp.bfloat16
MESH = pl.DeviceIdType.MESH
BASES = 256
WIDTH = 1024
HEADS = 16
PAIRS = 8
STATE = 64


def nt(left, right):
    return lax.dot_general(left, right, (((1,), (1,)), ((), ())), preferred_element_type=F32)


def tn(left, right):
    return lax.dot_general(left, right, (((0,), (0,)), ((), ())), preferred_element_type=F32)


def dot(left, right):
    return jnp.dot(left, right, preferred_element_type=F32)


def exact(left, right):
    return jnp.dot(left, right, preferred_element_type=F32, precision=HIGH)


def split3(x):
    a = x.astype(BF16).astype(F32)
    b = (x - a).astype(BF16).astype(F32)
    return a, b, x - a - b


def split2(x):
    a = x.astype(BF16)
    return a, (x - a.astype(F32)).astype(BF16)


def summed3(x, ones):
    r = dot(jnp.concatenate(split3(x), axis=0).astype(BF16), ones)
    n = x.shape[0]
    return r[0:n] + r[n:2 * n] + r[2 * n:3 * n]


def iota(shape, dim):
    return lax.broadcasted_iota(jnp.int32, shape, dim)


def spreads(j):
    r, c = iota((128, 256), 0), iota((128, 256), 1)
    kind = (r >= 48).astype(jnp.int32) + (r >= 96).astype(jnp.int32)
    return jnp.logical_and(kind == c // 128, (r & 15) == 2 * j + (c & 127) // 64).astype(F32).astype(BF16)


def gathers(j, base):
    r, c = iota((128, 128), 0), iota((128, 128), 1)
    return (c == base + 2 * j + r // 64).astype(F32).astype(BF16)


CHIPS = 16
SEMS = 216
ORDER = [(q, k) for q in range(4) for k in (2, 1, 0)]


def main_kernel(base, x, up, table, gain, w, mw, swt, bias, rate,
                grads_out, mixer_out, step_out, table_out, gain_out, scalars_out, stream_out,
                wv, tab, f, normed_s, inv_s, v, g, gg, quant, run_t, maps, maps_t, logit_t, step_t, drive_b, go_b, out, gd, pairs,
                acc, kk, gins, greads, src, from_core, totals, recv, scanned, res, ent, ent_out,
                gv, gate, gated, gm, glt, rates, ft, upt, rt, prod, core_in, ring, mid, ring2, fin, dp_in,
                prod_e, core_e, parts, mine_e, x_in, all_e, tp_in,
                wsem, send_c, recv_c, send_a, recv_a, send_b, recv_b, send_d, recv_d, send, receive):
    ctx, tp, dp = lax.axis_index("ctx"), lax.axis_index("tp"), lax.axis_index("dp")
    core, chip = ctx % 2, ctx // 2
    y, z = chip % 4, chip // 4

    def on(c):
        return {"ctx": c * 2 + core}

    other = {"ctx": chip * 2 + 1 - core}
    tp_dev, dp_dev, far_dev = {"tp": 1 - tp}, {"dp": 1 - dp}, {"tp": 1 - tp, "dp": 1 - dp}
    y_dev = [on(z * 4 + (y + i) % 4) for i in range(4)]
    z_dev = [on(((z + i) % 4) * 4 + y) for i in range(4)]

    barrier = pltpu.get_barrier_semaphore()

    def greet(i, c):
        pl.semaphore_signal(barrier, inc=1, device_id=on(lax.rem(chip + i, CHIPS)), device_id_type=MESH)
        return c

    lax.fori_loop(1, CHIPS, greet, 0)
    for device in (other, tp_dev, dp_dev, far_dev):
        pl.semaphore_signal(barrier, inc=1, device_id=device, device_id_type=MESH)
    copies = [pltpu.make_async_copy(w.at[k], wv.at[k], wsem.at[k]) for k in range(3)]
    for copy in copies:
        copy.start()

    tab[...] = jnp.zeros_like(tab)
    tab[0:5, :] = table[...]
    pieces = jnp.concatenate(split3(tab[...]), axis=0).astype(BF16)
    incoming = x[0].astype(F32)
    hots = []
    for d in range(2):
        ids = base[...]
        if d:
            ids = jnp.where(ids == 4, 4, 3 - ids)
        hot = (iota((8, BASES), 0) == ids).astype(F32)
        hots.append(hot.astype(BF16))
        embedded = incoming + tn(jnp.concatenate([hot, hot, hot], axis=0).astype(BF16), pieces)
        inv = lax.rsqrt(jnp.mean(embedded * embedded, axis=1, keepdims=True) + EPS)
        normed = embedded * inv
        rows = slice(BASES * d, BASES * (d + 1))
        normed_s[rows, :] = normed
        inv_s[rows, :] = inv
        f[rows, :] = (normed * gain[...]).astype(BF16)

    def column(row):
        square = jnp.broadcast_to(row, (HEADS, HEADS))
        return jnp.sum(jnp.where(iota((HEADS, HEADS), 0) == iota((HEADS, HEADS), 1), square, 0.0), axis=1, keepdims=True)

    rate_c = column(rate[...])
    mapped = dot(f[...], mw[...])
    for d in range(2):
        maps[d] = mapped[BASES * d:BASES * (d + 1)].astype(BF16)
        maps_t[d] = jnp.transpose(mapped[BASES * d:BASES * (d + 1)]).astype(BF16)
    logits = nt(swt[...], f[...]) + column(bias[...])
    rows_i, cols_i = iota((BASES, BASES), 0), iota((BASES, BASES), 1)
    for d in range(2):
        logit = logits[:, BASES * d:BASES * (d + 1)]
        step = jnp.maximum(logit, 0.0) + jnp.log1p(jnp.exp(-jnp.abs(logit)))
        logit_t[d] = logit
        step_t[d] = step
        upto = (rows_i <= cols_i) if d == 0 else (rows_i >= cols_i)
        run = summed3(-step * rate_c, upto.astype(F32).astype(BF16))
        run_t[d] = run
        whole = jnp.concatenate(split3(run) + split3(step) + (jnp.zeros((32, BASES), F32),), axis=0)
        quant[d] = jnp.transpose(whole).astype(BF16)
        pairs[d] = jnp.zeros((BASES, BASES), F32)
        acc[d] = jnp.zeros((BASES, 128), F32)
        kk[d] = jnp.zeros((8, 128), F32)
        gins[d] = jnp.zeros((BASES, STATE), F32)
        greads[d] = jnp.zeros((BASES, STATE), F32)
    for k, target in ((0, v), (1, g)):
        copies[k].wait()
        for c in range(4):
            block = dot(f[...], wv[k, :, 256 * c:256 * c + 256])
            for d in range(2):
                for i in range(2):
                    target[d, 2 * c + i] = block[BASES * d:BASES * (d + 1), 128 * i:128 * i + 128]
    copies[2].wait()
    for c in range(4):
        block = dot(up[0], wv[2, :, 256 * c:256 * c + 256])
        for i in range(2):
            gg[2 * c + i] = block[:, 128 * i:128 * i + 128]

    def expand(d, j):
        both = dot(quant[d], spreads(j))
        run_e, step_e = both[:, 0:128], both[:, 128:256]
        final = run_e[BASES - 1:BASES] if d == 0 else run_e[0:1]
        return run_e, step_e, final

    def to_core(i):
        return pltpu.make_async_remote_copy(
            src_ref=src.at[CHIPS * (1 - core) + i], dst_ref=from_core.at[i], send_sem=send_c.at[i], recv_sem=recv_c.at[i],
            device_id=other, device_id_type=MESH)

    def to_owner(i):
        return pltpu.make_async_remote_copy(
            src_ref=totals.at[i], dst_ref=recv.at[chip], send_sem=send_a.at[i], recv_sem=recv_a.at[chip],
            device_id=on(i), device_id_type=MESH)

    def from_chip(i):
        return pltpu.make_async_remote_copy(
            src_ref=totals.at[i], dst_ref=recv.at[i], send_sem=send_a.at[i], recv_sem=recv_a.at[i],
            device_id=on(i), device_id_type=MESH)

    def to_chip(i):
        return pltpu.make_async_remote_copy(
            src_ref=scanned.at[i], dst_ref=res.at[chip], send_sem=send_b.at[i], recv_sem=recv_b.at[chip],
            device_id=on(i), device_id_type=MESH)

    def from_owner(i):
        return pltpu.make_async_remote_copy(
            src_ref=scanned.at[i], dst_ref=res.at[i], send_sem=send_b.at[i], recv_sem=recv_b.at[i],
            device_id=on(i), device_id_type=MESH)

    def entering(i):
        return pltpu.make_async_remote_copy(
            src_ref=ent_out.at[i], dst_ref=ent.at[CHIPS * core + i], send_sem=send_d.at[i], recv_sem=recv_d.at[i],
            device_id=other, device_id_type=MESH)

    def entered(i):
        return pltpu.make_async_remote_copy(
            src_ref=ent_out.at[i], dst_ref=ent.at[CHIPS * (1 - core) + i], send_sem=send_d.at[i], recv_sem=recv_d.at[i],
            device_id=other, device_id_type=MESH)

    pl.semaphore_wait(barrier, CHIPS + 3)
    for d in range(2):
        def ends(j, c, d=d):
            run_e, step_e, final = expand(d, j)
            drive = step_e * v[d, j]
            gates = g[d, j]
            go = gg[j] * (gates * jax.nn.sigmoid(gates))
            drive_b[d, j] = drive.astype(BF16)
            go_b[d, j] = go.astype(BF16)
            state = dot(maps_t[d, 0:64, :], (drive * jnp.exp(final - run_e)).astype(BF16))
            grad = dot(maps_t[d, 64:128, :], (go * jnp.exp(run_e)).astype(BF16))
            decay = jnp.broadcast_to(jnp.exp(final), (8, 128))
            for t, value in ((16 * d + j, state), (24 - 16 * d + j, grad)):
                src[t, 0:64, :] = value
                src[t, 64:72, :] = decay
            to_core(j + 8 * (1 - core) if d == 0 else j + 8 * core).start()
            return c

        lax.fori_loop(0, PAIRS, ends, 0)

    def combine(i, c):
        to_core(i).wait_recv()
        here, there = src[CHIPS * core + i], from_core[i]
        totals[i, 0:64, :] = here[0:64] * there[64:65] + there[0:64]
        totals[i, 64:72, :] = here[64:72] * there[64:72]

        @pl.when(i != chip)
        def _():
            to_owner(i).start()
        return c

    lax.fori_loop(0, CHIPS, combine, 0)

    low = iota((BASES, 128), 1) < 64

    def inside(d):
        seen = (rows_i >= cols_i) if d == 0 else (rows_i <= cols_i)
        inflow_b, readout_b = maps[d, :, 0:64], maps[d, :, 64:128]
        affinity = nt(readout_b, inflow_b)

        def step(j, c):
            run_e, _, _ = expand(d, j)
            drive, go = drive_b[d, j], go_b[d, j]
            zero = jnp.zeros_like(drive)
            output = grad_drive = total = None
            for half in range(2):
                mine = low if half == 0 else jnp.logical_not(low)
                row = run_t[d, pl.ds(2 * j + half, 1), :]
                col = run_e[:, 64 * half:64 * half + 1]
                decay = jnp.exp(jnp.where(seen, col - row, -1e30))
                mixing = (decay * affinity).astype(BF16)
                drive_h = jnp.where(mine, drive, zero)
                go_h = jnp.where(mine, go, zero)
                a, b, e = dot(mixing, drive_h), tn(mixing, go_h), decay * nt(go_h, drive)
                output = a if output is None else output + a
                grad_drive = b if grad_drive is None else grad_drive + b
                total = e if total is None else total + e
            out[d, j] = output
            gd[d, j] = grad_drive
            pairs[d] += total
            return c

        lax.fori_loop(0, PAIRS, step, 0)

    inside(0)

    def others(act):
        def step(i, c):
            act(lax.rem(chip + i, CHIPS))
            return c

        lax.fori_loop(1, CHIPS, step, 0)

    recv[chip] = totals[chip]
    others(lambda i: from_chip(i).wait_recv())

    def scan(i, carry):
        t = i + core * (CHIPS - 1 - 2 * i)
        scanned[t] = carry

        @pl.when(t != chip)
        def _():
            to_chip(t).start()
        return carry * recv[t, 64:65, :] + recv[t, 0:64, :]

    lax.fori_loop(0, CHIPS, scan, jnp.zeros((STATE, 128), F32))
    res[chip] = scanned[chip]

    inside(1)
    for c in range(4):
        ft[256 * c:256 * c + 256, :] = jnp.transpose(f[:, 256 * c:256 * c + 256])
        upt[256 * c:256 * c + 256, :] = jnp.transpose(up[0, :, 256 * c:256 * c + 256])
    others(lambda i: from_owner(i).wait_recv())

    def hand_on(i, c):
        first = res[i]
        here = src[CHIPS * core + i]
        ent_out[i] = first * here[64:65] + here[0:64]
        entering(i).start()
        ent[CHIPS * core + i] = first
        return c

    lax.fori_loop(0, CHIPS, hand_on, 0)

    def wait_entered(i, c):
        entered(i).wait_recv()
        return c

    lax.fori_loop(0, CHIPS, wait_entered, 0)

    started = []

    def put(source, target, device):
        i = len(started)
        copy = pltpu.make_async_remote_copy(
            src_ref=source, dst_ref=target, send_sem=send.at[i], recv_sem=receive.at[i], device_id=device,
            device_id_type=MESH)
        copy.start()
        started.append(copy)
        return copy

    jobs = []
    for n, (q, k) in enumerate(ORDER):
        jobs.append(dict(stream=n % 2, prod=prod.at[n % 6], acc=core_in.at[n], ring=ring.at[n], mid=mid.at[n],
                         ring2=ring2.at[n], fin=fin.at[n], dp=dp_in.at[n]))

    def core_start(job):
        job["core"] = put(job["prod"].at[:, :, :, 1 - core], job["acc"], other)

    def core_end(job):
        job["core"].wait_recv()
        job["acc"][...] = job["acc"][...] + job["prod"][:, :, :, core]

    def chunk(ref, h, c, stream, stage):
        if stream == 0 and stage == 1:
            return ref.at[h, :, c]
        return ref.at[h, c]

    def place(job, stage):
        over_y = (job["stream"] == 0) == (stage == 1)
        return (y, y_dev) if over_y else (z, z_dev)

    def refs(job, stage):
        return (job["acc"], job["ring"], job["mid"]) if stage == 1 else (job["mid"], job["ring2"], job["fin"])

    def ring_start(job, stage):
        p, dev = place(job, stage)
        s = job["stream"]
        ref, buffer, _ = refs(job, stage)
        job["m1"] = put(chunk(ref, 0, (p + 2) % 4, s, stage), buffer.at[0], dev[1])
        job["m1p"] = put(chunk(ref, 1, (p + 2) % 4, s, stage), buffer.at[1], dev[3])
        job["m2"] = put(chunk(ref, 1, (p + 1) % 4, s, stage), buffer.at[2], dev[1])
        job["m2p"] = put(chunk(ref, 0, (p + 3) % 4, s, stage), buffer.at[3], dev[3])

    def ring_middle(job, stage):
        p, dev = place(job, stage)
        s = job["stream"]
        ref, buffer, _ = refs(job, stage)
        job["m1"].wait_recv()
        ahead = chunk(ref, 0, (p + 1) % 4, s, stage)
        ahead[...] = ahead[...] + buffer[0]
        job["m3"] = put(ahead, buffer.at[4], dev[1])
        job["m1p"].wait_recv()
        behind = chunk(ref, 1, (p + 3) % 4, s, stage)
        behind[...] = behind[...] + buffer[1]
        job["m3p"] = put(behind, buffer.at[5], dev[3])

    def ring_end(job, stage):
        p, dev = place(job, stage)
        s = job["stream"]
        ref, buffer, into = refs(job, stage)
        for name in ("m2", "m2p", "m3", "m3p"):
            job[name].wait_recv()
        into[0] = chunk(ref, 0, p, s, stage)[...] + buffer[3] + buffer[4]
        into[1] = chunk(ref, 1, p, s, stage)[...] + buffer[2] + buffer[5]

    mine = pl.ds(pl.multiple_of(16 * dp, 16), 16)
    yours = pl.ds(pl.multiple_of(16 * (1 - dp), 16), 16)

    def go_on(n):
        job = jobs[n]
        at = job.get("at", 0)
        job["at"] = at + 1
        if at == 0:
            core_end(job)
            ring_start(job, 1)
        elif at == 1:
            ring_middle(job, 1)
        elif at == 2:
            ring_end(job, 1)
            ring_start(job, 2)
        elif at == 3:
            ring_middle(job, 2)
        elif at == 4:
            ring_end(job, 2)
            job["over_dp"] = put(job["fin"].at[:, yours, :], job["dp"], dp_dev)
        else:
            q, k = ORDER[n]
            job["over_dp"].wait_recv()
            for h in range(2):
                first = 256 * q + 128 * h
                grads_out[k, :, first:first + 128] = job["fin"][h, mine, :] + job["dp"][h]

    def outside(d, q):
        rows = slice(BASES * d, BASES * (d + 1))
        inflow_b, readout_b = maps[d, :, 0:64], maps[d, :, 64:128]

        def step(j, c):
            run_e, step_e, final = expand(d, j)
            initial, after = ent[16 * d + j], ent[24 - 16 * d + j]
            initial_b, after_b = initial.astype(BF16), after.astype(BF16)
            head, tail = jnp.exp(run_e), jnp.exp(final - run_e)
            drive_r, go_r = drive_b[d, j].astype(F32), go_b[d, j].astype(F32)
            carried = dot(readout_b, initial_b) * head
            output = out[d, j] + carried
            grad_drive = gd[d, j] + dot(inflow_b, after_b) * tail
            values, gates, grad_gated = v[d, j], g[d, j], gg[j]
            sigma = jax.nn.sigmoid(gates)
            swish = gates * sigma
            a, b = split2(grad_drive * drive_r - go_r * output)
            p, r = split2(grad_drive * values)
            acc[d] += dot(a, gathers(j, 0)) + dot(b, gathers(j, 0)) + dot(p, gathers(j, 16)) + dot(r, gathers(j, 16))
            boundary = jnp.sum(go_r * carried, axis=0, keepdims=True) + jnp.exp(final) * jnp.sum(
                initial * after, axis=0, keepdims=True)
            a, b = split2(jnp.broadcast_to(boundary, (16, 128)))
            kk[d] += (dot(a, gathers(j, 32)) + dot(b, gathers(j, 32)))[0:8]
            gins[d] += nt((drive_r * tail).astype(BF16), after_b)
            greads[d] += nt((go_r * head).astype(BF16), initial_b)
            lanes = pl.ds(pl.multiple_of(128 * j, 128), 128)
            gv[rows, lanes] = (step_e * grad_drive).astype(BF16)
            gate[rows, lanes] = (grad_gated * output * sigma * (1.0 + gates * (1.0 - sigma))).astype(BF16)
            gated[rows, lanes] = (output * swish).astype(BF16)
            return c

        lax.fori_loop(2 * q, 2 * q + 2, step, 0)

    def product(n):
        q, k = ORDER[n]
        result = (gv, gate, gated)[k]
        lanes = slice(256 * q, 256 * q + 256)
        if n >= 6:
            jobs[n - 6]["core"].wait_send()

        def step(i, c):
            rows = pl.ds(pl.multiple_of(256 * i, 256), 256)
            if k == 2:
                block = dot(upt[rows, :], result[0:BASES, lanes]) + dot(upt[rows, :], result[BASES:, lanes])
            else:
                block = dot(ft[rows, :], result[:, lanes])
            for h in range(2):
                prod[n % 6, h, i] = block[:, 128 * h:128 * h + 128].reshape(4, 2, 32, 128)
            return c

        lax.fori_loop(0, 4, step, 0)
        core_start(jobs[n])

    for q in range(4):
        outside(0, q)
        if q:
            go_on(3 * q - 1)
        outside(1, q)
        for n in range(3 * q, 3 * q + 3):
            product(n)
            if n > 3 * q:
                go_on(n - 1)
            if n >= 5:
                go_on(n - 5)

    for d in range(2):
        rows = slice(BASES * d, BASES * (d + 1))
        inflow_b, readout_b = maps[d, :, 0:64], maps[d, :, 64:128]
        pairs_b = pairs[d].astype(BF16)
        gin = gins[d] + tn(pairs_b, readout_b)
        gread = greads[d] + dot(pairs_b, inflow_b)
        gm[rows, :] = jnp.concatenate([gin, gread], axis=1).astype(BF16)
        per_head = jnp.transpose(acc[d] + kk[d, 0:1, :])
        earlier = (rows_i < cols_i) if d == 0 else (rows_i > cols_i)
        grad_log = summed3(per_head[0:16], earlier.astype(F32).astype(BF16)) + per_head[32:48]
        grad_step = per_head[16:32] - grad_log * rate_c
        glt[:, rows] = grad_step * jax.nn.sigmoid(logit_t[d])
        rates[:, d:d + 1] = -jnp.sum(grad_log * step_t[d], axis=1, keepdims=True)
    go_on(11)

    glb = glt[...].astype(BF16)
    mean = [jnp.zeros((BASES, 1), F32)] * 2
    for c in range(4):
        lanes = slice(256 * c, 256 * c + 256)
        by_gain = jnp.zeros((1, 256), F32)
        for d in range(2):
            rows = slice(BASES * d, BASES * (d + 1))
            gf = (nt(gv[rows, :], wv[0, lanes, :]) + nt(gate[rows, :], wv[1, lanes, :]) + nt(gm[rows, :], mw[lanes, :])
                  + tn(glb[:, rows], swt[:, lanes]))
            nrm = normed_s[rows, lanes]
            scaled = gf * gain[:, lanes]
            for i in range(2):
                v[d, 2 * c + i] = scaled[:, 128 * i:128 * i + 128]
            mean[d] = mean[d] + jnp.sum(scaled * nrm, axis=1, keepdims=True)
            by_gain = by_gain + jnp.sum(gf * nrm, axis=0, keepdims=True)
        rt[32:40, lanes] = jnp.broadcast_to(by_gain, (8, 256))
    go_on(7)
    for c in range(8):
        lanes = slice(128 * c, 128 * c + 128)
        residual = 0.5 * up[0, :, lanes].astype(F32)
        by_base = jnp.zeros((8, 128), F32)
        whole = None
        for d in range(2):
            rows = slice(BASES * d, BASES * (d + 1))
            ge = inv_s[rows, :] * (v[d, c] - normed_s[rows, lanes] * (mean[d] * (1.0 / WIDTH))) + residual
            whole = ge if whole is None else whole + ge
            for part in split3(ge):
                by_base = by_base + dot(hots[d], part.astype(BF16))
        gg[c] = whole
        rt[40:48, lanes] = by_base
    to_tp = put(gg.at[pl.ds(4 * (1 - tp), 4)], tp_in, tp_dev)

    rt[0:32, :] = jnp.zeros((32, WIDTH), F32)
    rt[48:128, :] = jnp.zeros((80, WIDTH), F32)
    heads_at = pl.multiple_of(16 * tp, 16)
    scalars_at = pl.multiple_of(48 + 16 * tp, 16)
    rt[pl.ds(heads_at, 16), :] = dot(glb, f[...])
    rt[pl.ds(scalars_at, 16), 0:128] = jnp.broadcast_to(jnp.sum(glt[...], axis=1, keepdims=True), (HEADS, 128))
    rt[pl.ds(scalars_at, 16), 128:256] = jnp.broadcast_to(rates[:, 0:1] + rates[:, 1:2], (HEADS, 128))
    for i in range(4):
        prod_e[i, :, :, :, 0:128] = dot(ft[256 * i:256 * i + 256, :], gm[...]).reshape(4, 2, 32, 128)
    for i in range(8):
        prod_e[i // 2, 2 * (i % 2):2 * (i % 2) + 2, :, :, 128:256] = rt[:, 128 * i:128 * i + 128].reshape(2, 2, 32, 128)
    small_core = put(prod_e.at[:, :, 1 - core], core_e, other)
    for n in (0, 1):
        go_on(n)
    small_core.wait_recv()
    core_e[...] = core_e[...] + prod_e[:, :, core]
    offsets = [(dz, dy) for dz in range(4) for dy in range(4)][1:]
    small_in = [put(core_e.at[(z + dz) % 4, (y + dy) % 4], parts.at[4 * dz + dy], on(((z + dz) % 4) * 4 + (y + dy) % 4))
                for dz, dy in offsets]
    for n in (8, 2, 3, 4, 0, 1):
        go_on(n)
    total = core_e[z, y]
    for i, copy in enumerate(small_in):
        copy.wait_recv()
        total = total + parts[i + 1]
    mine_e[0] = total
    over_x = [put(mine_e.at[0], x_in.at[i], device) for i, device in enumerate((tp_dev, dp_dev, far_dev))]
    for n in (9, 5, 6, 2, 3):
        go_on(n)
    for copy in over_x:
        copy.wait_recv()
    mine_e[1] = (mine_e[0] + x_in[0]) + (x_in[1] + x_in[2])
    all_e[z, y, core] = mine_e[1]
    small_back = [put(mine_e.at[1], all_e.at[z, y, core], on(((z + dz) % 4) * 4 + (y + dy) % 4)) for dz, dy in offsets]
    for n in (10, 11, 7, 8, 4, 0, 1, 5, 2, 6, 3):
        go_on(n)
    for copy in small_back:
        copy.wait_recv()
    back_core = put(all_e.at[:, :, core], all_e.at[:, :, core], other)
    for n in (9, 10, 11, 7, 8, 4, 5):
        go_on(n)
    to_tp.wait_recv()
    for i in range(4):
        stream_out[:, 128 * i:128 * i + 128] = gg[4 * tp + i] + tp_in[i]
    back_core.wait_recv()
    mixer_out[...] = all_e[:, :, :, :, 0:128].reshape(WIDTH, 128)
    for i in range(8):
        rt[:, 128 * i:128 * i + 128] = all_e[i // 2, 2 * (i % 2):2 * (i % 2) + 2, :, :, 128:256].reshape(128, 128)
    step_out[...] = rt[pl.ds(heads_at, 16), :]
    gain_out[...] = rt[32:33, :]
    table_out[...] = rt[40:45, :]
    scalars_out[...] = rt[pl.ds(scalars_at, 16), 0:256]
    while any(job["at"] < 6 for job in jobs):
        low_at = min(job["at"] for job in jobs)
        for n, job in enumerate(jobs):
            if job["at"] == low_at:
                go_on(n)
    for n, copy in enumerate(started):
        if not any(copy is job["core"] for job in jobs[:6]):
            copy.wait_send()

    def wait_sent(i, c):
        to_core(i).wait_send()
        entering(i).wait_send()
        return c

    lax.fori_loop(0, CHIPS, wait_sent, 0)
    others(lambda i: to_owner(i).wait_send())
    others(lambda i: to_chip(i).wait_send())


def main(base, stream, cotangent, table, gain, w, mw, swt, bias, rate):
    vmem, anywhere = pl.BlockSpec(memory_space=pltpu.VMEM), pl.BlockSpec(memory_space=pl.ANY)
    rows = 2 * BASES

    def shape(*dims):
        return jax.ShapeDtypeStruct(dims, F32)

    def f32(*dims):
        return pltpu.VMEM(dims, F32)

    def bf16(*dims):
        return pltpu.VMEM(dims, BF16)

    def sems(n):
        return pltpu.SemaphoreType.DMA((n,))

    jobs = len(ORDER)
    return pl.pallas_call(
        main_kernel,
        out_shape=[
            shape(3, 16, WIDTH), shape(WIDTH, 128), shape(HEADS, WIDTH), shape(5, WIDTH), shape(1, WIDTH),
            shape(HEADS, 256), shape(BASES, WIDTH // 2),
        ],
        in_specs=[vmem] * 5 + [anywhere] + [vmem] * 4,
        out_specs=[vmem] * 7,
        scratch_shapes=[
            bf16(3, WIDTH, WIDTH), f32(8, WIDTH), bf16(rows, WIDTH), f32(rows, WIDTH), f32(rows, 1),
            f32(2, PAIRS, BASES, 128), f32(2, PAIRS, BASES, 128), f32(PAIRS, BASES, 128),
            bf16(2, BASES, 128), f32(2, HEADS, BASES), bf16(2, BASES, 128), bf16(2, 128, BASES), f32(2, HEADS, BASES),
            f32(2, HEADS, BASES), bf16(2, PAIRS, BASES, 128), bf16(2, PAIRS, BASES, 128),
            f32(2, PAIRS, BASES, 128), f32(2, PAIRS, BASES, 128), f32(2, BASES, BASES),
            f32(2, BASES, 128), f32(2, 8, 128), f32(2, BASES, STATE), f32(2, BASES, STATE),
            f32(2 * CHIPS, 72, 128), f32(CHIPS, 72, 128), f32(CHIPS, 72, 128), f32(CHIPS, 72, 128),
            f32(CHIPS, STATE, 128), f32(CHIPS, STATE, 128), f32(2 * CHIPS, STATE, 128), f32(CHIPS, STATE, 128),
            bf16(rows, WIDTH), bf16(rows, WIDTH), bf16(rows, WIDTH), bf16(rows, 128), f32(HEADS, rows), f32(HEADS, 2),
            bf16(WIDTH, rows), bf16(WIDTH, BASES), f32(128, WIDTH),
            f32(6, 2, 4, 4, 2, 32, 128), f32(jobs, 2, 4, 4, 32, 128), f32(jobs, 6, 4, 32, 128), f32(jobs, 2, 4, 32, 128),
            f32(jobs, 6, 32, 128), f32(jobs, 2, 32, 128), f32(jobs, 2, 16, 128),
            f32(4, 4, 2, 32, 256), f32(4, 4, 32, 256), f32(16, 32, 256), f32(2, 32, 256), f32(3, 32, 256),
            f32(4, 4, 2, 32, 256), f32(4, BASES, 128),
            sems(3), sems(CHIPS), sems(CHIPS), sems(CHIPS), sems(CHIPS), sems(CHIPS), sems(CHIPS), sems(CHIPS), sems(CHIPS),
            sems(SEMS), sems(SEMS),
        ],
        compiler_params=pltpu.CompilerParams(collective_id=0, has_side_effects=True, vmem_limit_bytes=61 << 20),
        name="main",
    )(base, stream, cotangent, table, gain, w, mw, swt, bias, rate)


def emit_kernel(grads, mixer, steps, by_base, by_gain, scalars, stream,
                grads_out, mixer_out, steps_out, base_out, gain_out, bias_out, rate_out, stream_out):
    for source, target in ((grads, grads_out), (mixer, mixer_out), (steps, steps_out), (by_base, base_out),
                           (by_gain, gain_out), (stream, stream_out)):
        target[...] = source[...]
    same = iota((HEADS, HEADS), 0) == iota((HEADS, HEADS), 1)
    for first, target in ((0, bias_out), (128, rate_out)):
        target[...] = jnp.sum(jnp.where(same, scalars[:, first:first + HEADS], 0.0), axis=0, keepdims=True)


def emit(*results):
    vmem = pl.BlockSpec(memory_space=pltpu.VMEM)
    like = [jax.ShapeDtypeStruct(r.shape, F32) for r in results]
    row = jax.ShapeDtypeStruct((1, HEADS), F32)
    return pl.pallas_call(
        emit_kernel,
        out_shape=like[:5] + [row, row] + like[6:],
        in_specs=[vmem] * 7,
        out_specs=[vmem] * 8,
        name="emit",
    )(*results)


def body(base_ids, stream, cotangent, table, gain, projections, mixer_weight, step_weight, step_bias, rate):
    results = main(
        base_ids, stream, cotangent, table, gain[None], jnp.transpose(projections, (1, 0, 2)), mixer_weight,
        jnp.transpose(step_weight), step_bias[None], rate[None])
    grads, mixer, steps, by_base, by_gain, by_bias, by_rate, stream_grad = emit(*results)
    return (
        jnp.transpose(grads, (1, 0, 2)),
        mixer,
        jnp.transpose(steps),
        by_bias[0],
        by_rate[0],
        by_base,
        by_gain[0],
        stream_grad[None],
    )


def solution(mesh):
    return jax.shard_map(
        body,
        mesh=mesh,
        in_specs=(
            P("dp", "ctx"),
            P("dp", "ctx", None),
            P("dp", "ctx", None),
            P(),
            P(),
            P(None, None, "tp"),
            P(),
            P(None, "tp"),
            P("tp"),
            P("tp"),
        ),
        out_specs=(
            P(("ctx", "dp"), None, "tp"),
            P(),
            P(None, "tp"),
            P("tp"),
            P("tp"),
            P(),
            P(),
            P("dp", "ctx", "tp"),
        ),
        check_vma=False,
    )
```

```python
import functools

import jax
import jax.numpy as jnp
import numpy as np
from jax import lax
from jax.experimental import pallas as pl
from jax.experimental.pallas import tpu as pltpu
from jax.sharding import PartitionSpec as P

EPS = 1e-05
HIGH = lax.Precision.HIGHEST
F32 = jnp.float32
BF16 = jnp.bfloat16
MESH = pl.DeviceIdType.MESH
BASES = 256
WIDTH = 1024
HEADS = 16
PAIRS = 8
STATE = 64


def nt(left, right):
    return lax.dot_general(left, right, (((1,), (1,)), ((), ())), preferred_element_type=F32)


def tn(left, right):
    return lax.dot_general(left, right, (((0,), (0,)), ((), ())), preferred_element_type=F32)


def dot(left, right):
    return jnp.dot(left, right, preferred_element_type=F32)


def exact(left, right):
    return jnp.dot(left, right, preferred_element_type=F32, precision=HIGH)


def split3(x):
    a = x.astype(BF16).astype(F32)
    b = (x - a).astype(BF16).astype(F32)
    return a, b, x - a - b


def split2(x):
    a = x.astype(BF16)
    return a, (x - a.astype(F32)).astype(BF16)


def summed3(x, ones):
    r = dot(jnp.concatenate(split3(x), axis=0).astype(BF16), ones)
    n = x.shape[0]
    return r[0:n] + r[n:2 * n] + r[2 * n:3 * n]


def iota(shape, dim):
    return lax.broadcasted_iota(jnp.int32, shape, dim)


def spreads():
    j, r, c = np.indices((PAIRS, 128, 256))
    return np.logical_and(r // 48 == c // 128, r % 16 == 2 * j + c % 128 // 64).astype(np.float32)


CHIPS = 16
ORDER = [(q, k) for q in range(4) for k in (2, 1, 0)]


def main_kernel(base, x, up, table, gain, w, mw, swt, bias, rate, spread,
                grads_out, mixer_out, step_out, table_out, gain_out, scalars_out, stream_out,
                wv, tab, f, normed_s, inv_s, v, g, gg, quant, run_t, maps, maps_t, logit_t, step_t, drive_b, go_b, out, gd, pairs,
                acc, acc_v, kk, gins, greads, swish_s, src, from_core, totals, recv, scanned, res, ent,
                gv, gate, gm, glt, rates, ft, upt, rt, prod, core_in, ring, mid, ring2, fin, dp_in,
                prod_e, core_e, parts, mine_e, x_in, all_e, tp_in,
                wsem, core_sem, state_sem, job_recv, job_core, job_send, small_sem):
    ctx, tp, dp = lax.axis_index("ctx"), lax.axis_index("tp"), lax.axis_index("dp")
    core, chip = ctx % 2, ctx // 2
    y, z = chip % 4, chip // 4

    def on(c):
        return {"ctx": c * 2 + core}

    other = {"ctx": chip * 2 + 1 - core}
    tp_dev, dp_dev, far_dev = {"tp": 1 - tp}, {"dp": 1 - dp}, {"tp": 1 - tp, "dp": 1 - dp}
    y_dev = [on(z * 4 + (y + i) % 4) for i in range(4)]
    z_dev = [on(((z + i) % 4) * 4 + y) for i in range(4)]

    barrier = pltpu.get_barrier_semaphore()

    def greet(i, c):
        pl.semaphore_signal(barrier, inc=1, device_id=on(lax.rem(chip + i, CHIPS)), device_id_type=MESH)
        return c

    lax.fori_loop(1, CHIPS, greet, 0)
    for device in (other, tp_dev, dp_dev, far_dev):
        pl.semaphore_signal(barrier, inc=1, device_id=device, device_id_type=MESH)
    copies = [pltpu.make_async_copy(w.at[k], wv.at[k], wsem.at[k]) for k in range(3)]
    for copy in copies:
        copy.start()

    tab[...] = jnp.zeros_like(tab)
    tab[0:5, :] = table[...]
    pieces = jnp.concatenate(split3(tab[...]), axis=0).astype(BF16)
    incoming = x[0].astype(F32)
    hots = []
    for d in range(2):
        ids = base[...]
        if d:
            ids = jnp.where(ids == 4, 4, 3 - ids)
        hot = (iota((8, BASES), 0) == ids).astype(F32)
        hots.append(hot.astype(BF16))
        embedded = incoming + tn(jnp.concatenate([hot, hot, hot], axis=0).astype(BF16), pieces)
        inv = lax.rsqrt(jnp.mean(embedded * embedded, axis=1, keepdims=True) + EPS)
        normed = embedded * inv
        rows = slice(BASES * d, BASES * (d + 1))
        normed_s[rows, :] = normed
        inv_s[rows, :] = inv
        f[rows, :] = (normed * gain[...]).astype(BF16)

    def column(row):
        square = jnp.broadcast_to(row, (HEADS, HEADS))
        return jnp.sum(jnp.where(iota((HEADS, HEADS), 0) == iota((HEADS, HEADS), 1), square, 0.0), axis=1, keepdims=True)

    rate_c = column(rate[...])
    mapped = dot(f[...], mw[...])
    for d in range(2):
        maps[d] = mapped[BASES * d:BASES * (d + 1)].astype(BF16)
        maps_t[d] = jnp.transpose(mapped[BASES * d:BASES * (d + 1)]).astype(BF16)
    logits = nt(swt[...], f[...]) + column(bias[...])
    rows_i, cols_i = iota((BASES, BASES), 0), iota((BASES, BASES), 1)
    for d in range(2):
        logit = logits[:, BASES * d:BASES * (d + 1)]
        step = jnp.maximum(logit, 0.0) + jnp.log1p(jnp.exp(-jnp.abs(logit)))
        logit_t[d] = logit
        step_t[d] = step
        upto = (rows_i <= cols_i) if d == 0 else (rows_i >= cols_i)
        run = summed3(-step * rate_c, upto.astype(F32).astype(BF16))
        run_t[d] = run
        whole = jnp.concatenate(split3(run) + split3(step) + (jnp.zeros((32, BASES), F32),), axis=0)
        quant[d] = jnp.transpose(whole).astype(BF16)
        pairs[d] = jnp.zeros((BASES, BASES), F32)
        acc[d] = jnp.zeros((BASES, 128), F32)
        acc_v[d] = jnp.zeros((BASES, 128), F32)
        kk[d] = jnp.zeros((8, 128), F32)
        gins[d] = jnp.zeros((BASES, STATE), F32)
        greads[d] = jnp.zeros((BASES, STATE), F32)
    for k, target in ((0, v), (1, g)):
        copies[k].wait()
        for c in range(4):
            block = dot(f[...], wv[k, :, 256 * c:256 * c + 256])
            for d in range(2):
                for i in range(2):
                    target[d, 2 * c + i] = block[BASES * d:BASES * (d + 1), 128 * i:128 * i + 128]
    copies[2].wait()
    for c in range(4):
        block = dot(up[0], wv[2, :, 256 * c:256 * c + 256])
        for i in range(2):
            gg[2 * c + i] = block[:, 128 * i:128 * i + 128]

    def expand(d, j):
        both = dot(quant[d], spread[j])
        run_e, step_e = both[:, 0:128], both[:, 128:256]
        final = run_e[BASES - 1:BASES] if d == 0 else run_e[0:1]
        return run_e, step_e, final

    def remote(source, target, sent, arrived, device):
        return pltpu.make_async_remote_copy(
            src_ref=source, dst_ref=target, send_sem=sent, recv_sem=arrived, device_id=device, device_id_type=MESH)

    def to_core(i, half, n=1):
        source = src.at[CHIPS * (1 - core) + i] if n == 1 else src.at[pl.ds(0, n)]
        target = from_core.at[i] if n == 1 else from_core.at[pl.ds(i, n)]
        return remote(source, target, core_sem.at[2], core_sem.at[half], other)

    def to_owner(i):
        return remote(totals.at[i], recv.at[chip], state_sem.at[0], state_sem.at[1], on(i))

    all_to_owners = remote(totals.at[pl.ds(0, 15)], recv.at[pl.ds(0, 15)], state_sem.at[0], state_sem.at[1], other)

    def to_chip(i):
        return remote(scanned.at[i], res.at[chip], state_sem.at[2], state_sem.at[3], on(i))

    all_to_chips = remote(scanned.at[pl.ds(0, 15)], res.at[pl.ds(0, 15)], state_sem.at[2], state_sem.at[3], other)

    def entering(i):
        return remote(from_core.at[i, pl.ds(0, 64)], ent.at[CHIPS * core + i], state_sem.at[4], state_sem.at[5], other)

    all_entering = remote(ent.at[pl.ds(CHIPS * core, CHIPS)], ent.at[pl.ds(CHIPS * (1 - core), CHIPS)], state_sem.at[4], state_sem.at[5], other)

    pl.semaphore_wait(barrier, CHIPS + 3)
    for d in range(2):
        def ends(j, c, d=d):
            run_e, step_e, final = expand(d, j)
            drive = step_e * v[d, j]
            gates = g[d, j]
            sigma = jax.nn.sigmoid(gates)
            swish = gates * sigma
            go = gg[j] * swish
            drive_b[d, j] = drive.astype(BF16)
            go_b[d, j] = go.astype(BF16)
            swish_s[d, j] = swish
            late_drive = (drive * jnp.exp(final - run_e)).astype(BF16)
            late_go = (go * jnp.exp(run_e)).astype(BF16)
            lanes = pl.ds(pl.multiple_of(128 * j, 128), 128)
            wv[2, BASES * d:BASES * (d + 1), lanes] = late_drive
            wv[2, BASES * (d + 2):BASES * (d + 3), lanes] = late_go
            state = dot(maps_t[d, 0:64, :], late_drive)
            grad = dot(maps_t[d, 64:128, :], late_go)
            decay = jnp.broadcast_to(jnp.exp(final), (8, 128))
            for t, value in ((16 * d + j, state), (24 - 16 * d + j, grad)):
                src[t, 0:64, :] = value
                src[t, 64:72, :] = decay
            half = (1 - core) if d == 0 else core
            to_core(j + 8 * half, half).start()
            return c

        lax.fori_loop(0, PAIRS, ends, 0)

    def combine(i, c):
        here, there = src[CHIPS * core + i], from_core[i]
        totals[i, 0:64, :] = here[0:64] * there[64:65] + there[0:64]
        totals[i, 64:72, :] = here[64:72] * there[64:72]

        @pl.when(i != chip)
        def _():
            to_owner(i).start()
        return c

    for part in range(2):
        half = (core + part) % 2
        to_core(8 * half, half, 8).wait_recv()
        lax.fori_loop(8 * half, 8 * half + 8, combine, 0)

    low = iota((BASES, 128), 1) < 64

    def inside(d):
        seen = (rows_i >= cols_i) if d == 0 else (rows_i <= cols_i)
        inflow_b, readout_b = maps[d, :, 0:64], maps[d, :, 64:128]
        affinity = nt(readout_b, inflow_b)

        def step(j, c):
            run_e, _, _ = expand(d, j)
            drive, go = drive_b[d, j], go_b[d, j]
            zero = jnp.zeros_like(drive)
            output = grad_drive = total = None
            for half in range(2):
                mine = low if half == 0 else jnp.logical_not(low)
                row = run_t[d, pl.ds(2 * j + half, 1), :]
                col = run_e[:, 64 * half:64 * half + 1]
                decay = jnp.exp(jnp.where(seen, col - row, -1e30))
                mixing = (decay * affinity).astype(BF16)
                drive_h = jnp.where(mine, drive, zero)
                go_h = jnp.where(mine, go, zero)
                a, b, e = dot(mixing, drive_h), tn(mixing, go_h), decay * nt(go_h, drive)
                output = a if output is None else output + a
                grad_drive = b if grad_drive is None else grad_drive + b
                total = e if total is None else total + e
            out[d, j] = output
            gd[d, j] = grad_drive
            pairs[d] += total
            return c

        lax.fori_loop(0, PAIRS, step, 0)

    inside(0)

    recv[chip] = totals[chip]
    all_to_owners.wait_recv()

    def scan(i, carry):
        t = i + core * (CHIPS - 1 - 2 * i)
        scanned[t] = carry

        @pl.when(t != chip)
        def _():
            to_chip(t).start()
        return carry * recv[t, 64:65, :] + recv[t, 0:64, :]

    lax.fori_loop(0, CHIPS, scan, jnp.zeros((STATE, 128), F32))
    res[chip] = scanned[chip]

    inside(1)
    for c in range(4):
        ft[256 * c:256 * c + 256, :] = jnp.transpose(f[:, 256 * c:256 * c + 256])
        upt[256 * c:256 * c + 256, :] = jnp.transpose(up[0, :, 256 * c:256 * c + 256])
    gated = f
    for d in range(2):
        def prepare(j, c, d=d):
            gates, swish = g[d, j], swish_s[d, j]
            sigma = jax.nn.sigmoid(gates)
            g[d, j] = gg[j] * (sigma + swish * (1.0 - sigma))
            return c

        lax.fori_loop(0, PAIRS, prepare, 0)
    all_to_chips.wait_recv()

    def hand_on(i, c):
        first = res[i]
        here = src[CHIPS * core + i]
        from_core[i, 0:64, :] = first * here[64:65] + here[0:64]
        entering(i).start()
        ent[CHIPS * core + i] = first
        return c

    lax.fori_loop(0, CHIPS, hand_on, 0)

    all_entering.wait_recv()

    def put(source, target, sent, arrived, device):
        copy = remote(source, target, sent, arrived, device)
        copy.start()
        return copy

    jobs = []
    for n, (q, k) in enumerate(ORDER):
        jobs.append(dict(n=n, stream=n % 2, prod=prod.at[n % 6], acc=core_in.at[n], ring=ring.at[n], mid=mid.at[n],
                         ring2=ring2.at[n], fin=fin.at[n], dp=dp_in.at[n]))

    def core_start(job):
        n = job["n"]
        job["core"] = put(job["prod"].at[:, :, :, 1 - core], job["acc"], job_core.at[n], job_recv.at[6 * n], other)

    def core_end(job):
        job["core"].wait_recv()
        job["acc"][...] = job["acc"][...] + job["prod"][:, :, :, core]

    def chunk(ref, h, c, stream, stage):
        if stream == 0 and stage == 1:
            return ref.at[h, :, c]
        return ref.at[h, c]

    def place(job, stage):
        over_y = (job["stream"] == 0) == (stage == 1)
        return (y, y_dev) if over_y else (z, z_dev)

    def refs(job, stage):
        return (job["acc"], job["ring"], job["mid"]) if stage == 1 else (job["mid"], job["ring2"], job["fin"])

    def ring_start(job, stage):
        p, dev = place(job, stage)
        s = job["stream"]
        ref, buffer, _ = refs(job, stage)
        sent, first, second = job_send.at[stage - 1], job_recv.at[6 * job["n"] + 2 * stage - 1], job_recv.at[6 * job["n"] + 2 * stage]
        put(chunk(ref, 0, (p + 2) % 4, s, stage), buffer.at[0], sent, first, dev[1])
        put(chunk(ref, 1, (p + 2) % 4, s, stage), buffer.at[1], sent, first, dev[3])
        put(chunk(ref, 1, (p + 1) % 4, s, stage), buffer.at[2], sent, second, dev[1])
        put(chunk(ref, 0, (p + 3) % 4, s, stage), buffer.at[3], sent, second, dev[3])

    def ring_middle(job, stage):
        p, dev = place(job, stage)
        s = job["stream"]
        ref, buffer, _ = refs(job, stage)
        sent, first, second = job_send.at[stage - 1], job_recv.at[6 * job["n"] + 2 * stage - 1], job_recv.at[6 * job["n"] + 2 * stage]
        remote(buffer.at[pl.ds(0, 2)], buffer.at[pl.ds(0, 2)], sent, first, other).wait_recv()
        ahead = chunk(ref, 0, (p + 1) % 4, s, stage)
        ahead[...] = ahead[...] + buffer[0]
        put(ahead, buffer.at[4], sent, second, dev[1])
        behind = chunk(ref, 1, (p + 3) % 4, s, stage)
        behind[...] = behind[...] + buffer[1]
        put(behind, buffer.at[5], sent, second, dev[3])

    def ring_end(job, stage):
        p, dev = place(job, stage)
        s = job["stream"]
        ref, buffer, into = refs(job, stage)
        sent, second = job_send.at[stage - 1], job_recv.at[6 * job["n"] + 2 * stage]
        remote(buffer.at[pl.ds(2, 4)], buffer.at[pl.ds(2, 4)], sent, second, other).wait_recv()
        into[0] = chunk(ref, 0, p, s, stage)[...] + buffer[3] + buffer[4]
        into[1] = chunk(ref, 1, p, s, stage)[...] + buffer[2] + buffer[5]

    mine = pl.ds(pl.multiple_of(16 * dp, 16), 16)
    yours = pl.ds(pl.multiple_of(16 * (1 - dp), 16), 16)

    def go_on(n):
        job = jobs[n]
        at = job.get("at", 0)
        job["at"] = at + 1
        if at == 0:
            core_end(job)
            ring_start(job, 1)
        elif at == 1:
            ring_middle(job, 1)
        elif at == 2:
            ring_end(job, 1)
            ring_start(job, 2)
        elif at == 3:
            ring_middle(job, 2)
        elif at == 4:
            ring_end(job, 2)
            job["over_dp"] = put(
                job["fin"].at[:, yours, :], job["dp"], job_send.at[2], job_recv.at[6 * n + 5], dp_dev)
        else:
            q, k = ORDER[n]
            job["over_dp"].wait_recv()
            for h in range(2):
                first = 256 * q + 128 * h
                grads_out[k, :, first:first + 128] = job["fin"][h, mine, :] + job["dp"][h]

    def outside(d, q):
        rows = slice(BASES * d, BASES * (d + 1))
        inflow_b, readout_b = maps[d, :, 0:64], maps[d, :, 64:128]

        def step(j, c):
            run_e, step_e, final = expand(d, j)
            initial, after = ent[16 * d + j], ent[24 - 16 * d + j]
            initial_b, after_b = initial.astype(BF16), after.astype(BF16)
            head, tail = jnp.exp(run_e), jnp.exp(final - run_e)
            drive_r, go_r = drive_b[d, j].astype(F32), go_b[d, j].astype(F32)
            carried = dot(readout_b, initial_b) * head
            output = out[d, j] + carried
            grad_drive = gd[d, j] + dot(inflow_b, after_b) * tail
            values, to_heads = v[d, j], spread[j, :, 0:128]
            a, b = split2(grad_drive * drive_r - go_r * output)
            acc[d] += nt(a, to_heads) + nt(b, to_heads)
            acc_v[d] += nt((grad_drive * values).astype(BF16), to_heads)
            boundary = jnp.sum(go_r * carried, axis=0, keepdims=True) + jnp.exp(final) * jnp.sum(
                initial * after, axis=0, keepdims=True)
            a, b = split2(jnp.broadcast_to(boundary, (16, 128)))
            kk[d] += (nt(a, to_heads) + nt(b, to_heads))[0:8]
            lanes = pl.ds(pl.multiple_of(128 * j, 128), 128)
            gins[d] += nt(wv[2, BASES * d:BASES * (d + 1), lanes], after_b)
            greads[d] += nt(wv[2, BASES * (d + 2):BASES * (d + 3), lanes], initial_b)
            gv[rows, lanes] = (step_e * grad_drive).astype(BF16)
            gate[rows, lanes] = (g[d, j] * output).astype(BF16)
            gated[rows, lanes] = (output * swish_s[d, j]).astype(BF16)
            return c

        lax.fori_loop(2 * q, 2 * q + 2, step, 0)

    def product(n):
        q, k = ORDER[n]
        result = (gv, gate, gated)[k]
        lanes = slice(256 * q, 256 * q + 256)
        if n >= 6:
            jobs[n - 6]["core"].wait_send()

        for i in range(2):
            rows = slice(512 * i, 512 * i + 512)
            if k == 2:
                block = dot(upt[rows, :], result[0:BASES, lanes]) + dot(upt[rows, :], result[BASES:, lanes])
            else:
                block = dot(ft[rows, :], result[:, lanes])
            for h in range(2):
                prod[n % 6, h, 2 * i:2 * i + 2] = block[:, 128 * h:128 * h + 128].reshape(2, 4, 2, 32, 128)
        core_start(jobs[n])

    outside(0, 0)
    outside(1, 0)
    for n in range(3):
        product(n)
    outside(0, 1)
    for n in range(3):
        go_on(n)
    outside(1, 1)
    for n in range(3, 6):
        product(n)
    outside(0, 2)
    for n in range(3, 6):
        go_on(n)
    outside(1, 2)
    outside(0, 3)
    go_on(0)
    go_on(1)
    outside(1, 3)

    for d in range(2):
        rows = slice(BASES * d, BASES * (d + 1))
        inflow_b, readout_b = maps[d, :, 0:64], maps[d, :, 64:128]
        pairs_b = pairs[d].astype(BF16)
        gin = gins[d] + tn(pairs_b, readout_b)
        gread = greads[d] + dot(pairs_b, inflow_b)
        gm[rows, :] = jnp.concatenate([gin, gread], axis=1).astype(BF16)
        per_head = jnp.transpose(acc[d])
        boundary = jnp.transpose(jnp.broadcast_to(kk[d, 0:1, :], (128, 128)))[0:16, 0:1]
        earlier = (rows_i < cols_i) if d == 0 else (rows_i > cols_i)
        grad_log = summed3(per_head[0:16], earlier.astype(F32).astype(BF16)) + boundary
        grad_step = jnp.transpose(acc_v[d])[0:16] - grad_log * rate_c
        glt[:, rows] = grad_step * jax.nn.sigmoid(logit_t[d])
        rates[:, d:d + 1] = -jnp.sum(grad_log * step_t[d], axis=1, keepdims=True)
    go_on(2)

    glb = glt[...].astype(BF16)
    mean = [jnp.zeros((BASES, 1), F32)] * 2
    for c in range(4):
        lanes = slice(256 * c, 256 * c + 256)
        by_gain = jnp.zeros((1, 256), F32)
        for d in range(2):
            rows = slice(BASES * d, BASES * (d + 1))
            gf = (nt(gv[rows, :], wv[0, lanes, :]) + nt(gate[rows, :], wv[1, lanes, :]) + nt(gm[rows, :], mw[lanes, :])
                  + tn(glb[:, rows], swt[:, lanes]))
            nrm = normed_s[rows, lanes]
            scaled = gf * gain[:, lanes]
            for i in range(2):
                v[d, 2 * c + i] = scaled[:, 128 * i:128 * i + 128]
            mean[d] = mean[d] + jnp.sum(scaled * nrm, axis=1, keepdims=True)
            by_gain = by_gain + jnp.sum(gf * nrm, axis=0, keepdims=True)
        rt[32:40, lanes] = jnp.broadcast_to(by_gain, (8, 256))
        if c in (1, 3):
            go_on(3 + c // 2)
    for c in range(8):
        lanes = slice(128 * c, 128 * c + 128)
        residual = 0.5 * up[0, :, lanes].astype(F32)
        by_base = jnp.zeros((8, 128), F32)
        whole = None
        for d in range(2):
            rows = slice(BASES * d, BASES * (d + 1))
            ge = inv_s[rows, :] * (v[d, c] - normed_s[rows, lanes] * (mean[d] * (1.0 / WIDTH))) + residual
            whole = ge if whole is None else whole + ge
            for part in split3(ge):
                by_base = by_base + dot(hots[d], part.astype(BF16))
        gg[c] = whole
        rt[40:48, lanes] = by_base
    to_tp = put(gg.at[pl.ds(4 * (1 - tp), 4)], tp_in, small_sem.at[0], small_sem.at[1], tp_dev)
    go_on(5)

    rt[0:32, :] = jnp.zeros((32, WIDTH), F32)
    rt[48:128, :] = jnp.zeros((80, WIDTH), F32)
    heads_at = pl.multiple_of(16 * tp, 16)
    scalars_at = pl.multiple_of(48 + 16 * tp, 16)
    rt[pl.ds(heads_at, 16), :] = nt(glb, ft[...])
    rt[pl.ds(scalars_at, 16), 0:128] = jnp.broadcast_to(jnp.sum(glt[...], axis=1, keepdims=True), (HEADS, 128))
    rt[pl.ds(scalars_at, 16), 128:256] = jnp.broadcast_to(rates[:, 0:1] + rates[:, 1:2], (HEADS, 128))
    for i in range(4):
        prod_e[i, :, :, :, 0:128] = dot(ft[256 * i:256 * i + 256, :], gm[...]).reshape(4, 2, 32, 128)
    for i in range(8):
        prod_e[i // 2, 2 * (i % 2):2 * (i % 2) + 2, :, :, 128:256] = rt[:, 128 * i:128 * i + 128].reshape(2, 2, 32, 128)
    small_core = put(prod_e.at[:, :, 1 - core], core_e, small_sem.at[2], small_sem.at[3], other)
    product(6)
    product(7)
    small_core.wait_recv()
    core_e[...] = core_e[...] + prod_e[:, :, core]
    offsets = [(dz, dy) for dz in range(4) for dy in range(4)][1:]

    def to_all(source, place_of, sent, arrived):
        for dz, dy in offsets:
            zz, yy = (z + dz) % 4, (y + dy) % 4
            mine_of, theirs = source(zz, yy), place_of(4 * dz + dy)
            put(mine_of, theirs, sent, arrived, on(zz * 4 + yy))
        return remote(parts.at[pl.ds(1, 15)], parts.at[pl.ds(1, 15)], sent, arrived, other)

    small_in = to_all(lambda zz, yy: core_e.at[zz, yy], lambda i: parts.at[i], small_sem.at[4], small_sem.at[5])
    go_on(6)
    product(8)
    go_on(7)
    product(9)
    go_on(8)
    product(10)
    for n in (9, 0, 1):
        go_on(n)
    product(11)
    for n in (10, 2, 3, 11):
        go_on(n)
    small_in.wait_recv()
    total = core_e[z, y]
    for i in range(15):
        total = total + parts[i + 1]
    mine_e[0] = total
    for i, device in enumerate((tp_dev, dp_dev, far_dev)):
        put(mine_e.at[0], x_in.at[i], small_sem.at[6], small_sem.at[7], device)
    over_x = remote(x_in, x_in, small_sem.at[6], small_sem.at[7], other)
    for n in (4, 5, 0, 1, 6, 7):
        go_on(n)
    over_x.wait_recv()
    mine_e[1] = (mine_e[0] + x_in[0]) + (x_in[1] + x_in[2])
    all_e[z, y, core] = mine_e[1]
    small_back = to_all(lambda zz, yy: mine_e.at[1], lambda i: all_e.at[z, y, core], small_sem.at[8], small_sem.at[9])
    for n in (2, 3, 8, 9, 0, 1, 4, 5, 10, 11):
        go_on(n)
    small_back.wait_recv()
    back_core = put(all_e.at[:, :, core], all_e.at[:, :, core], small_sem.at[10], small_sem.at[11], other)
    for n in (2, 3, 6, 7, 4, 5, 8, 9):
        go_on(n)
    to_tp.wait_recv()
    for i in range(4):
        stream_out[:, 128 * i:128 * i + 128] = gg[4 * tp + i] + tp_in[i]
    back_core.wait_recv()
    mixer_out[...] = all_e[:, :, :, :, 0:128].reshape(WIDTH, 128)
    for i in range(8):
        rt[:, 128 * i:128 * i + 128] = all_e[i // 2, 2 * (i % 2):2 * (i % 2) + 2, :, :, 128:256].reshape(128, 128)
    step_out[...] = rt[pl.ds(heads_at, 16), :]
    gain_out[...] = rt[32:33, :]
    table_out[...] = rt[40:45, :]
    scalars_out[...] = rt[pl.ds(scalars_at, 16), 0:256]
    while any(job["at"] < 6 for job in jobs):
        low_at = min(job["at"] for job in jobs)
        for n, job in enumerate(jobs):
            if job["at"] == low_at:
                go_on(n)
    for n in range(6, 12):
        jobs[n]["core"].wait_send()
    remote(ring, ring, job_send.at[0], job_recv.at[0], other).wait_send()
    remote(ring2, ring2, job_send.at[1], job_recv.at[0], other).wait_send()
    remote(dp_in, dp_in, job_send.at[2], job_recv.at[0], other).wait_send()
    for copy in (to_tp, small_core, small_in, over_x, small_back, back_core):
        copy.wait_send()
    to_core(0, 0, 16).wait_send()
    for copy in (all_to_owners, all_to_chips, all_entering):
        copy.wait_send()


def main(base, stream, cotangent, table, gain, w, mw, swt, bias, rate, spread):
    vmem, anywhere = pl.BlockSpec(memory_space=pltpu.VMEM), pl.BlockSpec(memory_space=pl.ANY)
    rows = 2 * BASES

    def shape(*dims):
        return jax.ShapeDtypeStruct(dims, F32)

    def f32(*dims):
        return pltpu.VMEM(dims, F32)

    def bf16(*dims):
        return pltpu.VMEM(dims, BF16)

    def sems(n):
        return pltpu.SemaphoreType.DMA((n,))

    jobs = len(ORDER)
    return pl.pallas_call(
        main_kernel,
        out_shape=[
            shape(3, 16, WIDTH), shape(WIDTH, 128), shape(HEADS, WIDTH), shape(5, WIDTH), shape(1, WIDTH),
            shape(HEADS, 256), shape(BASES, WIDTH // 2),
        ],
        in_specs=[vmem] * 5 + [anywhere] + [vmem] * 5,
        out_specs=[vmem] * 7,
        scratch_shapes=[
            bf16(3, WIDTH, WIDTH), f32(8, WIDTH), bf16(rows, WIDTH), f32(rows, WIDTH), f32(rows, 1),
            f32(2, PAIRS, BASES, 128), f32(2, PAIRS, BASES, 128), f32(PAIRS, BASES, 128),
            bf16(2, BASES, 128), f32(2, HEADS, BASES), bf16(2, BASES, 128), bf16(2, 128, BASES), f32(2, HEADS, BASES),
            f32(2, HEADS, BASES), bf16(2, PAIRS, BASES, 128), bf16(2, PAIRS, BASES, 128),
            f32(2, PAIRS, BASES, 128), f32(2, PAIRS, BASES, 128), f32(2, BASES, BASES),
            f32(2, BASES, 128), f32(2, BASES, 128), f32(2, 8, 128), f32(2, BASES, STATE), f32(2, BASES, STATE),
            f32(2, PAIRS, BASES, 128),
            f32(2 * CHIPS, 72, 128), f32(CHIPS, 72, 128), f32(CHIPS, 72, 128), f32(CHIPS, 72, 128),
            f32(CHIPS, STATE, 128), f32(CHIPS, STATE, 128), f32(2 * CHIPS, STATE, 128),
            bf16(rows, WIDTH), bf16(rows, WIDTH), bf16(rows, 128), f32(HEADS, rows), f32(HEADS, 2),
            bf16(WIDTH, rows), bf16(WIDTH, BASES), f32(128, WIDTH),
            f32(6, 2, 4, 4, 2, 32, 128), f32(jobs, 2, 4, 4, 32, 128), f32(jobs, 6, 4, 32, 128), f32(jobs, 2, 4, 32, 128),
            f32(jobs, 6, 32, 128), f32(jobs, 2, 32, 128), f32(jobs, 2, 16, 128),
            f32(4, 4, 2, 32, 256), f32(4, 4, 32, 256), f32(16, 32, 256), f32(2, 32, 256), f32(3, 32, 256),
            f32(4, 4, 2, 32, 256), f32(4, BASES, 128),
            sems(3), sems(3), sems(6), sems(6 * jobs), sems(jobs), sems(3), sems(12),
        ],
        compiler_params=pltpu.CompilerParams(collective_id=0, has_side_effects=True, vmem_limit_bytes=62 << 20),
        name="main",
    )(base, stream, cotangent, table, gain, w, mw, swt, bias, rate, spread)


def emit_kernel(grads, mixer, steps, by_base, by_gain, scalars, stream,
                grads_out, mixer_out, steps_out, base_out, gain_out, bias_out, rate_out, stream_out):
    for source, target in ((grads, grads_out), (mixer, mixer_out), (steps, steps_out), (by_base, base_out),
                           (by_gain, gain_out), (stream, stream_out)):
        target[...] = source[...]
    same = iota((HEADS, HEADS), 0) == iota((HEADS, HEADS), 1)
    for first, target in ((0, bias_out), (128, rate_out)):
        target[...] = jnp.sum(jnp.where(same, scalars[:, first:first + HEADS], 0.0), axis=0, keepdims=True)


def emit(*results):
    vmem = pl.BlockSpec(memory_space=pltpu.VMEM)
    like = [jax.ShapeDtypeStruct(r.shape, F32) for r in results]
    row = jax.ShapeDtypeStruct((1, HEADS), F32)
    return pl.pallas_call(
        emit_kernel,
        out_shape=like[:5] + [row, row] + like[6:],
        in_specs=[vmem] * 7,
        out_specs=[vmem] * 8,
        name="emit",
    )(*results)


def body(base_ids, stream, cotangent, table, gain, projections, mixer_weight, step_weight, step_bias, rate):
    results = main(
        base_ids, stream, cotangent, table, gain[None], jnp.transpose(projections, (1, 0, 2)), mixer_weight,
        jnp.transpose(step_weight), step_bias[None], rate[None], jnp.asarray(spreads(), BF16))
    grads, mixer, steps, by_base, by_gain, by_bias, by_rate, stream_grad = emit(*results)
    return (
        jnp.transpose(grads, (1, 0, 2)),
        mixer,
        jnp.transpose(steps),
        by_bias[0],
        by_rate[0],
        by_base,
        by_gain[0],
        stream_grad[None],
    )


def solution(mesh):
    return jax.shard_map(
        body,
        mesh=mesh,
        in_specs=(
            P("dp", "ctx"),
            P("dp", "ctx", None),
            P("dp", "ctx", None),
            P(),
            P(),
            P(None, None, "tp"),
            P(),
            P(None, "tp"),
            P("tp"),
            P("tp"),
        ),
        out_specs=(
            P(("ctx", "dp"), None, "tp"),
            P(),
            P(None, "tp"),
            P("tp"),
            P("tp"),
            P(),
            P(),
            P("dp", "ctx", "tp"),
        ),
        check_vma=False,
    )
```

```python
import functools

import jax
import jax.numpy as jnp
import numpy as np
from jax import lax
from jax.experimental import pallas as pl
from jax.experimental.pallas import tpu as pltpu
from jax.sharding import PartitionSpec as P

EPS = 1e-05
HIGH = lax.Precision.HIGHEST
F32 = jnp.float32
BF16 = jnp.bfloat16
MESH = pl.DeviceIdType.MESH
BASES = 256
WIDTH = 1024
HEADS = 16
PAIRS = 8
STATE = 64


def nt(left, right):
    return lax.dot_general(left, right, (((1,), (1,)), ((), ())), preferred_element_type=F32)


def tn(left, right):
    return lax.dot_general(left, right, (((0,), (0,)), ((), ())), preferred_element_type=F32)


def dot(left, right):
    return jnp.dot(left, right, preferred_element_type=F32)


def exact(left, right):
    return jnp.dot(left, right, preferred_element_type=F32, precision=HIGH)


def split3(x):
    a = x.astype(BF16).astype(F32)
    b = (x - a).astype(BF16).astype(F32)
    return a, b, x - a - b


def split2(x):
    a = x.astype(BF16)
    return a, (x - a.astype(F32)).astype(BF16)


def summed3(x, ones):
    r = dot(jnp.concatenate(split3(x), axis=0).astype(BF16), ones)
    n = x.shape[0]
    return r[0:n] + r[n:2 * n] + r[2 * n:3 * n]


def iota(shape, dim):
    return lax.broadcasted_iota(jnp.int32, shape, dim)


def spreads():
    j, r, c = np.indices((PAIRS, 128, 256))
    return np.logical_and(r // 48 == c // 128, r % 16 == 2 * j + c % 128 // 64).astype(np.float32)


CHIPS = 16
ORDER = [(q, k) for q in range(4) for k in (2, 1, 0)]
PLAN = [
    ("outside", 0, 0), ("outside", 1, 0), ("product", 0), ("product", 1), ("product", 2), ("outside", 0, 1),
    ("outside", 1, 1), ("job", 0), ("job", 1), ("product", 3), ("product", 4), ("job", 2),
    ("product", 5), ("outside", 0, 2), ("job", 3), ("outside", 1, 2), ("job", 0), ("job", 4),
    ("job", 1), ("outside", 0, 3), ("job", 5), ("outside", 1, 3), ("job", 2), ("finish",),
    ("job", 3), ("small", 0, 0), ("features", 0), ("features", 1), ("job", 0), ("job", 1),
    ("features", 2), ("small", 0, 1), ("job", 4), ("features", 3), ("job", 5), ("embedded",),
    ("small", 1, 0), ("product", 6), ("job", 2), ("job", 3), ("job", 1), ("job", 0),
    ("product", 7), ("small", 1, 1), ("job", 4), ("small", 0, 2), ("job", 5), ("job", 6),
    ("product", 8), ("job", 2), ("job", 3), ("job", 7), ("job", 0), ("job", 1),
    ("product", 9), ("job", 4), ("product", 10), ("job", 8), ("product", 11), ("job", 5),
    ("job", 2), ("small", 1, 2), ("job", 9), ("job", 10), ("job", 6), ("small", 0, 3),
    ("job", 7), ("job", 11), ("job", 3), ("job", 4), ("job", 8), ("small", 0, 4),
    ("job", 9), ("job", 5), ("job", 7), ("job", 10), ("small", 1, 3), ("job", 11),
    ("job", 0), ("job", 1), ("job", 2), ("job", 3), ("job", 4), ("job", 6),
    ("job", 5), ("small", 1, 4), ("job", 8), ("job", 9), ("job", 7), ("job", 11),
    ("job", 6), ("small", 0, 5), ("job", 10), ("job", 8), ("job", 9), ("job", 6),
    ("job", 7), ("job", 11), ("job", 10), ("small", 1, 5), ("job", 8), ("job", 9),
    ("small", 0, 6), ("job", 11), ("job", 10), ("job", 6), ("small", 0, 7), ("job", 7),
    ("small", 1, 6), ("job", 8), ("small", 1, 7), ("job", 9), ("job", 11), ("job", 10),
]


def main_kernel(base, x, up, table, gain, w, mw, swt, bias, rate, spread,
                grads_out, mixer_out, step_out, table_out, gain_out, scalars_out, stream_out,
                wv, f, normed_s, inv_s, v, g, gg, quant, run_t, maps, maps_t, logit_t, step_t, drive_b, go_b, out, gd, pairs,
                acc, acc_v, kk, gmaps, swish_s, src, from_core, totals, recv, scanned, res, ent,
                gv, gate, gm, glt, rates, ft, upt, rt, prod, core_in, ring, mid, ring2, fin, dp_in,
                prod_e, core_e, parts, mine_e, far_in, tp_in_e, sum_x, gat, all_e, tp_in,
                wsem, core_sem, state_sem, job_recv, job_core, job_send, small_sem):
    ctx, tp, dp = lax.axis_index("ctx"), lax.axis_index("tp"), lax.axis_index("dp")
    core, chip = ctx % 2, ctx // 2
    y, z = chip % 4, chip // 4

    def on(c):
        return {"ctx": c * 2 + core}

    other = {"ctx": chip * 2 + 1 - core}
    tp_dev, dp_dev, far_dev = {"tp": 1 - tp}, {"dp": 1 - dp}, {"tp": 1 - tp, "dp": 1 - dp}
    y_dev = [on(z * 4 + (y + i) % 4) for i in range(4)]
    z_dev = [on(((z + i) % 4) * 4 + y) for i in range(4)]

    barrier = pltpu.get_barrier_semaphore()

    def greet(i, c):
        pl.semaphore_signal(barrier, inc=1, device_id=on(lax.rem(chip + i, CHIPS)), device_id_type=MESH)
        return c

    lax.fori_loop(1, CHIPS, greet, 0)
    for device in (other, tp_dev, dp_dev, far_dev):
        pl.semaphore_signal(barrier, inc=1, device_id=device, device_id_type=MESH)
    copies = [pltpu.make_async_copy(w.at[k], wv.at[k], wsem.at[k]) for k in range(3)]
    for copy in copies:
        copy.start()

    rt[0:8, :] = jnp.zeros((8, WIDTH), F32)
    rt[0:5, :] = table[...]
    pieces = jnp.concatenate(split3(rt[0:8, :]), axis=0).astype(BF16)
    incoming = x[0].astype(F32)
    hots = []
    for d in range(2):
        ids = base[...]
        if d:
            ids = jnp.where(ids == 4, 4, 3 - ids)
        hot = (iota((8, BASES), 0) == ids).astype(F32)
        hots.append(hot.astype(BF16))
        embedded = incoming + tn(jnp.concatenate([hot, hot, hot], axis=0).astype(BF16), pieces)
        inv = lax.rsqrt(jnp.mean(embedded * embedded, axis=1, keepdims=True) + EPS)
        normed = embedded * inv
        rows = slice(BASES * d, BASES * (d + 1))
        normed_s[rows, :] = normed
        inv_s[rows, :] = inv
        f[rows, :] = (normed * gain[...]).astype(BF16)

    def column(row):
        square = jnp.broadcast_to(row, (HEADS, HEADS))
        return jnp.sum(jnp.where(iota((HEADS, HEADS), 0) == iota((HEADS, HEADS), 1), square, 0.0), axis=1, keepdims=True)

    rate_c = column(rate[...])
    mapped = dot(f[...], mw[...])
    for d in range(2):
        maps[d] = mapped[BASES * d:BASES * (d + 1)].astype(BF16)
        maps_t[d] = jnp.transpose(mapped[BASES * d:BASES * (d + 1)]).astype(BF16)
    logits = nt(swt[...], f[...]) + column(bias[...])
    rows_i, cols_i = iota((BASES, BASES), 0), iota((BASES, BASES), 1)
    for d in range(2):
        logit = logits[:, BASES * d:BASES * (d + 1)]
        step = jnp.maximum(logit, 0.0) + jnp.log1p(jnp.exp(-jnp.abs(logit)))
        logit_t[d] = logit
        step_t[d] = step
        upto = (rows_i <= cols_i) if d == 0 else (rows_i >= cols_i)
        run = summed3(-step * rate_c, upto.astype(F32).astype(BF16))
        run_t[d] = run
        whole = jnp.concatenate(split3(run) + split3(step) + (jnp.zeros((32, BASES), F32),), axis=0)
        quant[d] = jnp.transpose(whole).astype(BF16)
        pairs[d] = jnp.zeros((BASES, BASES), F32)
        acc[d] = jnp.zeros((BASES, 128), F32)
        acc_v[d] = jnp.zeros((BASES, 128), F32)
        kk[d] = jnp.zeros((8, 128), F32)
        gmaps[d] = jnp.zeros((BASES, 128), F32)
    for k, target in ((0, v), (1, g)):
        copies[k].wait()
        for c in range(4):
            block = dot(f[...], wv[k, :, 256 * c:256 * c + 256])
            for d in range(2):
                for i in range(2):
                    target[d, 2 * c + i] = block[BASES * d:BASES * (d + 1), 128 * i:128 * i + 128]
    copies[2].wait()
    for c in range(4):
        block = dot(up[0], wv[2, :, 256 * c:256 * c + 256])
        for i in range(2):
            gg[2 * c + i] = block[:, 128 * i:128 * i + 128]

    def expand(d, j):
        both = dot(quant[d], spread[j])
        run_e, step_e = both[:, 0:128], both[:, 128:256]
        final = run_e[BASES - 1:BASES] if d == 0 else run_e[0:1]
        return run_e, step_e, final

    def remote(source, target, sent, arrived, device):
        return pltpu.make_async_remote_copy(
            src_ref=source, dst_ref=target, send_sem=sent, recv_sem=arrived, device_id=device, device_id_type=MESH)

    def to_core(i, half, n=1):
        source = src.at[CHIPS * (1 - core) + i] if n == 1 else src.at[pl.ds(0, n)]
        target = from_core.at[i] if n == 1 else from_core.at[pl.ds(i, n)]
        return remote(source, target, core_sem.at[2], core_sem.at[half], other)

    def to_owner(i):
        return remote(totals.at[i], recv.at[chip], state_sem.at[0], state_sem.at[1], on(i))

    all_to_owners = remote(totals.at[pl.ds(0, 15)], recv.at[pl.ds(0, 15)], state_sem.at[0], state_sem.at[1], other)

    def to_chip(i):
        return remote(scanned.at[i], res.at[chip], state_sem.at[2], state_sem.at[3], on(i))

    all_to_chips = remote(scanned.at[pl.ds(0, 15)], res.at[pl.ds(0, 15)], state_sem.at[2], state_sem.at[3], other)

    def entering(i):
        return remote(from_core.at[i, pl.ds(0, 64)], ent.at[CHIPS * core + i], state_sem.at[4], state_sem.at[5], other)

    all_entering = remote(ent.at[pl.ds(CHIPS * core, CHIPS)], ent.at[pl.ds(CHIPS * (1 - core), CHIPS)], state_sem.at[4], state_sem.at[5], other)

    pl.semaphore_wait(barrier, CHIPS + 3)

    def ends(d, first, last):
        def step(j, c):
            run_e, step_e, final = expand(d, j)
            drive = step_e * v[d, j]
            gates = g[d, j]
            sigma = jax.nn.sigmoid(gates)
            swish = gates * sigma
            go = gg[j] * swish
            drive_b[d, j] = drive.astype(BF16)
            go_b[d, j] = go.astype(BF16)
            swish_s[d, j] = swish
            late_drive = (drive * jnp.exp(final - run_e)).astype(BF16)
            late_go = (go * jnp.exp(run_e)).astype(BF16)
            lanes = pl.ds(pl.multiple_of(128 * j, 128), 128)
            wv[2, BASES * d:BASES * (d + 1), lanes] = late_drive
            wv[2, BASES * (d + 2):BASES * (d + 3), lanes] = late_go
            state = dot(maps_t[d, 0:64, :], late_drive)
            grad = dot(maps_t[d, 64:128, :], late_go)
            decay = jnp.broadcast_to(jnp.exp(final), (8, 128))
            for t, value in ((16 * d + j, state), (24 - 16 * d + j, grad)):
                src[t, 0:64, :] = value
                src[t, 64:72, :] = decay
            half = (1 - core) if d == 0 else core
            to_core(j + 8 * half, half).start()
            return c

        lax.fori_loop(first, last, step, 0)

    def combine(i, c):
        here, there = src[CHIPS * core + i], from_core[i]
        totals[i, 0:64, :] = here[0:64] * there[64:65] + there[0:64]
        totals[i, 64:72, :] = here[64:72] * there[64:72]

        @pl.when(i != chip)
        def _():
            to_owner(i).start()
        return c

    def combine_half(half):
        to_core(8 * half, half, 8).wait_recv()
        lax.fori_loop(8 * half, 8 * half + 8, combine, 0)

    ends(0, 0, PAIRS)
    ends(1, 0, PAIRS // 2)
    combine_half(core)
    ends(1, PAIRS // 2, PAIRS)
    combine_half(1 - core)

    low = iota((BASES, 128), 1) < 64

    def inside(d):
        seen = (rows_i >= cols_i) if d == 0 else (rows_i <= cols_i)
        inflow_b, readout_b = maps[d, :, 0:64], maps[d, :, 64:128]
        affinity = nt(readout_b, inflow_b)

        def step(j, c):
            run_e, _, _ = expand(d, j)
            drive, go = drive_b[d, j], go_b[d, j]
            zero = jnp.zeros_like(drive)
            output = grad_drive = total = None
            for half in range(2):
                mine = low if half == 0 else jnp.logical_not(low)
                row = run_t[d, pl.ds(2 * j + half, 1), :]
                col = run_e[:, 64 * half:64 * half + 1]
                decay = jnp.exp(jnp.where(seen, col - row, -1e30))
                mixing = (decay * affinity).astype(BF16)
                drive_h = jnp.where(mine, drive, zero)
                go_h = jnp.where(mine, go, zero)
                a, b, e = dot(mixing, drive_h), tn(mixing, go_h), decay * nt(go_h, drive)
                output = a if output is None else output + a
                grad_drive = b if grad_drive is None else grad_drive + b
                total = e if total is None else total + e
            out[d, j] = output
            gd[d, j] = grad_drive
            pairs[d] += total
            return c

        lax.fori_loop(0, PAIRS, step, 0)

    inside(0)

    recv[chip] = totals[chip]
    all_to_owners.wait_recv()

    def scan(i, carry):
        t = i + core * (CHIPS - 1 - 2 * i)
        scanned[t] = carry

        @pl.when(t != chip)
        def _():
            to_chip(t).start()
        return carry * recv[t, 64:65, :] + recv[t, 0:64, :]

    lax.fori_loop(0, CHIPS, scan, jnp.zeros((STATE, 128), F32))
    res[chip] = scanned[chip]

    inside(1)
    for c in range(4):
        ft[256 * c:256 * c + 256, :] = jnp.transpose(f[:, 256 * c:256 * c + 256])
        upt[256 * c:256 * c + 256, :] = jnp.transpose(up[0, :, 256 * c:256 * c + 256])
    gated = f
    for d in range(2):
        def prepare(j, c, d=d):
            gates, swish = g[d, j], swish_s[d, j]
            sigma = jax.nn.sigmoid(gates)
            g[d, j] = gg[j] * (sigma + swish * (1.0 - sigma))
            return c

        lax.fori_loop(0, PAIRS, prepare, 0)
    all_to_chips.wait_recv()

    def hand_on(i, c):
        first = res[i]
        here = src[CHIPS * core + i]
        from_core[i, 0:64, :] = first * here[64:65] + here[0:64]
        entering(i).start()
        ent[CHIPS * core + i] = first
        return c

    lax.fori_loop(0, CHIPS, hand_on, 0)

    all_entering.wait_recv()

    def put(source, target, sent, arrived, device):
        copy = remote(source, target, sent, arrived, device)
        copy.start()
        return copy

    jobs = []
    for n, (q, k) in enumerate(ORDER):
        jobs.append(dict(n=n, stream=n % 2, prod=prod.at[n % 6], acc=core_in.at[n], ring=ring.at[n], mid=mid.at[n],
                         ring2=ring2.at[n], fin=fin.at[n], dp=dp_in.at[n]))

    def core_start(job):
        n = job["n"]
        job["core"] = put(job["prod"].at[:, :, :, 1 - core], job["acc"], job_core.at[n], job_recv.at[6 * n], other)

    def core_end(job):
        job["core"].wait_recv()
        job["acc"][...] = job["acc"][...] + job["prod"][:, :, :, core]

    def chunk(ref, h, c, stream, stage):
        if stream == 0 and stage == 1:
            return ref.at[h, :, c]
        return ref.at[h, c]

    def place(job, stage):
        over_y = (job["stream"] == 0) == (stage == 1)
        return (y, y_dev) if over_y else (z, z_dev)

    def refs(job, stage):
        return (job["acc"], job["ring"], job["mid"]) if stage == 1 else (job["mid"], job["ring2"], job["fin"])

    def ring_start(job, stage):
        p, dev = place(job, stage)
        s = job["stream"]
        ref, buffer, _ = refs(job, stage)
        sent, first, second = job_send.at[stage - 1], job_recv.at[6 * job["n"] + 2 * stage - 1], job_recv.at[6 * job["n"] + 2 * stage]
        put(chunk(ref, 0, (p + 2) % 4, s, stage), buffer.at[0], sent, first, dev[1])
        put(chunk(ref, 1, (p + 2) % 4, s, stage), buffer.at[1], sent, first, dev[3])
        put(chunk(ref, 1, (p + 1) % 4, s, stage), buffer.at[2], sent, second, dev[1])
        put(chunk(ref, 0, (p + 3) % 4, s, stage), buffer.at[3], sent, second, dev[3])

    def ring_middle(job, stage):
        p, dev = place(job, stage)
        s = job["stream"]
        ref, buffer, _ = refs(job, stage)
        sent, first, second = job_send.at[stage - 1], job_recv.at[6 * job["n"] + 2 * stage - 1], job_recv.at[6 * job["n"] + 2 * stage]
        remote(buffer.at[pl.ds(0, 2)], buffer.at[pl.ds(0, 2)], sent, first, other).wait_recv()
        ahead = chunk(ref, 0, (p + 1) % 4, s, stage)
        ahead[...] = ahead[...] + buffer[0]
        put(ahead, buffer.at[4], sent, second, dev[1])
        behind = chunk(ref, 1, (p + 3) % 4, s, stage)
        behind[...] = behind[...] + buffer[1]
        put(behind, buffer.at[5], sent, second, dev[3])

    def ring_end(job, stage):
        p, dev = place(job, stage)
        s = job["stream"]
        ref, buffer, into = refs(job, stage)
        sent, second = job_send.at[stage - 1], job_recv.at[6 * job["n"] + 2 * stage]
        remote(buffer.at[pl.ds(2, 4)], buffer.at[pl.ds(2, 4)], sent, second, other).wait_recv()
        into[0] = chunk(ref, 0, p, s, stage)[...] + buffer[3] + buffer[4]
        into[1] = chunk(ref, 1, p, s, stage)[...] + buffer[2] + buffer[5]

    mine = pl.ds(pl.multiple_of(16 * dp, 16), 16)
    yours = pl.ds(pl.multiple_of(16 * (1 - dp), 16), 16)

    def go_on(n):
        job = jobs[n]
        at = job.get("at", 0)
        job["at"] = at + 1
        q, k = ORDER[n]
        if at == 0:
            core_end(job)
            ring_start(job, 1)
        elif at == 1:
            ring_middle(job, 1)
        elif at == 2:
            ring_end(job, 1)
            ring_start(job, 2)
        elif at == 3:
            ring_middle(job, 2)
        elif at == 4:
            ring_end(job, 2)
            job["over_dp"] = put(
                job["fin"].at[:, yours, :], job["dp"], job_send.at[2], job_recv.at[6 * n + 5], dp_dev)
        else:
            job["over_dp"].wait_recv()
            for h in range(2):
                first = 256 * q + 128 * h
                grads_out[k, :, first:first + 128] = job["fin"][h, mine, :] + job["dp"][h]

    def outside(d, q):
        rows = slice(BASES * d, BASES * (d + 1))
        inflow_b, readout_b = maps[d, :, 0:64], maps[d, :, 64:128]

        def step(j, c):
            run_e, step_e, final = expand(d, j)
            initial, after = ent[16 * d + j], ent[24 - 16 * d + j]
            initial_b, after_b = initial.astype(BF16), after.astype(BF16)
            head, tail = jnp.exp(run_e), jnp.exp(final - run_e)
            drive_r, go_r = drive_b[d, j].astype(F32), go_b[d, j].astype(F32)
            carried = dot(readout_b, initial_b) * head
            output = out[d, j] + carried
            grad_drive = gd[d, j] + dot(inflow_b, after_b) * tail
            values, to_heads = v[d, j], spread[j, :, 0:128]
            a, b = split2(grad_drive * drive_r - go_r * output)
            acc[d] += nt(a, to_heads) + nt(b, to_heads)
            acc_v[d] += nt((grad_drive * values).astype(BF16), to_heads)
            boundary = jnp.sum(go_r * carried, axis=0, keepdims=True) + jnp.exp(final) * jnp.sum(
                initial * after, axis=0, keepdims=True)
            a, b = split2(jnp.broadcast_to(boundary, (16, 128)))
            kk[d] += (nt(a, to_heads) + nt(b, to_heads))[0:8]
            lanes = pl.ds(pl.multiple_of(128 * j, 128), 128)
            gmaps[d, :, 0:64] += nt(wv[2, BASES * d:BASES * (d + 1), lanes], after_b)
            gmaps[d, :, 64:128] += nt(wv[2, BASES * (d + 2):BASES * (d + 3), lanes], initial_b)
            gv[rows, lanes] = (step_e * grad_drive).astype(BF16)
            gate[rows, lanes] = (g[d, j] * output).astype(BF16)
            gated[rows, lanes] = (output * swish_s[d, j]).astype(BF16)
            return c

        lax.fori_loop(2 * q, 2 * q + 2, step, 0)

    def product(n):
        q, k = ORDER[n]
        result = (gv, gate, gated)[k]
        lanes = slice(256 * q, 256 * q + 256)
        if n >= 6:
            jobs[n - 6]["core"].wait_send()

        for i in range(2):
            rows = slice(512 * i, 512 * i + 512)
            if k == 2:
                block = dot(upt[rows, :], result[0:BASES, lanes]) + dot(upt[rows, :], result[BASES:, lanes])
            else:
                block = dot(ft[rows, :], result[:, lanes])
            for h in range(2):
                prod[n % 6, h, 2 * i:2 * i + 2] = block[:, 128 * h:128 * h + 128].reshape(2, 4, 2, 32, 128)
        core_start(jobs[n])

    def finish():
        for d in range(2):
            rows = slice(BASES * d, BASES * (d + 1))
            inflow_b, readout_b = maps[d, :, 0:64], maps[d, :, 64:128]
            pairs_b = pairs[d].astype(BF16)
            gin = gmaps[d, :, 0:64] + tn(pairs_b, readout_b)
            gread = gmaps[d, :, 64:128] + dot(pairs_b, inflow_b)
            gm[rows, :] = jnp.concatenate([gin, gread], axis=1).astype(BF16)
            per_head = jnp.transpose(acc[d])
            boundary = jnp.transpose(jnp.broadcast_to(kk[d, 0:1, :], (128, 128)))[0:16, 0:1]
            earlier = (rows_i < cols_i) if d == 0 else (rows_i > cols_i)
            grad_log = summed3(per_head[0:16], earlier.astype(F32).astype(BF16)) + boundary
            grad_step = jnp.transpose(acc_v[d])[0:16] - grad_log * rate_c
            glt[:, rows] = grad_step * jax.nn.sigmoid(logit_t[d])
            rates[:, d:d + 1] = -jnp.sum(grad_log * step_t[d], axis=1, keepdims=True)

    mean = [jnp.zeros((BASES, 1), F32)] * 2

    def features(c):
        glb = glt[...].astype(BF16)
        lanes = slice(256 * c, 256 * c + 256)
        by_gain = jnp.zeros((1, 256), F32)
        for d in range(2):
            rows = slice(BASES * d, BASES * (d + 1))
            gf = (nt(gv[rows, :], wv[0, lanes, :]) + nt(gate[rows, :], wv[1, lanes, :]) + nt(gm[rows, :], mw[lanes, :])
                  + tn(glb[:, rows], swt[:, lanes]))
            nrm = normed_s[rows, lanes]
            scaled = gf * gain[:, lanes]
            for i in range(2):
                v[d, 2 * c + i] = scaled[:, 128 * i:128 * i + 128]
            mean[d] = mean[d] + jnp.sum(scaled * nrm, axis=1, keepdims=True)
            by_gain = by_gain + jnp.sum(gf * nrm, axis=0, keepdims=True)
        rt[32:40, lanes] = jnp.broadcast_to(by_gain, (8, 256))

    def embedded_grad():
        for c in range(8):
            lanes = slice(128 * c, 128 * c + 128)
            residual = 0.5 * up[0, :, lanes].astype(F32)
            by_base = jnp.zeros((8, 128), F32)
            whole = None
            for d in range(2):
                rows = slice(BASES * d, BASES * (d + 1))
                ge = inv_s[rows, :] * (v[d, c] - normed_s[rows, lanes] * (mean[d] * (1.0 / WIDTH))) + residual
                whole = ge if whole is None else whole + ge
                for part in split3(ge):
                    by_base = by_base + dot(hots[d], part.astype(BF16))
            gg[c] = whole
            rt[40:48, lanes] = by_base

    heads_at = pl.multiple_of(16 * tp, 16)
    scalars_at = pl.multiple_of(48 + 16 * tp, 16)
    offsets = [(dz, dy) for dz in range(4) for dy in range(4)][1:]
    small = [{}, {}]

    def small_step(h, at):
        now = small[h]

        def pair(i):
            return small_sem.at[2 + 12 * h + 2 * i], small_sem.at[3 + 12 * h + 2 * i]

        fifteen = parts.at[h, pl.ds(1, 15)]
        if at == 0:
            if h == 0:
                for i in range(4):
                    prod_e[0, i] = dot(ft[256 * i:256 * i + 256, :], gm[...]).reshape(4, 2, 32, 128)
            else:
                rt[0:32, :] = jnp.zeros((32, WIDTH), F32)
                rt[48:128, :] = jnp.zeros((80, WIDTH), F32)
                rt[pl.ds(heads_at, 16), :] = nt(glt[...].astype(BF16), ft[...])
                rt[pl.ds(scalars_at, 16), 0:128] = jnp.broadcast_to(
                    jnp.sum(glt[...], axis=1, keepdims=True), (HEADS, 128))
                rt[pl.ds(scalars_at, 16), 128:256] = jnp.broadcast_to(rates[:, 0:1] + rates[:, 1:2], (HEADS, 128))
                for i in range(8):
                    prod_e[1, i // 2, 2 * (i % 2):2 * (i % 2) + 2] = rt[:, 128 * i:128 * i + 128].reshape(2, 2, 32, 128)
            now[0] = put(prod_e.at[h, :, :, 1 - core], core_e.at[h], *pair(0), other)
        elif at == 1:
            now[0].wait_recv()
            core_e[h] = core_e[h] + prod_e[h, :, :, core]
            now[1] = put(core_e.at[h, :, :, yours], far_in.at[h], *pair(1), far_dev)
            if h == 1:
                now["tp"] = put(gg.at[pl.ds(4 * (1 - tp), 4)], tp_in, small_sem.at[0], small_sem.at[1], tp_dev)
        elif at == 2:
            now[1].wait_recv()
            sum_x[h] = core_e[h, :, :, mine] + far_in[h]
            for dz, dy in offsets:
                zz, yy = (z + dz) % 4, (y + dy) % 4
                put(sum_x.at[h, zz, yy], parts.at[h, 4 * dz + dy], *pair(2), on(zz * 4 + yy))
            now[2] = remote(fifteen, fifteen, *pair(2), other)
        elif at == 3:
            now[2].wait_recv()
            total = sum_x[h, z, y]
            for i in range(15):
                total = total + parts[h, i + 1]
            mine_e[h, 0] = total
            now[3] = put(mine_e.at[h, 0], tp_in_e.at[h], *pair(3), tp_dev)
        elif at == 4:
            now[3].wait_recv()
            total = mine_e[h, 0] + tp_in_e[h]
            mine_e[h, 1] = total
            gat[h, z, y] = total
            for dz, dy in offsets:
                put(mine_e.at[h, 1], gat.at[h, z, y], *pair(4), on(((z + dz) % 4) * 4 + (y + dy) % 4))
            now[4] = remote(fifteen, fifteen, *pair(4), other)
        elif at == 5:
            now[4].wait_recv()
            all_e[h, :, :, core, mine] = gat[h]
            now[5] = put(gat.at[h], all_e.at[h, :, :, core, mine], *pair(5), far_dev)
        elif at == 6:
            now[5].wait_recv()
            now[6] = put(all_e.at[h, :, :, core], all_e.at[h, :, :, core], small_sem.at[26 + 2 * h],
                         small_sem.at[27 + 2 * h], other)
        else:
            now[6].wait_recv()
            if h == 0:
                mixer_out[...] = all_e[0].reshape(WIDTH, 128)
            else:
                for i in range(8):
                    rt[:, 128 * i:128 * i + 128] = all_e[1, i // 2, 2 * (i % 2):2 * (i % 2) + 2].reshape(128, 128)
                step_out[...] = rt[pl.ds(heads_at, 16), :]
                gain_out[...] = rt[32:33, :]
                table_out[...] = rt[40:45, :]
                scalars_out[...] = rt[pl.ds(scalars_at, 16), 0:256]

    acts = dict(outside=outside, product=product, finish=finish, features=features, embedded=embedded_grad,
                small=small_step, job=go_on)
    for name, *which in PLAN:
        acts[name](*which)
    small[1]["tp"].wait_recv()
    for i in range(4):
        stream_out[:, 128 * i:128 * i + 128] = gg[4 * tp + i] + tp_in[i]

    for n in range(6, 12):
        jobs[n]["core"].wait_send()
    remote(ring, ring, job_send.at[0], job_recv.at[0], other).wait_send()
    remote(ring2, ring2, job_send.at[1], job_recv.at[0], other).wait_send()
    remote(dp_in, dp_in, job_send.at[2], job_recv.at[0], other).wait_send()
    for half in small:
        for copy in half.values():
            copy.wait_send()
    to_core(0, 0, 16).wait_send()
    for copy in (all_to_owners, all_to_chips, all_entering):
        copy.wait_send()


def main(base, stream, cotangent, table, gain, w, mw, swt, bias, rate, spread):
    vmem, anywhere = pl.BlockSpec(memory_space=pltpu.VMEM), pl.BlockSpec(memory_space=pl.ANY)
    rows = 2 * BASES

    def shape(*dims):
        return jax.ShapeDtypeStruct(dims, F32)

    def f32(*dims):
        return pltpu.VMEM(dims, F32)

    def bf16(*dims):
        return pltpu.VMEM(dims, BF16)

    def sems(n):
        return pltpu.SemaphoreType.DMA((n,))

    jobs = len(ORDER)
    return pl.pallas_call(
        main_kernel,
        out_shape=[
            shape(3, 16, WIDTH), shape(WIDTH, 128), shape(HEADS, WIDTH), shape(5, WIDTH), shape(1, WIDTH),
            shape(HEADS, 256), shape(BASES, WIDTH // 2),
        ],
        in_specs=[vmem] * 5 + [anywhere] + [vmem] * 5,
        out_specs=[vmem] * 7,
        scratch_shapes=[
            bf16(3, WIDTH, WIDTH), bf16(rows, WIDTH), f32(rows, WIDTH), f32(rows, 1),
            f32(2, PAIRS, BASES, 128), f32(2, PAIRS, BASES, 128), f32(PAIRS, BASES, 128),
            bf16(2, BASES, 128), f32(2, HEADS, BASES), bf16(2, BASES, 128), bf16(2, 128, BASES), f32(2, HEADS, BASES),
            f32(2, HEADS, BASES), bf16(2, PAIRS, BASES, 128), bf16(2, PAIRS, BASES, 128),
            f32(2, PAIRS, BASES, 128), f32(2, PAIRS, BASES, 128), f32(2, BASES, BASES),
            f32(2, BASES, 128), f32(2, BASES, 128), f32(2, 8, 128), f32(2, BASES, 128),
            f32(2, PAIRS, BASES, 128),
            f32(2 * CHIPS, 72, 128), f32(CHIPS, 72, 128), f32(CHIPS, 72, 128), f32(CHIPS, 72, 128),
            f32(CHIPS, STATE, 128), f32(CHIPS, STATE, 128), f32(2 * CHIPS, STATE, 128),
            bf16(rows, WIDTH), bf16(rows, WIDTH), bf16(rows, 128), f32(HEADS, rows), f32(HEADS, 2),
            bf16(WIDTH, rows), bf16(WIDTH, BASES), f32(128, WIDTH),
            f32(6, 2, 4, 4, 2, 32, 128), f32(jobs, 2, 4, 4, 32, 128), f32(jobs, 6, 4, 32, 128), f32(jobs, 2, 4, 32, 128),
            f32(jobs, 6, 32, 128), f32(jobs, 2, 32, 128), f32(jobs, 2, 16, 128),
            f32(2, 4, 4, 2, 32, 128), f32(2, 4, 4, 32, 128), f32(2, 16, 16, 128), f32(2, 2, 16, 128), f32(2, 4, 4, 16, 128),
            f32(2, 16, 128), f32(2, 4, 4, 16, 128), f32(2, 4, 4, 16, 128), f32(2, 4, 4, 2, 32, 128), f32(4, BASES, 128),
            sems(3), sems(3), sems(6), sems(6 * jobs), sems(jobs), sems(3), sems(30),
        ],
        compiler_params=pltpu.CompilerParams(collective_id=0, has_side_effects=True, vmem_limit_bytes=125 << 19),
        name="main",
    )(base, stream, cotangent, table, gain, w, mw, swt, bias, rate, spread)


def emit_kernel(grads, mixer, steps, by_base, by_gain, scalars, stream,
                grads_out, mixer_out, steps_out, base_out, gain_out, bias_out, rate_out, stream_out):
    for source, target in ((grads, grads_out), (mixer, mixer_out), (steps, steps_out), (by_base, base_out),
                           (by_gain, gain_out), (stream, stream_out)):
        target[...] = source[...]
    same = iota((HEADS, HEADS), 0) == iota((HEADS, HEADS), 1)
    for first, target in ((0, bias_out), (128, rate_out)):
        target[...] = jnp.sum(jnp.where(same, scalars[:, first:first + HEADS], 0.0), axis=0, keepdims=True)


def emit(*results):
    vmem = pl.BlockSpec(memory_space=pltpu.VMEM)
    like = [jax.ShapeDtypeStruct(r.shape, F32) for r in results]
    row = jax.ShapeDtypeStruct((1, HEADS), F32)
    return pl.pallas_call(
        emit_kernel,
        out_shape=like[:5] + [row, row] + like[6:],
        in_specs=[vmem] * 7,
        out_specs=[vmem] * 8,
        name="emit",
    )(*results)


def body(base_ids, stream, cotangent, table, gain, projections, mixer_weight, step_weight, step_bias, rate):
    results = main(
        base_ids, stream, cotangent, table, gain[None], jnp.transpose(projections, (1, 0, 2)), mixer_weight,
        jnp.transpose(step_weight), step_bias[None], rate[None], jnp.asarray(spreads(), BF16))
    grads, mixer, steps, by_base, by_gain, by_bias, by_rate, stream_grad = emit(*results)
    return (
        jnp.transpose(grads, (1, 0, 2)),
        mixer,
        jnp.transpose(steps),
        by_bias[0],
        by_rate[0],
        by_base,
        by_gain[0],
        stream_grad[None],
    )


def solution(mesh):
    return jax.shard_map(
        body,
        mesh=mesh,
        in_specs=(
            P("dp", "ctx"),
            P("dp", "ctx", None),
            P("dp", "ctx", None),
            P(),
            P(),
            P(None, None, "tp"),
            P(),
            P(None, "tp"),
            P("tp"),
            P("tp"),
        ),
        out_specs=(
            P(("ctx", "dp"), None, "tp"),
            P(),
            P(None, "tp"),
            P("tp"),
            P("tp"),
            P(),
            P(),
            P("dp", "ctx", "tp"),
        ),
        check_vma=False,
    )
```

```python
import functools

import jax
import jax.numpy as jnp
import numpy as np
from jax import lax
from jax.experimental import pallas as pl
from jax.experimental.pallas import tpu as pltpu
from jax.sharding import PartitionSpec as P

EPS = 1e-05
HIGH = lax.Precision.HIGHEST
F32 = jnp.float32
BF16 = jnp.bfloat16
MESH = pl.DeviceIdType.MESH
BASES = 256
WIDTH = 1024
HEADS = 16
PAIRS = 8
STATE = 64


def nt(left, right):
    return lax.dot_general(left, right, (((1,), (1,)), ((), ())), preferred_element_type=F32)


def tn(left, right):
    return lax.dot_general(left, right, (((0,), (0,)), ((), ())), preferred_element_type=F32)


def dot(left, right):
    return jnp.dot(left, right, preferred_element_type=F32)


def exact(left, right):
    return jnp.dot(left, right, preferred_element_type=F32, precision=HIGH)


def split3(x):
    a = x.astype(BF16).astype(F32)
    b = (x - a).astype(BF16).astype(F32)
    return a, b, x - a - b


def split2(x):
    a = x.astype(BF16)
    return a, (x - a.astype(F32)).astype(BF16)


def summed3(x, ones):
    r = dot(jnp.concatenate(split3(x), axis=0).astype(BF16), ones)
    n = x.shape[0]
    return r[0:n] + r[n:2 * n] + r[2 * n:3 * n]


def iota(shape, dim):
    return lax.broadcasted_iota(jnp.int32, shape, dim)


def spreads():
    j, r, c = np.indices((PAIRS, 128, 256))
    return np.logical_and(r // 48 == c // 128, r % 16 == 2 * j + c % 128 // 64).astype(np.float32)


CHIPS = 16
ORDER = [(q, k) for q in range(4) for k in (2, 1, 0)]
PLAN = [
    ("outside", 0, 0), ("outside", 1, 0), ("product", 0), ("product", 1), ("outside", 0, 1), ("product", 2),
    ("outside", 1, 1), ("job", 0), ("job", 1), ("product", 3), ("product", 4), ("job", 2),
    ("outside", 0, 2), ("product", 5), ("job", 3), ("outside", 0, 3), ("outside", 1, 2), ("job", 1),
    ("job", 0), ("job", 4), ("job", 5), ("outside", 1, 3), ("finish",), ("small", 0, 0),
    ("job", 3), ("product", 6), ("job", 2), ("product", 7), ("features", 0), ("small", 0, 1),
    ("job", 0), ("job", 1), ("job", 6), ("features", 1), ("job", 4), ("job", 7),
    ("features", 2), ("features", 3), ("embedded",), ("small", 1, 0), ("job", 2), ("job", 5),
    ("product", 8), ("job", 3), ("small", 0, 2), ("small", 1, 1), ("product", 9), ("job", 7),
    ("job", 8), ("product", 10), ("job", 1), ("job", 9), ("job", 3), ("job", 6),
    ("product", 11), ("small", 1, 2), ("job", 7), ("job", 0), ("job", 11), ("small", 0, 3),
    ("job", 10), ("job", 3), ("job", 2), ("job", 5), ("job", 9), ("job", 0),
    ("small", 0, 4), ("job", 6), ("small", 1, 3), ("job", 8), ("job", 4), ("job", 10),
    ("job", 11), ("job", 7), ("job", 1), ("small", 1, 4), ("job", 2), ("job", 6),
    ("job", 4), ("job", 5), ("job", 9), ("job", 8), ("small", 0, 5), ("job", 10),
    ("job", 11), ("job", 0), ("job", 3), ("job", 6), ("job", 7), ("job", 5),
    ("job", 8), ("job", 4), ("job", 9), ("job", 10), ("small", 1, 5), ("job", 11),
    ("job", 8), ("job", 9), ("job", 10), ("job", 11), ("job", 7), ("job", 2),
    ("small", 0, 6), ("job", 6), ("job", 1), ("small", 1, 6), ("small", 0, 7), ("job", 5),
    ("job", 4), ("job", 8), ("small", 1, 7), ("job", 9), ("job", 10), ("job", 11),
]


def main_kernel(base, x, up, table, gain, w, mw, swt, bias, rate, spread,
                grads_out, mixer_out, step_out, table_out, gain_out, scalars_out, stream_out,
                wv, f, normed_s, inv_s, v, g, gg, quant, run_t, maps, maps_t, logit_t, step_t, drive_b, go_b, out, gd, pairs,
                acc, acc_v, kk, gmaps, swish_s, src, from_core, totals, recv, scanned, res, ent,
                gv, gate, gm, glt, rates, ft, upt, rt, prod, core_in, ring, mid, ring2, fin, dp_in,
                prod_e, core_e, parts, mine_e, far_in, tp_in_e, sum_x, gat, all_e, tp_in,
                wsem, core_sem, state_sem, job_recv, job_core, job_send, small_sem):
    ctx, tp, dp = lax.axis_index("ctx"), lax.axis_index("tp"), lax.axis_index("dp")
    core, chip = ctx % 2, ctx // 2
    y, z = chip % 4, chip // 4

    def on(c):
        return {"ctx": c * 2 + core}

    other = {"ctx": chip * 2 + 1 - core}
    tp_dev, dp_dev, far_dev = {"tp": 1 - tp}, {"dp": 1 - dp}, {"tp": 1 - tp, "dp": 1 - dp}
    y_dev = [on(z * 4 + (y + i) % 4) for i in range(4)]
    z_dev = [on(((z + i) % 4) * 4 + y) for i in range(4)]

    barrier = pltpu.get_barrier_semaphore()

    def greet(i, c):
        pl.semaphore_signal(barrier, inc=1, device_id=on(lax.rem(chip + i, CHIPS)), device_id_type=MESH)
        return c

    lax.fori_loop(1, CHIPS, greet, 0)
    for device in (other, tp_dev, dp_dev, far_dev):
        pl.semaphore_signal(barrier, inc=1, device_id=device, device_id_type=MESH)
    copies = [pltpu.make_async_copy(w.at[k], wv.at[k], wsem.at[k]) for k in range(3)]
    for copy in copies:
        copy.start()

    rt[0:8, :] = jnp.zeros((8, WIDTH), F32)
    rt[0:5, :] = table[...]
    pieces = jnp.concatenate(split3(rt[0:8, :]), axis=0).astype(BF16)
    incoming = x[0].astype(F32)
    hots = []
    for d in range(2):
        ids = base[...]
        if d:
            ids = jnp.where(ids == 4, 4, 3 - ids)
        hot = (iota((8, BASES), 0) == ids).astype(F32)
        hots.append(hot.astype(BF16))
        embedded = incoming + tn(jnp.concatenate([hot, hot, hot], axis=0).astype(BF16), pieces)
        inv = lax.rsqrt(jnp.mean(embedded * embedded, axis=1, keepdims=True) + EPS)
        normed = embedded * inv
        rows = slice(BASES * d, BASES * (d + 1))
        normed_s[rows, :] = normed
        inv_s[rows, :] = inv
        f[rows, :] = (normed * gain[...]).astype(BF16)

    def column(row):
        square = jnp.broadcast_to(row, (HEADS, HEADS))
        return jnp.sum(jnp.where(iota((HEADS, HEADS), 0) == iota((HEADS, HEADS), 1), square, 0.0), axis=1, keepdims=True)

    rate_c = column(rate[...])
    mapped = dot(f[...], mw[...])
    for d in range(2):
        maps[d] = mapped[BASES * d:BASES * (d + 1)].astype(BF16)
        maps_t[d] = jnp.transpose(mapped[BASES * d:BASES * (d + 1)]).astype(BF16)
    logits = nt(swt[...], f[...]) + column(bias[...])
    rows_i, cols_i = iota((BASES, BASES), 0), iota((BASES, BASES), 1)
    for d in range(2):
        logit = logits[:, BASES * d:BASES * (d + 1)]
        step = jnp.maximum(logit, 0.0) + jnp.log1p(jnp.exp(-jnp.abs(logit)))
        logit_t[d] = logit
        step_t[d] = step
        upto = (rows_i <= cols_i) if d == 0 else (rows_i >= cols_i)
        run = summed3(-step * rate_c, upto.astype(F32).astype(BF16))
        run_t[d] = run
        whole = jnp.concatenate(split3(run) + split3(step) + (jnp.zeros((32, BASES), F32),), axis=0)
        quant[d] = jnp.transpose(whole).astype(BF16)
        pairs[d] = jnp.zeros((BASES, BASES), F32)
        acc[d] = jnp.zeros((BASES, 128), F32)
        acc_v[d] = jnp.zeros((BASES, 128), F32)
        kk[d] = jnp.zeros((8, 128), F32)
        gmaps[d] = jnp.zeros((BASES, 128), F32)
    for k, target in ((0, v), (1, g)):
        copies[k].wait()
        for c in range(4):
            block = dot(f[...], wv[k, :, 256 * c:256 * c + 256])
            for d in range(2):
                for i in range(2):
                    target[d, 2 * c + i] = block[BASES * d:BASES * (d + 1), 128 * i:128 * i + 128]
    copies[2].wait()
    for c in range(4):
        block = dot(up[0], wv[2, :, 256 * c:256 * c + 256])
        for i in range(2):
            gg[2 * c + i] = block[:, 128 * i:128 * i + 128]

    def expand(d, j):
        both = dot(quant[d], spread[j])
        run_e, step_e = both[:, 0:128], both[:, 128:256]
        final = run_e[BASES - 1:BASES] if d == 0 else run_e[0:1]
        return run_e, step_e, final

    def remote(source, target, sent, arrived, device):
        return pltpu.make_async_remote_copy(
            src_ref=source, dst_ref=target, send_sem=sent, recv_sem=arrived, device_id=device, device_id_type=MESH)

    def to_core(i, half, n=1):
        source = src.at[CHIPS * (1 - core) + i] if n == 1 else src.at[pl.ds(0, n)]
        target = from_core.at[i] if n == 1 else from_core.at[pl.ds(i, n)]
        return remote(source, target, core_sem.at[2], core_sem.at[half], other)

    def to_owner(i):
        return remote(totals.at[i], recv.at[chip], state_sem.at[0], state_sem.at[1], on(i))

    all_to_owners = remote(totals.at[pl.ds(0, 15)], recv.at[pl.ds(0, 15)], state_sem.at[0], state_sem.at[1], other)

    def to_chip(i):
        return remote(scanned.at[i], res.at[chip], state_sem.at[2], state_sem.at[3], on(i))

    all_to_chips = remote(scanned.at[pl.ds(0, 15)], res.at[pl.ds(0, 15)], state_sem.at[2], state_sem.at[3], other)

    def entering(i):
        return remote(from_core.at[i, pl.ds(0, 64)], ent.at[CHIPS * core + i], state_sem.at[4], state_sem.at[5], other)

    all_entering = remote(ent.at[pl.ds(CHIPS * core, CHIPS)], ent.at[pl.ds(CHIPS * (1 - core), CHIPS)], state_sem.at[4], state_sem.at[5], other)

    pl.semaphore_wait(barrier, CHIPS + 3)

    def ends(d, first, last):
        def step(j, c):
            run_e, step_e, final = expand(d, j)
            drive = step_e * v[d, j]
            gates = g[d, j]
            sigma = jax.nn.sigmoid(gates)
            swish = gates * sigma
            go = gg[j] * swish
            drive_b[d, j] = drive.astype(BF16)
            go_b[d, j] = go.astype(BF16)
            swish_s[d, j] = swish
            late_drive = (drive * jnp.exp(final - run_e)).astype(BF16)
            late_go = (go * jnp.exp(run_e)).astype(BF16)
            lanes = pl.ds(pl.multiple_of(128 * j, 128), 128)
            wv[2, BASES * d:BASES * (d + 1), lanes] = late_drive
            wv[2, BASES * (d + 2):BASES * (d + 3), lanes] = late_go
            state = dot(maps_t[d, 0:64, :], late_drive)
            grad = dot(maps_t[d, 64:128, :], late_go)
            decay = jnp.broadcast_to(jnp.exp(final), (8, 128))
            for t, value in ((16 * d + j, state), (24 - 16 * d + j, grad)):
                src[t, 0:64, :] = value
                src[t, 64:72, :] = decay
            half = (1 - core) if d == 0 else core
            to_core(j + 8 * half, half).start()
            return c

        lax.fori_loop(first, last, step, 0, unroll=2)

    def combine(i, c):
        here, there = src[CHIPS * core + i], from_core[i]
        totals[i, 0:64, :] = here[0:64] * there[64:65] + there[0:64]
        totals[i, 64:72, :] = here[64:72] * there[64:72]

        @pl.when(i != chip)
        def _():
            to_owner(i).start()
        return c

    def combine_half(half):
        to_core(8 * half, half, 8).wait_recv()
        lax.fori_loop(8 * half, 8 * half + 8, combine, 0)

    ends(0, 0, PAIRS)
    ends(1, 0, PAIRS // 2)
    combine_half(core)
    ends(1, PAIRS // 2, PAIRS)
    combine_half(1 - core)

    low = iota((BASES, 128), 1) < 64

    def inside(d):
        seen = (rows_i >= cols_i) if d == 0 else (rows_i <= cols_i)
        inflow_b, readout_b = maps[d, :, 0:64], maps[d, :, 64:128]
        affinity = nt(readout_b, inflow_b)

        def step(j, c):
            run_e, _, _ = expand(d, j)
            drive, go = drive_b[d, j], go_b[d, j]
            zero = jnp.zeros_like(drive)
            output = grad_drive = total = None
            for half in range(2):
                mine = low if half == 0 else jnp.logical_not(low)
                row = run_t[d, pl.ds(2 * j + half, 1), :]
                col = run_e[:, 64 * half:64 * half + 1]
                decay = jnp.exp(jnp.where(seen, col - row, -1e30))
                mixing = (decay * affinity).astype(BF16)
                drive_h = jnp.where(mine, drive, zero)
                go_h = jnp.where(mine, go, zero)
                a, b, e = dot(mixing, drive_h), tn(mixing, go_h), decay * nt(go_h, drive)
                output = a if output is None else output + a
                grad_drive = b if grad_drive is None else grad_drive + b
                total = e if total is None else total + e
            out[d, j] = output
            gd[d, j] = grad_drive
            pairs[d] += total
            return c

        lax.fori_loop(0, PAIRS, step, 0)

    inside(0)

    recv[chip] = totals[chip]
    all_to_owners.wait_recv()

    def scan(i, carry):
        t = i + core * (CHIPS - 1 - 2 * i)
        scanned[t] = carry

        @pl.when(t != chip)
        def _():
            to_chip(t).start()
        return carry * recv[t, 64:65, :] + recv[t, 0:64, :]

    lax.fori_loop(0, CHIPS, scan, jnp.zeros((STATE, 128), F32))
    res[chip] = scanned[chip]

    inside(1)
    for c in range(4):
        ft[256 * c:256 * c + 256, :] = jnp.transpose(f[:, 256 * c:256 * c + 256])
        upt[256 * c:256 * c + 256, :] = jnp.transpose(up[0, :, 256 * c:256 * c + 256])
    gated = f
    for d in range(2):
        def prepare(j, c, d=d):
            gates, swish = g[d, j], swish_s[d, j]
            sigma = jax.nn.sigmoid(gates)
            g[d, j] = gg[j] * (sigma + swish * (1.0 - sigma))
            return c

        lax.fori_loop(0, PAIRS, prepare, 0)
    all_to_chips.wait_recv()

    def hand_on(i, c):
        first = res[i]
        here = src[CHIPS * core + i]
        from_core[i, 0:64, :] = first * here[64:65] + here[0:64]
        entering(i).start()
        ent[CHIPS * core + i] = first
        return c

    lax.fori_loop(0, CHIPS, hand_on, 0)

    all_entering.wait_recv()

    def put(source, target, sent, arrived, device):
        copy = remote(source, target, sent, arrived, device)
        copy.start()
        return copy

    jobs = []
    for n, (q, k) in enumerate(ORDER):
        jobs.append(dict(n=n, stream=n % 2, prod=prod.at[n % 6], acc=core_in.at[n], ring=ring.at[n], mid=mid.at[n],
                         ring2=ring2.at[n], fin=fin.at[n], dp=dp_in.at[n]))

    def core_start(job):
        n = job["n"]
        job["core"] = put(job["prod"].at[:, :, :, 1 - core], job["acc"], job_core.at[n], job_recv.at[6 * n], other)

    def core_end(job):
        job["core"].wait_recv()
        job["acc"][...] = job["acc"][...] + job["prod"][:, :, :, core]

    def chunk(ref, h, c, stream, stage):
        if stream == 0 and stage == 1:
            return ref.at[h, :, c]
        return ref.at[h, c]

    def place(job, stage):
        over_y = (job["stream"] == 0) == (stage == 1)
        return (y, y_dev) if over_y else (z, z_dev)

    def refs(job, stage):
        return (job["acc"], job["ring"], job["mid"]) if stage == 1 else (job["mid"], job["ring2"], job["fin"])

    def ring_start(job, stage):
        p, dev = place(job, stage)
        s = job["stream"]
        ref, buffer, _ = refs(job, stage)
        sent, first, second = job_send.at[stage - 1], job_recv.at[6 * job["n"] + 2 * stage - 1], job_recv.at[6 * job["n"] + 2 * stage]
        put(chunk(ref, 0, (p + 2) % 4, s, stage), buffer.at[0], sent, first, dev[1])
        put(chunk(ref, 1, (p + 2) % 4, s, stage), buffer.at[1], sent, first, dev[3])
        put(chunk(ref, 1, (p + 1) % 4, s, stage), buffer.at[2], sent, second, dev[1])
        put(chunk(ref, 0, (p + 3) % 4, s, stage), buffer.at[3], sent, second, dev[3])

    def ring_middle(job, stage):
        p, dev = place(job, stage)
        s = job["stream"]
        ref, buffer, _ = refs(job, stage)
        sent, first, second = job_send.at[stage - 1], job_recv.at[6 * job["n"] + 2 * stage - 1], job_recv.at[6 * job["n"] + 2 * stage]
        remote(buffer.at[pl.ds(0, 2)], buffer.at[pl.ds(0, 2)], sent, first, other).wait_recv()
        ahead = chunk(ref, 0, (p + 1) % 4, s, stage)
        ahead[...] = ahead[...] + buffer[0]
        put(ahead, buffer.at[4], sent, second, dev[1])
        behind = chunk(ref, 1, (p + 3) % 4, s, stage)
        behind[...] = behind[...] + buffer[1]
        put(behind, buffer.at[5], sent, second, dev[3])

    def ring_end(job, stage):
        p, dev = place(job, stage)
        s = job["stream"]
        ref, buffer, into = refs(job, stage)
        sent, second = job_send.at[stage - 1], job_recv.at[6 * job["n"] + 2 * stage]
        remote(buffer.at[pl.ds(2, 4)], buffer.at[pl.ds(2, 4)], sent, second, other).wait_recv()
        into[0] = chunk(ref, 0, p, s, stage)[...] + buffer[3] + buffer[4]
        into[1] = chunk(ref, 1, p, s, stage)[...] + buffer[2] + buffer[5]

    mine = pl.ds(pl.multiple_of(16 * dp, 16), 16)
    yours = pl.ds(pl.multiple_of(16 * (1 - dp), 16), 16)

    def go_on(n):
        job = jobs[n]
        at = job.get("at", 0)
        job["at"] = at + 1
        q, k = ORDER[n]
        if at == 0:
            core_end(job)
            ring_start(job, 1)
        elif at == 1:
            ring_middle(job, 1)
        elif at == 2:
            ring_end(job, 1)
            ring_start(job, 2)
        elif at == 3:
            ring_middle(job, 2)
        elif at == 4:
            ring_end(job, 2)
            job["over_dp"] = put(
                job["fin"].at[:, yours, :], job["dp"], job_send.at[2], job_recv.at[6 * n + 5], dp_dev)
        else:
            job["over_dp"].wait_recv()
            for h in range(2):
                first = 256 * q + 128 * h
                grads_out[k, :, first:first + 128] = job["fin"][h, mine, :] + job["dp"][h]

    def outside(d, q):
        rows = slice(BASES * d, BASES * (d + 1))
        inflow_b, readout_b = maps[d, :, 0:64], maps[d, :, 64:128]

        def step(j, c):
            run_e, step_e, final = expand(d, j)
            initial, after = ent[16 * d + j], ent[24 - 16 * d + j]
            initial_b, after_b = initial.astype(BF16), after.astype(BF16)
            head, tail = jnp.exp(run_e), jnp.exp(final - run_e)
            drive_r, go_r = drive_b[d, j].astype(F32), go_b[d, j].astype(F32)
            carried = dot(readout_b, initial_b) * head
            output = out[d, j] + carried
            grad_drive = gd[d, j] + dot(inflow_b, after_b) * tail
            values, to_heads = v[d, j], spread[j, :, 0:128]
            a, b = split2(grad_drive * drive_r - go_r * output)
            acc[d] += nt(a, to_heads) + nt(b, to_heads)
            acc_v[d] += nt((grad_drive * values).astype(BF16), to_heads)
            boundary = jnp.sum(go_r * carried, axis=0, keepdims=True) + jnp.exp(final) * jnp.sum(
                initial * after, axis=0, keepdims=True)
            a, b = split2(jnp.broadcast_to(boundary, (16, 128)))
            kk[d] += (nt(a, to_heads) + nt(b, to_heads))[0:8]
            lanes = pl.ds(pl.multiple_of(128 * j, 128), 128)
            gmaps[d, :, 0:64] += nt(wv[2, BASES * d:BASES * (d + 1), lanes], after_b)
            gmaps[d, :, 64:128] += nt(wv[2, BASES * (d + 2):BASES * (d + 3), lanes], initial_b)
            gv[rows, lanes] = (step_e * grad_drive).astype(BF16)
            gate[rows, lanes] = (g[d, j] * output).astype(BF16)
            gated[rows, lanes] = (output * swish_s[d, j]).astype(BF16)
            return c

        lax.fori_loop(2 * q, 2 * q + 2, step, 0, unroll=2)

    def product(n):
        q, k = ORDER[n]
        result = (gv, gate, gated)[k]
        lanes = slice(256 * q, 256 * q + 256)
        if n >= 6:
            jobs[n - 6]["core"].wait_send()

        for i in range(2):
            rows = slice(512 * i, 512 * i + 512)
            if k == 2:
                block = dot(upt[rows, :], result[0:BASES, lanes]) + dot(upt[rows, :], result[BASES:, lanes])
            else:
                block = dot(ft[rows, :], result[:, lanes])
            for h in range(2):
                prod[n % 6, h, 2 * i:2 * i + 2] = block[:, 128 * h:128 * h + 128].reshape(2, 4, 2, 32, 128)
        core_start(jobs[n])

    def finish():
        for d in range(2):
            rows = slice(BASES * d, BASES * (d + 1))
            inflow_b, readout_b = maps[d, :, 0:64], maps[d, :, 64:128]
            pairs_b = pairs[d].astype(BF16)
            gin = gmaps[d, :, 0:64] + tn(pairs_b, readout_b)
            gread = gmaps[d, :, 64:128] + dot(pairs_b, inflow_b)
            gm[rows, :] = jnp.concatenate([gin, gread], axis=1).astype(BF16)
            per_head = jnp.transpose(acc[d])
            boundary = jnp.transpose(jnp.broadcast_to(kk[d, 0:1, :], (128, 128)))[0:16, 0:1]
            earlier = (rows_i < cols_i) if d == 0 else (rows_i > cols_i)
            grad_log = summed3(per_head[0:16], earlier.astype(F32).astype(BF16)) + boundary
            grad_step = jnp.transpose(acc_v[d])[0:16] - grad_log * rate_c
            glt[:, rows] = grad_step * jax.nn.sigmoid(logit_t[d])
            rates[:, d:d + 1] = -jnp.sum(grad_log * step_t[d], axis=1, keepdims=True)

    mean = [jnp.zeros((BASES, 1), F32)] * 2

    def features(c):
        glb = glt[...].astype(BF16)
        lanes = slice(256 * c, 256 * c + 256)
        by_gain = jnp.zeros((1, 256), F32)
        for d in range(2):
            rows = slice(BASES * d, BASES * (d + 1))
            gf = (nt(gv[rows, :], wv[0, lanes, :]) + nt(gate[rows, :], wv[1, lanes, :]) + nt(gm[rows, :], mw[lanes, :])
                  + tn(glb[:, rows], swt[:, lanes]))
            nrm = normed_s[rows, lanes]
            scaled = gf * gain[:, lanes]
            for i in range(2):
                v[d, 2 * c + i] = scaled[:, 128 * i:128 * i + 128]
            mean[d] = mean[d] + jnp.sum(scaled * nrm, axis=1, keepdims=True)
            by_gain = by_gain + jnp.sum(gf * nrm, axis=0, keepdims=True)
        rt[32:40, lanes] = jnp.broadcast_to(by_gain, (8, 256))

    def embedded_grad():
        for c in range(8):
            lanes = slice(128 * c, 128 * c + 128)
            residual = 0.5 * up[0, :, lanes].astype(F32)
            by_base = jnp.zeros((8, 128), F32)
            whole = None
            for d in range(2):
                rows = slice(BASES * d, BASES * (d + 1))
                ge = inv_s[rows, :] * (v[d, c] - normed_s[rows, lanes] * (mean[d] * (1.0 / WIDTH))) + residual
                whole = ge if whole is None else whole + ge
                for part in split3(ge):
                    by_base = by_base + dot(hots[d], part.astype(BF16))
            gg[c] = whole
            rt[40:48, lanes] = by_base

    heads_at = pl.multiple_of(16 * tp, 16)
    scalars_at = pl.multiple_of(48 + 16 * tp, 16)
    offsets = [(dz, dy) for dz in range(4) for dy in range(4)][1:]
    small = [{}, {}]

    def small_step(h, at):
        now = small[h]

        def pair(i):
            return small_sem.at[2 + 12 * h + 2 * i], small_sem.at[3 + 12 * h + 2 * i]

        fifteen = parts.at[h, pl.ds(1, 15)]
        if at == 0:
            if h == 0:
                for i in range(4):
                    prod_e[0, i] = dot(ft[256 * i:256 * i + 256, :], gm[...]).reshape(4, 2, 32, 128)
            else:
                rt[0:32, :] = jnp.zeros((32, WIDTH), F32)
                rt[48:128, :] = jnp.zeros((80, WIDTH), F32)
                rt[pl.ds(heads_at, 16), :] = nt(glt[...].astype(BF16), ft[...])
                rt[pl.ds(scalars_at, 16), 0:128] = jnp.broadcast_to(
                    jnp.sum(glt[...], axis=1, keepdims=True), (HEADS, 128))
                rt[pl.ds(scalars_at, 16), 128:256] = jnp.broadcast_to(rates[:, 0:1] + rates[:, 1:2], (HEADS, 128))
                for i in range(8):
                    prod_e[1, i // 2, 2 * (i % 2):2 * (i % 2) + 2] = rt[:, 128 * i:128 * i + 128].reshape(2, 2, 32, 128)
            now[0] = put(prod_e.at[h, :, :, 1 - core], core_e.at[h], *pair(0), other)
        elif at == 1:
            now[0].wait_recv()
            core_e[h] = core_e[h] + prod_e[h, :, :, core]
            now[1] = put(core_e.at[h, :, :, yours], far_in.at[h], *pair(1), far_dev)
            if h == 1:
                now["tp"] = put(gg.at[pl.ds(4 * (1 - tp), 4)], tp_in, small_sem.at[0], small_sem.at[1], tp_dev)
        elif at == 2:
            now[1].wait_recv()
            sum_x[h] = core_e[h, :, :, mine] + far_in[h]
            for dz, dy in offsets:
                zz, yy = (z + dz) % 4, (y + dy) % 4
                put(sum_x.at[h, zz, yy], parts.at[h, 4 * dz + dy], *pair(2), on(zz * 4 + yy))
            now[2] = remote(fifteen, fifteen, *pair(2), other)
        elif at == 3:
            now[2].wait_recv()
            total = sum_x[h, z, y]
            for i in range(15):
                total = total + parts[h, i + 1]
            mine_e[h, 0] = total
            now[3] = put(mine_e.at[h, 0], tp_in_e.at[h], *pair(3), tp_dev)
        elif at == 4:
            now[3].wait_recv()
            total = mine_e[h, 0] + tp_in_e[h]
            mine_e[h, 1] = total
            gat[h, z, y] = total
            for dz, dy in offsets:
                put(mine_e.at[h, 1], gat.at[h, z, y], *pair(4), on(((z + dz) % 4) * 4 + (y + dy) % 4))
            now[4] = remote(fifteen, fifteen, *pair(4), other)
        elif at == 5:
            now[4].wait_recv()
            all_e[h, :, :, core, mine] = gat[h]
            now[5] = put(gat.at[h], all_e.at[h, :, :, core, mine], *pair(5), far_dev)
        elif at == 6:
            now[5].wait_recv()
            now[6] = put(all_e.at[h, :, :, core], all_e.at[h, :, :, core], small_sem.at[26 + 2 * h],
                         small_sem.at[27 + 2 * h], other)
            if h == 1:
                now["tp"].wait_recv()
                for i in range(4):
                    stream_out[:, 128 * i:128 * i + 128] = gg[4 * tp + i] + tp_in[i]
        else:
            now[6].wait_recv()
            if h == 0:
                mixer_out[...] = all_e[0].reshape(WIDTH, 128)
            else:
                for i in range(8):
                    rt[:, 128 * i:128 * i + 128] = all_e[1, i // 2, 2 * (i % 2):2 * (i % 2) + 2].reshape(128, 128)
                step_out[...] = rt[pl.ds(heads_at, 16), :]
                gain_out[...] = rt[32:33, :]
                table_out[...] = rt[40:45, :]
                scalars_out[...] = rt[pl.ds(scalars_at, 16), 0:256]

    acts = dict(outside=outside, product=product, finish=finish, features=features, embedded=embedded_grad,
                small=small_step, job=go_on)
    for name, *which in PLAN:
        acts[name](*which)
    for n in range(6, 12):
        jobs[n]["core"].wait_send()
    remote(ring, ring, job_send.at[0], job_recv.at[0], other).wait_send()
    remote(ring2, ring2, job_send.at[1], job_recv.at[0], other).wait_send()
    remote(dp_in, dp_in, job_send.at[2], job_recv.at[0], other).wait_send()
    for half in small:
        for copy in half.values():
            copy.wait_send()
    to_core(0, 0, 16).wait_send()
    for copy in (all_to_owners, all_to_chips, all_entering):
        copy.wait_send()


def main(base, stream, cotangent, table, gain, w, mw, swt, bias, rate, spread):
    vmem, anywhere = pl.BlockSpec(memory_space=pltpu.VMEM), pl.BlockSpec(memory_space=pl.ANY)
    rows = 2 * BASES

    def shape(*dims):
        return jax.ShapeDtypeStruct(dims, F32)

    def f32(*dims):
        return pltpu.VMEM(dims, F32)

    def bf16(*dims):
        return pltpu.VMEM(dims, BF16)

    def sems(n):
        return pltpu.SemaphoreType.DMA((n,))

    jobs = len(ORDER)
    return pl.pallas_call(
        main_kernel,
        out_shape=[
            shape(3, 16, WIDTH), shape(WIDTH, 128), shape(HEADS, WIDTH), shape(5, WIDTH), shape(1, WIDTH),
            shape(HEADS, 256), shape(BASES, WIDTH // 2),
        ],
        in_specs=[vmem] * 5 + [anywhere] + [vmem] * 5,
        out_specs=[vmem] * 7,
        scratch_shapes=[
            bf16(3, WIDTH, WIDTH), bf16(rows, WIDTH), f32(rows, WIDTH), f32(rows, 1),
            f32(2, PAIRS, BASES, 128), f32(2, PAIRS, BASES, 128), f32(PAIRS, BASES, 128),
            bf16(2, BASES, 128), f32(2, HEADS, BASES), bf16(2, BASES, 128), bf16(2, 128, BASES), f32(2, HEADS, BASES),
            f32(2, HEADS, BASES), bf16(2, PAIRS, BASES, 128), bf16(2, PAIRS, BASES, 128),
            f32(2, PAIRS, BASES, 128), f32(2, PAIRS, BASES, 128), f32(2, BASES, BASES),
            f32(2, BASES, 128), f32(2, BASES, 128), f32(2, 8, 128), f32(2, BASES, 128),
            f32(2, PAIRS, BASES, 128),
            f32(2 * CHIPS, 72, 128), f32(CHIPS, 72, 128), f32(CHIPS, 72, 128), f32(CHIPS, 72, 128),
            f32(CHIPS, STATE, 128), f32(CHIPS, STATE, 128), f32(2 * CHIPS, STATE, 128),
            bf16(rows, WIDTH), bf16(rows, WIDTH), bf16(rows, 128), f32(HEADS, rows), f32(HEADS, 2),
            bf16(WIDTH, rows), bf16(WIDTH, BASES), f32(128, WIDTH),
            f32(6, 2, 4, 4, 2, 32, 128), f32(jobs, 2, 4, 4, 32, 128), f32(jobs, 6, 4, 32, 128), f32(jobs, 2, 4, 32, 128),
            f32(jobs, 6, 32, 128), f32(jobs, 2, 32, 128), f32(jobs, 2, 16, 128),
            f32(2, 4, 4, 2, 32, 128), f32(2, 4, 4, 32, 128), f32(2, 16, 16, 128), f32(2, 2, 16, 128), f32(2, 4, 4, 16, 128),
            f32(2, 16, 128), f32(2, 4, 4, 16, 128), f32(2, 4, 4, 16, 128), f32(2, 4, 4, 2, 32, 128), f32(4, BASES, 128),
            sems(3), sems(3), sems(6), sems(6 * jobs), sems(jobs), sems(3), sems(30),
        ],
        compiler_params=pltpu.CompilerParams(collective_id=0, has_side_effects=True, vmem_limit_bytes=125 << 19),
        name="main",
    )(base, stream, cotangent, table, gain, w, mw, swt, bias, rate, spread)


def emit_kernel(grads, mixer, steps, by_base, by_gain, scalars, stream,
                grads_out, mixer_out, steps_out, base_out, gain_out, bias_out, rate_out, stream_out):
    for source, target in ((grads, grads_out), (mixer, mixer_out), (steps, steps_out), (by_base, base_out),
                           (by_gain, gain_out), (stream, stream_out)):
        target[...] = source[...]
    same = iota((HEADS, HEADS), 0) == iota((HEADS, HEADS), 1)
    for first, target in ((0, bias_out), (128, rate_out)):
        target[...] = jnp.sum(jnp.where(same, scalars[:, first:first + HEADS], 0.0), axis=0, keepdims=True)


def emit(*results):
    vmem = pl.BlockSpec(memory_space=pltpu.VMEM)
    like = [jax.ShapeDtypeStruct(r.shape, F32) for r in results]
    row = jax.ShapeDtypeStruct((1, HEADS), F32)
    return pl.pallas_call(
        emit_kernel,
        out_shape=like[:5] + [row, row] + like[6:],
        in_specs=[vmem] * 7,
        out_specs=[vmem] * 8,
        name="emit",
    )(*results)


def body(base_ids, stream, cotangent, table, gain, projections, mixer_weight, step_weight, step_bias, rate):
    results = main(
        base_ids, stream, cotangent, table, gain[None], jnp.transpose(projections, (1, 0, 2)), mixer_weight,
        jnp.transpose(step_weight), step_bias[None], rate[None], jnp.asarray(spreads(), BF16))
    grads, mixer, steps, by_base, by_gain, by_bias, by_rate, stream_grad = emit(*results)
    return (
        jnp.transpose(grads, (1, 0, 2)),
        mixer,
        jnp.transpose(steps),
        by_bias[0],
        by_rate[0],
        by_base,
        by_gain[0],
        stream_grad[None],
    )


def solution(mesh):
    return jax.shard_map(
        body,
        mesh=mesh,
        in_specs=(
            P("dp", "ctx"),
            P("dp", "ctx", None),
            P("dp", "ctx", None),
            P(),
            P(),
            P(None, None, "tp"),
            P(),
            P(None, "tp"),
            P("tp"),
            P("tp"),
        ),
        out_specs=(
            P(("ctx", "dp"), None, "tp"),
            P(),
            P(None, "tp"),
            P("tp"),
            P("tp"),
            P(),
            P(),
            P("dp", "ctx", "tp"),
        ),
        check_vma=False,
    )
```

```python
import functools

import jax
import jax.numpy as jnp
import numpy as np
from jax import lax
from jax.experimental import pallas as pl
from jax.experimental.pallas import tpu as pltpu
from jax.sharding import PartitionSpec as P

EPS = 1e-05
HIGH = lax.Precision.HIGHEST
F32 = jnp.float32
BF16 = jnp.bfloat16
MESH = pl.DeviceIdType.MESH
BASES = 256
WIDTH = 1024
HEADS = 16
PAIRS = 8
STATE = 64


def nt(left, right):
    return lax.dot_general(left, right, (((1,), (1,)), ((), ())), preferred_element_type=F32)


def tn(left, right):
    return lax.dot_general(left, right, (((0,), (0,)), ((), ())), preferred_element_type=F32)


def dot(left, right):
    return jnp.dot(left, right, preferred_element_type=F32)


def exact(left, right):
    return jnp.dot(left, right, preferred_element_type=F32, precision=HIGH)


def split3(x):
    a = x.astype(BF16).astype(F32)
    b = (x - a).astype(BF16).astype(F32)
    return a, b, x - a - b


def split2(x):
    a = x.astype(BF16)
    return a, (x - a.astype(F32)).astype(BF16)


def summed3(x, ones):
    r = dot(jnp.concatenate(split3(x), axis=0).astype(BF16), ones)
    n = x.shape[0]
    return r[0:n] + r[n:2 * n] + r[2 * n:3 * n]


def iota(shape, dim):
    return lax.broadcasted_iota(jnp.int32, shape, dim)


def spreads():
    j, r, c = np.indices((PAIRS, 128, 256))
    return np.logical_and(r // 48 == c // 128, r % 16 == 2 * j + c % 128 // 64).astype(np.float32)


CHIPS = 16
ORDER = [(q, k) for q in range(4) for k in (2, 1, 0)]
PLAN = [
    ("outside", 0, 0), ("outside", 1, 0), ("product", 0), ("product", 1), ("outside", 0, 1), ("product", 2),
    ("outside", 1, 1), ("job", 0), ("job", 1), ("product", 3), ("product", 4), ("job", 2),
    ("outside", 0, 2), ("product", 5), ("job", 3), ("outside", 0, 3), ("outside", 1, 2), ("job", 1),
    ("job", 0), ("job", 4), ("job", 5), ("outside", 1, 3), ("finish",), ("small", 0, 0),
    ("job", 3), ("product", 6), ("job", 2), ("product", 7), ("features", 0), ("small", 0, 1),
    ("job", 0), ("job", 1), ("job", 6), ("features", 1), ("job", 4), ("job", 7),
    ("features", 2), ("features", 3), ("embedded",), ("small", 1, 0), ("job", 2), ("job", 5),
    ("product", 8), ("job", 3), ("small", 0, 2), ("small", 1, 1), ("product", 9), ("job", 7),
    ("job", 8), ("product", 10), ("job", 1), ("job", 9), ("job", 3), ("job", 6),
    ("product", 11), ("small", 1, 2), ("job", 7), ("job", 0), ("job", 11), ("small", 0, 3),
    ("job", 10), ("job", 3), ("job", 2), ("job", 5), ("job", 9), ("job", 0),
    ("small", 0, 4), ("job", 6), ("small", 1, 3), ("job", 8), ("job", 4), ("job", 10),
    ("job", 11), ("job", 7), ("job", 1), ("small", 1, 4), ("job", 2), ("job", 6),
    ("job", 4), ("job", 5), ("job", 9), ("job", 8), ("small", 0, 5), ("job", 10),
    ("job", 11), ("job", 0), ("job", 3), ("job", 6), ("job", 7), ("job", 5),
    ("job", 8), ("job", 4), ("job", 9), ("job", 10), ("small", 1, 5), ("job", 11),
    ("job", 8), ("job", 9), ("job", 10), ("job", 11), ("job", 7), ("job", 2),
    ("small", 0, 6), ("job", 6), ("job", 1), ("small", 1, 6), ("small", 0, 7), ("job", 5),
    ("job", 4), ("job", 8), ("small", 1, 7), ("job", 9), ("job", 10), ("job", 11),
]


def main_kernel(base, x, up, table, gain, w, mw, swt, bias, rate, spread,
                grads_out, mixer_out, step_out, table_out, gain_out, scalars_out, stream_out,
                wv, f, normed_s, inv_s, v, g, gg, quant, run_t, maps, maps_t, logit_t, step_t, drive_b, go_b, out, gd, pairs,
                acc, acc_v, kk, gmaps, swish_s, src, from_core, totals, recv, scanned, res, ent,
                gv, gate, gm, glt, rates, ft, upt, rt, prod, core_in, ring, mid, ring2, fin, dp_in,
                prod_e, core_e, parts, mine_e, far_in, tp_in_e, sum_x, gat, all_e, tp_in,
                wsem, core_sem, state_sem, job_recv, job_core, job_send, small_sem):
    ctx, tp, dp = lax.axis_index("ctx"), lax.axis_index("tp"), lax.axis_index("dp")
    core, chip = ctx % 2, ctx // 2
    y, z = chip % 4, chip // 4

    def on(c):
        return {"ctx": c * 2 + core}

    other = {"ctx": chip * 2 + 1 - core}
    tp_dev, dp_dev, far_dev = {"tp": 1 - tp}, {"dp": 1 - dp}, {"tp": 1 - tp, "dp": 1 - dp}
    y_dev = [on(z * 4 + (y + i) % 4) for i in range(4)]
    z_dev = [on(((z + i) % 4) * 4 + y) for i in range(4)]

    barrier = pltpu.get_barrier_semaphore()

    def greet(i, c):
        pl.semaphore_signal(barrier, inc=1, device_id=on(lax.rem(chip + i, CHIPS)), device_id_type=MESH)
        return c

    lax.fori_loop(1, CHIPS, greet, 0)
    for device in (other, tp_dev, dp_dev, far_dev):
        pl.semaphore_signal(barrier, inc=1, device_id=device, device_id_type=MESH)
    copies = [pltpu.make_async_copy(w.at[k], wv.at[k], wsem.at[k]) for k in range(3)]
    for copy in copies:
        copy.start()

    rt[0:8, :] = jnp.zeros((8, WIDTH), F32)
    rt[0:5, :] = table[...]
    pieces = jnp.concatenate(split3(rt[0:8, :]), axis=0).astype(BF16)
    incoming = x[0].astype(F32)
    hots = []
    for d in range(2):
        ids = base[...]
        if d:
            ids = jnp.where(ids == 4, 4, 3 - ids)
        hot = (iota((8, BASES), 0) == ids).astype(F32)
        hots.append(hot.astype(BF16))
        embedded = incoming + tn(jnp.concatenate([hot, hot, hot], axis=0).astype(BF16), pieces)
        inv = lax.rsqrt(jnp.mean(embedded * embedded, axis=1, keepdims=True) + EPS)
        normed = embedded * inv
        rows = slice(BASES * d, BASES * (d + 1))
        normed_s[rows, :] = normed
        inv_s[rows, :] = inv
        f[rows, :] = (normed * gain[...]).astype(BF16)

    def column(row):
        square = jnp.broadcast_to(row, (HEADS, HEADS))
        return jnp.sum(jnp.where(iota((HEADS, HEADS), 0) == iota((HEADS, HEADS), 1), square, 0.0), axis=1, keepdims=True)

    rate_c = column(rate[...])
    mapped = dot(f[...], mw[...])
    for d in range(2):
        maps[d] = mapped[BASES * d:BASES * (d + 1)].astype(BF16)
        maps_t[d] = jnp.transpose(mapped[BASES * d:BASES * (d + 1)]).astype(BF16)
    logits = nt(swt[...], f[...]) + column(bias[...])
    rows_i, cols_i = iota((BASES, BASES), 0), iota((BASES, BASES), 1)
    for d in range(2):
        logit = logits[:, BASES * d:BASES * (d + 1)]
        step = jnp.maximum(logit, 0.0) + jnp.log1p(jnp.exp(-jnp.abs(logit)))
        logit_t[d] = logit
        step_t[d] = step
        upto = (rows_i <= cols_i) if d == 0 else (rows_i >= cols_i)
        run = summed3(-step * rate_c, upto.astype(F32).astype(BF16))
        run_t[d] = run
        whole = jnp.concatenate(split3(run) + split3(step) + (jnp.zeros((32, BASES), F32),), axis=0)
        quant[d] = jnp.transpose(whole).astype(BF16)
        pairs[d] = jnp.zeros((BASES, BASES), F32)
        acc[d] = jnp.zeros((BASES, 128), F32)
        acc_v[d] = jnp.zeros((BASES, 128), F32)
        kk[d] = jnp.zeros((8, 128), F32)
        gmaps[d] = jnp.zeros((BASES, 128), F32)
    for k, target in ((0, v), (1, g)):
        copies[k].wait()
        for c in range(4):
            block = dot(f[...], wv[k, :, 256 * c:256 * c + 256])
            for d in range(2):
                for i in range(2):
                    target[d, 2 * c + i] = block[BASES * d:BASES * (d + 1), 128 * i:128 * i + 128]
    copies[2].wait()
    for c in range(4):
        block = dot(up[0], wv[2, :, 256 * c:256 * c + 256])
        for i in range(2):
            gg[2 * c + i] = block[:, 128 * i:128 * i + 128]

    def expand(d, j):
        both = dot(quant[d], spread[j])
        run_e, step_e = both[:, 0:128], both[:, 128:256]
        final = run_e[BASES - 1:BASES] if d == 0 else run_e[0:1]
        return run_e, step_e, final

    def remote(source, target, sent, arrived, device):
        return pltpu.make_async_remote_copy(
            src_ref=source, dst_ref=target, send_sem=sent, recv_sem=arrived, device_id=device, device_id_type=MESH)

    def to_core(i, half, n=1):
        source = src.at[CHIPS * (1 - core) + i] if n == 1 else src.at[pl.ds(0, n)]
        target = from_core.at[i] if n == 1 else from_core.at[pl.ds(i, n)]
        return remote(source, target, core_sem.at[2], core_sem.at[half], other)

    def to_owner(i):
        return remote(totals.at[i], recv.at[chip], state_sem.at[0], state_sem.at[1], on(i))

    all_to_owners = remote(totals.at[pl.ds(0, 15)], recv.at[pl.ds(0, 15)], state_sem.at[0], state_sem.at[1], other)

    def to_chip(i):
        return remote(scanned.at[i], res.at[chip], state_sem.at[2], state_sem.at[3], on(i))

    all_to_chips = remote(scanned.at[pl.ds(0, 15)], res.at[pl.ds(0, 15)], state_sem.at[2], state_sem.at[3], other)

    def entering(i):
        return remote(from_core.at[i, pl.ds(0, 64)], ent.at[CHIPS * core + i], state_sem.at[4], state_sem.at[5], other)

    all_entering = remote(ent.at[pl.ds(CHIPS * core, CHIPS)], ent.at[pl.ds(CHIPS * (1 - core), CHIPS)], state_sem.at[4], state_sem.at[5], other)

    pl.semaphore_wait(barrier, CHIPS + 3)

    def ends(d, first, last):
        def step(j, c):
            run_e, step_e, final = expand(d, j)
            drive = step_e * v[d, j]
            gates = g[d, j]
            sigma = jax.nn.sigmoid(gates)
            swish = gates * sigma
            go = gg[j] * swish
            drive_b[d, j] = drive.astype(BF16)
            go_b[d, j] = go.astype(BF16)
            swish_s[d, j] = swish
            late_drive = (drive * jnp.exp(final - run_e)).astype(BF16)
            late_go = (go * jnp.exp(run_e)).astype(BF16)
            lanes = pl.ds(pl.multiple_of(128 * j, 128), 128)
            wv[2, BASES * d:BASES * (d + 1), lanes] = late_drive
            wv[2, BASES * (d + 2):BASES * (d + 3), lanes] = late_go
            state = dot(maps_t[d, 0:64, :], late_drive)
            grad = dot(maps_t[d, 64:128, :], late_go)
            decay = jnp.broadcast_to(jnp.exp(final), (8, 128))
            for t, value in ((16 * d + j, state), (24 - 16 * d + j, grad)):
                src[t, 0:64, :] = value
                src[t, 64:72, :] = decay
            half = (1 - core) if d == 0 else core
            to_core(j + 8 * half, half).start()
            return c

        lax.fori_loop(first, last, step, 0, unroll=2)

    def combine(i, c):
        here, there = src[CHIPS * core + i], from_core[i]
        totals[i, 0:64, :] = here[0:64] * there[64:65] + there[0:64]
        totals[i, 64:72, :] = here[64:72] * there[64:72]

        @pl.when(i != chip)
        def _():
            to_owner(i).start()
        return c

    def combine_half(half):
        to_core(8 * half, half, 8).wait_recv()
        lax.fori_loop(0, 8, lambda i, c: combine(8 * half + i, c), 0, unroll=4)

    ends(0, 0, PAIRS)
    ends(1, 0, PAIRS // 2)
    combine_half(core)
    ends(1, PAIRS // 2, PAIRS)
    combine_half(1 - core)

    low = iota((BASES, 128), 1) < 64

    def inside(d):
        seen = (rows_i >= cols_i) if d == 0 else (rows_i <= cols_i)
        inflow_b, readout_b = maps[d, :, 0:64], maps[d, :, 64:128]
        affinity = nt(readout_b, inflow_b)

        def step(j, c):
            run_e, _, _ = expand(d, j)
            drive, go = drive_b[d, j], go_b[d, j]
            zero = jnp.zeros_like(drive)
            output = grad_drive = total = None
            for half in range(2):
                mine = low if half == 0 else jnp.logical_not(low)
                row = run_t[d, pl.ds(2 * j + half, 1), :]
                col = run_e[:, 64 * half:64 * half + 1]
                decay = jnp.exp(jnp.where(seen, col - row, -1e30))
                mixing = (decay * affinity).astype(BF16)
                drive_h = jnp.where(mine, drive, zero)
                go_h = jnp.where(mine, go, zero)
                a, b, e = dot(mixing, drive_h), tn(mixing, go_h), decay * nt(go_h, drive)
                output = a if output is None else output + a
                grad_drive = b if grad_drive is None else grad_drive + b
                total = e if total is None else total + e
            out[d, j] = output
            gd[d, j] = grad_drive
            pairs[d] += total
            return c

        lax.fori_loop(0, PAIRS, step, 0)

    inside(0)

    recv[chip] = totals[chip]
    all_to_owners.wait_recv()

    def scan(i, carry):
        t = i + core * (CHIPS - 1 - 2 * i)
        scanned[t] = carry

        @pl.when(t != chip)
        def _():
            to_chip(t).start()
        return carry * recv[t, 64:65, :] + recv[t, 0:64, :]

    lax.fori_loop(0, CHIPS, scan, jnp.zeros((STATE, 128), F32), unroll=4)
    res[chip] = scanned[chip]

    inside(1)
    for c in range(4):
        ft[256 * c:256 * c + 256, :] = jnp.transpose(f[:, 256 * c:256 * c + 256])
        upt[256 * c:256 * c + 256, :] = jnp.transpose(up[0, :, 256 * c:256 * c + 256])
    gated = f
    for d in range(2):
        def prepare(j, c, d=d):
            gates, swish = g[d, j], swish_s[d, j]
            sigma = jax.nn.sigmoid(gates)
            g[d, j] = gg[j] * (sigma + swish * (1.0 - sigma))
            return c

        lax.fori_loop(0, PAIRS, prepare, 0)
    all_to_chips.wait_recv()

    def hand_on(i, c):
        first = res[i]
        here = src[CHIPS * core + i]
        from_core[i, 0:64, :] = first * here[64:65] + here[0:64]
        entering(i).start()
        ent[CHIPS * core + i] = first
        return c

    lax.fori_loop(0, CHIPS, hand_on, 0, unroll=4)

    all_entering.wait_recv()

    def put(source, target, sent, arrived, device):
        copy = remote(source, target, sent, arrived, device)
        copy.start()
        return copy

    jobs = []
    for n, (q, k) in enumerate(ORDER):
        jobs.append(dict(n=n, stream=n % 2, prod=prod.at[n % 6], acc=core_in.at[n], ring=ring.at[n], mid=mid.at[n],
                         ring2=ring2.at[n], fin=fin.at[n], dp=dp_in.at[n]))

    def core_start(job):
        n = job["n"]
        job["core"] = put(job["prod"].at[:, :, :, 1 - core], job["acc"], job_core.at[n], job_recv.at[6 * n], other)

    def core_end(job):
        job["core"].wait_recv()
        job["acc"][...] = job["acc"][...] + job["prod"][:, :, :, core]

    def chunk(ref, h, c, stream, stage):
        if stream == 0 and stage == 1:
            return ref.at[h, :, c]
        return ref.at[h, c]

    def place(job, stage):
        over_y = (job["stream"] == 0) == (stage == 1)
        return (y, y_dev) if over_y else (z, z_dev)

    def refs(job, stage):
        return (job["acc"], job["ring"], job["mid"]) if stage == 1 else (job["mid"], job["ring2"], job["fin"])

    def ring_start(job, stage):
        p, dev = place(job, stage)
        s = job["stream"]
        ref, buffer, _ = refs(job, stage)
        sent, first, second = job_send.at[stage - 1], job_recv.at[6 * job["n"] + 2 * stage - 1], job_recv.at[6 * job["n"] + 2 * stage]
        put(chunk(ref, 0, (p + 2) % 4, s, stage), buffer.at[0], sent, first, dev[1])
        put(chunk(ref, 1, (p + 2) % 4, s, stage), buffer.at[1], sent, first, dev[3])
        put(chunk(ref, 1, (p + 1) % 4, s, stage), buffer.at[2], sent, second, dev[1])
        put(chunk(ref, 0, (p + 3) % 4, s, stage), buffer.at[3], sent, second, dev[3])

    def ring_middle(job, stage):
        p, dev = place(job, stage)
        s = job["stream"]
        ref, buffer, _ = refs(job, stage)
        sent, first, second = job_send.at[stage - 1], job_recv.at[6 * job["n"] + 2 * stage - 1], job_recv.at[6 * job["n"] + 2 * stage]
        remote(buffer.at[pl.ds(0, 2)], buffer.at[pl.ds(0, 2)], sent, first, other).wait_recv()
        ahead = chunk(ref, 0, (p + 1) % 4, s, stage)
        ahead[...] = ahead[...] + buffer[0]
        put(ahead, buffer.at[4], sent, second, dev[1])
        behind = chunk(ref, 1, (p + 3) % 4, s, stage)
        behind[...] = behind[...] + buffer[1]
        put(behind, buffer.at[5], sent, second, dev[3])

    def ring_end(job, stage):
        p, dev = place(job, stage)
        s = job["stream"]
        ref, buffer, into = refs(job, stage)
        sent, second = job_send.at[stage - 1], job_recv.at[6 * job["n"] + 2 * stage]
        remote(buffer.at[pl.ds(2, 4)], buffer.at[pl.ds(2, 4)], sent, second, other).wait_recv()
        into[0] = chunk(ref, 0, p, s, stage)[...] + buffer[3] + buffer[4]
        into[1] = chunk(ref, 1, p, s, stage)[...] + buffer[2] + buffer[5]

    mine = pl.ds(pl.multiple_of(16 * dp, 16), 16)
    yours = pl.ds(pl.multiple_of(16 * (1 - dp), 16), 16)

    def go_on(n):
        job = jobs[n]
        at = job.get("at", 0)
        job["at"] = at + 1
        q, k = ORDER[n]
        if at == 0:
            core_end(job)
            ring_start(job, 1)
        elif at == 1:
            ring_middle(job, 1)
        elif at == 2:
            ring_end(job, 1)
            ring_start(job, 2)
        elif at == 3:
            ring_middle(job, 2)
        elif at == 4:
            ring_end(job, 2)
            job["over_dp"] = put(
                job["fin"].at[:, yours, :], job["dp"], job_send.at[2], job_recv.at[6 * n + 5], dp_dev)
        else:
            job["over_dp"].wait_recv()
            for h in range(2):
                first = 256 * q + 128 * h
                grads_out[k, :, first:first + 128] = job["fin"][h, mine, :] + job["dp"][h]

    def outside(d, q):
        rows = slice(BASES * d, BASES * (d + 1))
        inflow_b, readout_b = maps[d, :, 0:64], maps[d, :, 64:128]

        def step(j, c):
            run_e, step_e, final = expand(d, j)
            initial, after = ent[16 * d + j], ent[24 - 16 * d + j]
            initial_b, after_b = initial.astype(BF16), after.astype(BF16)
            head, tail = jnp.exp(run_e), jnp.exp(final - run_e)
            drive_r, go_r = drive_b[d, j].astype(F32), go_b[d, j].astype(F32)
            carried = dot(readout_b, initial_b) * head
            output = out[d, j] + carried
            grad_drive = gd[d, j] + dot(inflow_b, after_b) * tail
            values, to_heads = v[d, j], spread[j, :, 0:128]
            a, b = split2(grad_drive * drive_r - go_r * output)
            acc[d] += nt(a, to_heads) + nt(b, to_heads)
            acc_v[d] += nt((grad_drive * values).astype(BF16), to_heads)
            boundary = jnp.sum(go_r * carried, axis=0, keepdims=True) + jnp.exp(final) * jnp.sum(
                initial * after, axis=0, keepdims=True)
            a, b = split2(jnp.broadcast_to(boundary, (16, 128)))
            kk[d] += (nt(a, to_heads) + nt(b, to_heads))[0:8]
            lanes = pl.ds(pl.multiple_of(128 * j, 128), 128)
            gmaps[d, :, 0:64] += nt(wv[2, BASES * d:BASES * (d + 1), lanes], after_b)
            gmaps[d, :, 64:128] += nt(wv[2, BASES * (d + 2):BASES * (d + 3), lanes], initial_b)
            gv[rows, lanes] = (step_e * grad_drive).astype(BF16)
            gate[rows, lanes] = (g[d, j] * output).astype(BF16)
            gated[rows, lanes] = (output * swish_s[d, j]).astype(BF16)
            return c

        lax.fori_loop(2 * q, 2 * q + 2, step, 0, unroll=2)

    def product(n):
        q, k = ORDER[n]
        result = (gv, gate, gated)[k]
        lanes = slice(256 * q, 256 * q + 256)
        if n >= 6:
            jobs[n - 6]["core"].wait_send()

        for i in range(2):
            rows = slice(512 * i, 512 * i + 512)
            if k == 2:
                block = dot(upt[rows, :], result[0:BASES, lanes]) + dot(upt[rows, :], result[BASES:, lanes])
            else:
                block = dot(ft[rows, :], result[:, lanes])
            for h in range(2):
                prod[n % 6, h, 2 * i:2 * i + 2] = block[:, 128 * h:128 * h + 128].reshape(2, 4, 2, 32, 128)
        core_start(jobs[n])

    def finish():
        for d in range(2):
            rows = slice(BASES * d, BASES * (d + 1))
            inflow_b, readout_b = maps[d, :, 0:64], maps[d, :, 64:128]
            pairs_b = pairs[d].astype(BF16)
            gin = gmaps[d, :, 0:64] + tn(pairs_b, readout_b)
            gread = gmaps[d, :, 64:128] + dot(pairs_b, inflow_b)
            gm[rows, :] = jnp.concatenate([gin, gread], axis=1).astype(BF16)
            per_head = jnp.transpose(acc[d])
            boundary = jnp.transpose(jnp.broadcast_to(kk[d, 0:1, :], (128, 128)))[0:16, 0:1]
            earlier = (rows_i < cols_i) if d == 0 else (rows_i > cols_i)
            grad_log = summed3(per_head[0:16], earlier.astype(F32).astype(BF16)) + boundary
            grad_step = jnp.transpose(acc_v[d])[0:16] - grad_log * rate_c
            glt[:, rows] = grad_step * jax.nn.sigmoid(logit_t[d])
            rates[:, d:d + 1] = -jnp.sum(grad_log * step_t[d], axis=1, keepdims=True)

    mean = [jnp.zeros((BASES, 1), F32)] * 2

    def features(c):
        glb = glt[...].astype(BF16)
        lanes = slice(256 * c, 256 * c + 256)
        by_gain = jnp.zeros((1, 256), F32)
        for d in range(2):
            rows = slice(BASES * d, BASES * (d + 1))
            gf = (nt(gv[rows, :], wv[0, lanes, :]) + nt(gate[rows, :], wv[1, lanes, :]) + nt(gm[rows, :], mw[lanes, :])
                  + tn(glb[:, rows], swt[:, lanes]))
            nrm = normed_s[rows, lanes]
            scaled = gf * gain[:, lanes]
            for i in range(2):
                v[d, 2 * c + i] = scaled[:, 128 * i:128 * i + 128]
            mean[d] = mean[d] + jnp.sum(scaled * nrm, axis=1, keepdims=True)
            by_gain = by_gain + jnp.sum(gf * nrm, axis=0, keepdims=True)
        rt[32:40, lanes] = jnp.broadcast_to(by_gain, (8, 256))

    def embedded_grad():
        for c in range(8):
            lanes = slice(128 * c, 128 * c + 128)
            residual = 0.5 * up[0, :, lanes].astype(F32)
            by_base = jnp.zeros((8, 128), F32)
            whole = None
            for d in range(2):
                rows = slice(BASES * d, BASES * (d + 1))
                ge = inv_s[rows, :] * (v[d, c] - normed_s[rows, lanes] * (mean[d] * (1.0 / WIDTH))) + residual
                whole = ge if whole is None else whole + ge
                for part in split3(ge):
                    by_base = by_base + dot(hots[d], part.astype(BF16))
            gg[c] = whole
            rt[40:48, lanes] = by_base

    heads_at = pl.multiple_of(16 * tp, 16)
    scalars_at = pl.multiple_of(48 + 16 * tp, 16)
    offsets = [(dz, dy) for dz in range(4) for dy in range(4)][1:]
    small = [{}, {}]

    def small_step(h, at):
        now = small[h]

        def pair(i):
            return small_sem.at[2 + 12 * h + 2 * i], small_sem.at[3 + 12 * h + 2 * i]

        fifteen = parts.at[h, pl.ds(1, 15)]
        if at == 0:
            if h == 0:
                for i in range(4):
                    prod_e[0, i] = dot(ft[256 * i:256 * i + 256, :], gm[...]).reshape(4, 2, 32, 128)
            else:
                rt[0:32, :] = jnp.zeros((32, WIDTH), F32)
                rt[48:128, :] = jnp.zeros((80, WIDTH), F32)
                rt[pl.ds(heads_at, 16), :] = nt(glt[...].astype(BF16), ft[...])
                rt[pl.ds(scalars_at, 16), 0:128] = jnp.broadcast_to(
                    jnp.sum(glt[...], axis=1, keepdims=True), (HEADS, 128))
                rt[pl.ds(scalars_at, 16), 128:256] = jnp.broadcast_to(rates[:, 0:1] + rates[:, 1:2], (HEADS, 128))
                for i in range(8):
                    prod_e[1, i // 2, 2 * (i % 2):2 * (i % 2) + 2] = rt[:, 128 * i:128 * i + 128].reshape(2, 2, 32, 128)
            now[0] = put(prod_e.at[h, :, :, 1 - core], core_e.at[h], *pair(0), other)
        elif at == 1:
            now[0].wait_recv()
            core_e[h] = core_e[h] + prod_e[h, :, :, core]
            now[1] = put(core_e.at[h, :, :, yours], far_in.at[h], *pair(1), far_dev)
            if h == 1:
                now["tp"] = put(gg.at[pl.ds(4 * (1 - tp), 4)], tp_in, small_sem.at[0], small_sem.at[1], tp_dev)
        elif at == 2:
            now[1].wait_recv()
            sum_x[h] = core_e[h, :, :, mine] + far_in[h]
            for dz, dy in offsets:
                zz, yy = (z + dz) % 4, (y + dy) % 4
                put(sum_x.at[h, zz, yy], parts.at[h, 4 * dz + dy], *pair(2), on(zz * 4 + yy))
            now[2] = remote(fifteen, fifteen, *pair(2), other)
        elif at == 3:
            now[2].wait_recv()
            total = sum_x[h, z, y]
            for i in range(15):
                total = total + parts[h, i + 1]
            mine_e[h, 0] = total
            now[3] = put(mine_e.at[h, 0], tp_in_e.at[h], *pair(3), tp_dev)
        elif at == 4:
            now[3].wait_recv()
            total = mine_e[h, 0] + tp_in_e[h]
            mine_e[h, 1] = total
            gat[h, z, y] = total
            for dz, dy in offsets:
                put(mine_e.at[h, 1], gat.at[h, z, y], *pair(4), on(((z + dz) % 4) * 4 + (y + dy) % 4))
            now[4] = remote(fifteen, fifteen, *pair(4), other)
        elif at == 5:
            now[4].wait_recv()
            all_e[h, :, :, core, mine] = gat[h]
            now[5] = put(gat.at[h], all_e.at[h, :, :, core, mine], *pair(5), far_dev)
        elif at == 6:
            now[5].wait_recv()
            now[6] = put(all_e.at[h, :, :, core], all_e.at[h, :, :, core], small_sem.at[26 + 2 * h],
                         small_sem.at[27 + 2 * h], other)
            if h == 1:
                now["tp"].wait_recv()
                for i in range(4):
                    stream_out[:, 128 * i:128 * i + 128] = gg[4 * tp + i] + tp_in[i]
        else:
            now[6].wait_recv()
            if h == 0:
                mixer_out[...] = all_e[0].reshape(WIDTH, 128)
            else:
                for i in range(8):
                    rt[:, 128 * i:128 * i + 128] = all_e[1, i // 2, 2 * (i % 2):2 * (i % 2) + 2].reshape(128, 128)
                step_out[...] = rt[pl.ds(heads_at, 16), :]
                gain_out[...] = rt[32:33, :]
                table_out[...] = rt[40:45, :]
                scalars_out[...] = rt[pl.ds(scalars_at, 16), 0:256]

    acts = dict(outside=outside, product=product, finish=finish, features=features, embedded=embedded_grad,
                small=small_step, job=go_on)
    for name, *which in PLAN:
        acts[name](*which)
    for n in range(6, 12):
        jobs[n]["core"].wait_send()
    remote(ring, ring, job_send.at[0], job_recv.at[0], other).wait_send()
    remote(ring2, ring2, job_send.at[1], job_recv.at[0], other).wait_send()
    remote(dp_in, dp_in, job_send.at[2], job_recv.at[0], other).wait_send()
    for half in small:
        for copy in half.values():
            copy.wait_send()
    to_core(0, 0, 16).wait_send()
    for copy in (all_to_owners, all_to_chips, all_entering):
        copy.wait_send()


def main(base, stream, cotangent, table, gain, w, mw, swt, bias, rate, spread):
    vmem, anywhere = pl.BlockSpec(memory_space=pltpu.VMEM), pl.BlockSpec(memory_space=pl.ANY)
    rows = 2 * BASES

    def shape(*dims):
        return jax.ShapeDtypeStruct(dims, F32)

    def f32(*dims):
        return pltpu.VMEM(dims, F32)

    def bf16(*dims):
        return pltpu.VMEM(dims, BF16)

    def sems(n):
        return pltpu.SemaphoreType.DMA((n,))

    jobs = len(ORDER)
    return pl.pallas_call(
        main_kernel,
        out_shape=[
            shape(3, 16, WIDTH), shape(WIDTH, 128), shape(HEADS, WIDTH), shape(5, WIDTH), shape(1, WIDTH),
            shape(HEADS, 256), shape(BASES, WIDTH // 2),
        ],
        in_specs=[vmem] * 5 + [anywhere] + [vmem] * 5,
        out_specs=[vmem] * 7,
        scratch_shapes=[
            bf16(3, WIDTH, WIDTH), bf16(rows, WIDTH), f32(rows, WIDTH), f32(rows, 1),
            f32(2, PAIRS, BASES, 128), f32(2, PAIRS, BASES, 128), f32(PAIRS, BASES, 128),
            bf16(2, BASES, 128), f32(2, HEADS, BASES), bf16(2, BASES, 128), bf16(2, 128, BASES), f32(2, HEADS, BASES),
            f32(2, HEADS, BASES), bf16(2, PAIRS, BASES, 128), bf16(2, PAIRS, BASES, 128),
            f32(2, PAIRS, BASES, 128), f32(2, PAIRS, BASES, 128), f32(2, BASES, BASES),
            f32(2, BASES, 128), f32(2, BASES, 128), f32(2, 8, 128), f32(2, BASES, 128),
            f32(2, PAIRS, BASES, 128),
            f32(2 * CHIPS, 72, 128), f32(CHIPS, 72, 128), f32(CHIPS, 72, 128), f32(CHIPS, 72, 128),
            f32(CHIPS, STATE, 128), f32(CHIPS, STATE, 128), f32(2 * CHIPS, STATE, 128),
            bf16(rows, WIDTH), bf16(rows, WIDTH), bf16(rows, 128), f32(HEADS, rows), f32(HEADS, 2),
            bf16(WIDTH, rows), bf16(WIDTH, BASES), f32(128, WIDTH),
            f32(6, 2, 4, 4, 2, 32, 128), f32(jobs, 2, 4, 4, 32, 128), f32(jobs, 6, 4, 32, 128), f32(jobs, 2, 4, 32, 128),
            f32(jobs, 6, 32, 128), f32(jobs, 2, 32, 128), f32(jobs, 2, 16, 128),
            f32(2, 4, 4, 2, 32, 128), f32(2, 4, 4, 32, 128), f32(2, 16, 16, 128), f32(2, 2, 16, 128), f32(2, 4, 4, 16, 128),
            f32(2, 16, 128), f32(2, 4, 4, 16, 128), f32(2, 4, 4, 16, 128), f32(2, 4, 4, 2, 32, 128), f32(4, BASES, 128),
            sems(3), sems(3), sems(6), sems(6 * jobs), sems(jobs), sems(3), sems(30),
        ],
        compiler_params=pltpu.CompilerParams(collective_id=0, has_side_effects=True, vmem_limit_bytes=125 << 19),
        name="main",
    )(base, stream, cotangent, table, gain, w, mw, swt, bias, rate, spread)


def emit_kernel(grads, mixer, steps, by_base, by_gain, scalars, stream,
                grads_out, mixer_out, steps_out, base_out, gain_out, bias_out, rate_out, stream_out):
    for source, target in ((grads, grads_out), (mixer, mixer_out), (steps, steps_out), (by_base, base_out),
                           (by_gain, gain_out), (stream, stream_out)):
        target[...] = source[...]
    same = iota((HEADS, HEADS), 0) == iota((HEADS, HEADS), 1)
    for first, target in ((0, bias_out), (128, rate_out)):
        target[...] = jnp.sum(jnp.where(same, scalars[:, first:first + HEADS], 0.0), axis=0, keepdims=True)


def emit(*results):
    vmem = pl.BlockSpec(memory_space=pltpu.VMEM)
    like = [jax.ShapeDtypeStruct(r.shape, F32) for r in results]
    row = jax.ShapeDtypeStruct((1, HEADS), F32)
    return pl.pallas_call(
        emit_kernel,
        out_shape=like[:5] + [row, row] + like[6:],
        in_specs=[vmem] * 7,
        out_specs=[vmem] * 8,
        name="emit",
    )(*results)


def body(base_ids, stream, cotangent, table, gain, projections, mixer_weight, step_weight, step_bias, rate):
    results = main(
        base_ids, stream, cotangent, table, gain[None], jnp.transpose(projections, (1, 0, 2)), mixer_weight,
        jnp.transpose(step_weight), step_bias[None], rate[None], jnp.asarray(spreads(), BF16))
    grads, mixer, steps, by_base, by_gain, by_bias, by_rate, stream_grad = emit(*results)
    return (
        jnp.transpose(grads, (1, 0, 2)),
        mixer,
        jnp.transpose(steps),
        by_bias[0],
        by_rate[0],
        by_base,
        by_gain[0],
        stream_grad[None],
    )


def solution(mesh):
    return jax.shard_map(
        body,
        mesh=mesh,
        in_specs=(
            P("dp", "ctx"),
            P("dp", "ctx", None),
            P("dp", "ctx", None),
            P(),
            P(),
            P(None, None, "tp"),
            P(),
            P(None, "tp"),
            P("tp"),
            P("tp"),
        ),
        out_specs=(
            P(("ctx", "dp"), None, "tp"),
            P(),
            P(None, "tp"),
            P("tp"),
            P("tp"),
            P(),
            P(),
            P("dp", "ctx", "tp"),
        ),
        check_vma=False,
    )
```
